32 devices in a mesh: section: 2 (over y), seq: 4 (over x, core), head: 4 (over z).
Axes of the slice: x: 2, y: 2, z: 4, core: 2. Of those that a mesh axis runs over, the one named last changes fastest.
Arguments:
- tokens: bfloat16 [2, 4096, 1536], P(None, 'seq'), may hold values from -6 to 6
- cotangent: bfloat16 [2, 4096, 1536], P(None, 'seq'), may hold values from -6 to 6
- norm_gain: float32 [2, 1536], P('section'), may hold values from 0.5 to 1.5
- w_z: bfloat16 [2, 1536, 3072], P('section', None, 'head'), may hold values from -0.15625 to 0.15625
- w_x: bfloat16 [2, 1536, 3072], P('section', None, 'head'), may hold values from -0.15625 to 0.15625
- w_bc: bfloat16 [2, 1536, 256], P('section'), may hold values from -0.15625 to 0.15625
- w_dt: bfloat16 [2, 1536, 48], P('section', None, 'head'), may hold values from -0.15625 to 0.15625
- conv_x: float32 [2, 3072, 4], P('section', 'head'), may hold values from -3 to 3
- conv_bc: float32 [2, 256, 4], P('section'), may hold values from -3 to 3
- dt_bias: float32 [2, 48], P('section', 'head'), may hold values from -6 to -2
- a_log: float32 [2, 48], P('section', 'head'), may hold values from -1 to 2.5
- skip_d: float32 [2, 48], P('section', 'head'), may hold values from 0.5 to 1.5
- gate_gain: float32 [2, 3072], P('section', 'head'), may hold values from 0.5 to 1.5
- w_out: bfloat16 [2, 1536, 3072], P('section', None, 'head'), may hold values from -0.109375 to 0.109375
Outputs:
- block_outputs: bfloat16 [2, 2, 4096, 1536], P('section', None, 'seq', 'head')
- input_grads: bfloat16 [2, 2, 4096, 1536], P('section', None, 'seq', 'head')
- grad_norm_gain: float32 [2, 1536], P('section', 'head')
- grad_w_z: float32 [2, 1536, 3072], P('section', 'seq', 'head')
- grad_w_x: float32 [2, 1536, 3072], P('section', 'seq', 'head')
- grad_w_bc: float32 [2, 1536, 256], P('section', 'seq', 'head')
- grad_w_dt: float32 [2, 1536, 48], P('section', 'seq', 'head')
- grad_conv_x: float32 [2, 3072, 4], P('section', 'head')
- grad_conv_bc: float32 [2, 256, 4], P('section')
- grad_dt_bias: float32 [2, 48], P('section', 'head')
- grad_a_log: float32 [2, 48], P('section', 'head')
- grad_skip_d: float32 [2, 48], P('section', 'head')
- grad_gate_gain: float32 [2, 3072], P('section', 'head')
- grad_w_out: float32 [2, 1536, 3072], P('section', 'seq', 'head')
The draws below stay inside these ranges and needn't reach their ends.
All inputs are finite; a program needn't handle non-finite values.
Results may differ from the reference program's by a relative error of at most 0.02.
Values may be sent and summed in bfloat16 or wider, within the bound.
No kernel may reach another device: no remote copies, remote signals or barrier semaphores. Data moves between devices by JAX's collectives and lax.ppermute only.
A program may use at most 320 MiB of HBM per device.

```python
from functools import partial
import jax
import jax.numpy as jnp
from jax import lax

D = 1536
INNER = 3072
HEADS = 48
HEAD_DIM = 64
STATE = 128
CONV = 4
SPAN = 256
SEQS = 2
L = 4096


def level_of(rng, shape, shards, smallest, largest):
    def one(dim, shards_of):
        heights = jax.random.uniform(jax.random.fold_in(jax.random.fold_in(rng, 6), dim), (shards_of,), jnp.float32, smallest / len(shards), largest / len(shards))
        return jnp.repeat(jnp.exp(heights), shape[dim] // shards_of).reshape((-1,) + (1,) * (len(shape) - dim - 1))

    factor_of = one(*shards[0])
    for cut in shards[1:]:
        factor_of = factor_of * one(*cut)
    return factor_of


def bell_draw(own_key, dims, width, reach, cuts=(), dtype=jnp.bfloat16):
    array = width * jax.random.normal(own_key, dims, jnp.float32)
    if cuts:
        array = array * level_of(own_key, dims, cuts, -0.22, 0.18)
    return jnp.clip(array, -reach, reach).astype(dtype)


def setup_inputs(seed: int = 0) -> dict:
    seeds = jax.random.split(jax.random.key(seed), 15)
    return {
        "tokens": bell_draw(seeds[0], (SEQS, L, D), 1.0, 6.0, ((1, 4),)),
        "cotangent": bell_draw(seeds[1], (SEQS, L, D), 1.0, 6.0, ((1, 4),)),
        "norm_gain": jnp.clip(1.0 + 0.1 * jax.random.normal(seeds[2], (2, D), jnp.float32), 0.5, 1.5),
        "w_z": bell_draw(seeds[3], (2, D, INNER), D ** -0.5, 0.15625, ((0, 2), (2, 4))),
        "w_x": bell_draw(seeds[4], (2, D, INNER), D ** -0.5, 0.15625, ((0, 2), (2, 4))),
        "w_bc": bell_draw(seeds[5], (2, D, 2 * STATE), D ** -0.5, 0.15625, ((0, 2),)),
        "w_dt": bell_draw(seeds[6], (2, D, HEADS), D ** -0.5, 0.15625, ((0, 2), (2, 4))),
        "conv_x": bell_draw(seeds[7], (2, INNER, CONV), CONV ** -0.5, 3.0, ((0, 2), (1, 4)), jnp.float32),
        "conv_bc": bell_draw(seeds[8], (2, 2 * STATE, CONV), CONV ** -0.5, 3.0, ((0, 2),), jnp.float32),
        "dt_bias": jnp.clip(-6.0 + 4.0 * jax.random.uniform(seeds[9], (2, HEADS), jnp.float32) ** level_of(seeds[9], (2, HEADS), ((0, 2), (1, 4)), -0.2, 0.2), -6.0, -2.0),
        "a_log": jnp.clip(-1.0 + 3.5 * jax.random.uniform(seeds[10], (2, HEADS), jnp.float32) ** level_of(seeds[10], (2, HEADS), ((0, 2), (1, 4)), -0.2, 0.2), -1.0, 2.5),
        "skip_d": jnp.clip(0.5 + 1.0 * jax.random.uniform(seeds[11], (2, HEADS), jnp.float32) ** level_of(seeds[11], (2, HEADS), ((0, 2), (1, 4)), -0.2, 0.2), 0.5, 1.5),
        "gate_gain": jnp.clip(1.0 + 0.1 * jax.random.normal(seeds[12], (2, INNER), jnp.float32), 0.5, 1.5),
        "w_out": bell_draw(seeds[13], (2, D, INNER), INNER ** -0.5, 0.109375, ((0, 2), (2, 4))),
    }


epsilon = 1e-05
exact_mode = lax.Precision.HIGHEST

@jax.custom_vjp
def low(v):
    return lax.optimization_barrier(v.astype(jnp.bfloat16)).astype(jnp.float32)

@jax.custom_vjp
def low_back(v):
    return v

def low_keep(v):
    return (low(v), None)

def low_pass(kept, grad):
    return (grad,)

def back_keep(v):
    return (v, None)

def back_low(kept, grad):
    return (low(grad),)
low.defvjp(low_keep, low_pass)
low_back.defvjp(back_keep, back_low)

def matmul(left_side, right_side):
    return jnp.dot(left_side, right_side, precision=exact_mode)

def swish_value(values):
    return values * jax.nn.sigmoid(values)

def causal_mix(values, weight):
    row_count = values.shape[0]
    padded = jnp.pad(values, ((CONV - 1, 0), (0, 0)))
    summation = padded[0:row_count] * weight[:, 0]
    for offset in range(1, CONV):
        summation = summation + padded[offset:offset + row_count] * weight[:, offset]
    return summation

def span_step(decay_rate, carried, inputs):
    span_x, span_dt, span_b, span_c = inputs
    log_decay = span_dt * decay_rate[None, :]
    running = jnp.cumsum(log_decay, axis=0)
    spread = running[:, None, :] - running[None, :, :]
    length = span_dt.shape[0]
    causal = jnp.arange(length)[:, None] >= jnp.arange(length)[None, :]
    factors = jnp.exp(jnp.where(causal[:, :, None], spread, -jnp.inf))
    intersection = jnp.dot(span_c, span_b.T, precision=exact_mode)
    mixing = intersection[:, :, None] * factors * span_dt[None, :, :]
    inner_out = jnp.einsum('tsh,shp->thp', mixing, span_x, precision=exact_mode)
    carried_out = jnp.einsum('tn,hpn->thp', span_c, carried, precision=exact_mode)
    outputs = inner_out + jnp.exp(running)[:, :, None] * carried_out
    to_end = jnp.exp(running[-1][None, :] - running) * span_dt
    new_state = jnp.exp(running[-1])[:, None, None] * carried + jnp.einsum('sh,shp,sn->hpn', to_end, span_x, span_b, precision=exact_mode)
    return (new_state, outputs)

def scan_states(heads_x, step_sizes, decay_rate, b_in, c_in):
    row_count, head_count, head_width = heads_x.shape
    blocks = row_count // SPAN
    start_state = jnp.zeros((head_count, head_width, b_in.shape[1]), jnp.float32)
    pieces = (heads_x.reshape(blocks, SPAN, head_count, head_width), step_sizes.reshape(blocks, SPAN, head_count), b_in.reshape(blocks, SPAN, -1), c_in.reshape(blocks, SPAN, -1))
    end_state, outputs = lax.scan(jax.checkpoint(partial(span_step, decay_rate)), start_state, pieces)
    return outputs.reshape(row_count, head_count, head_width)

def mixer(weights, sequence):
    norm_gain, w_z, w_x, w_bc, w_dt, conv_x, conv_bc, dt_bias, a_log, skip_d, gate_gain, w_out = weights
    residual = low_back(sequence)
    rescale = lax.rsqrt(lax.optimization_barrier(jnp.mean(residual * residual, axis=-1, keepdims=True)) + epsilon)
    normed = low(residual * rescale * norm_gain)
    gate_in = low_back(matmul(normed, w_z))
    inner_raw = low(low_back(matmul(normed, w_x)))
    shared_raw = low(low_back(matmul(normed, w_bc)))
    step_raw = low_back(matmul(normed, w_dt))
    inner_act = swish_value(causal_mix(inner_raw, conv_x))
    shared_act = swish_value(causal_mix(shared_raw, conv_bc))
    step_sizes = jax.nn.softplus(step_raw + dt_bias)
    decay_rate = -jnp.exp(a_log)
    row_count = sequence.shape[0]
    heads_x = inner_act.reshape(row_count, HEADS, HEAD_DIM)
    states_out = scan_states(heads_x, step_sizes, decay_rate, shared_act[:, :STATE], shared_act[:, STATE:])
    mixed = (states_out + skip_d[None, :, None] * heads_x).reshape(row_count, INNER)
    gated = mixed * swish_value(gate_in)
    row_scale = lax.rsqrt(lax.optimization_barrier(jnp.mean(gated * gated, axis=-1, keepdims=True)) + epsilon)
    scaled = low(gated * gate_gain)
    summed = low_back(matmul(scaled, w_out.T))
    return low(residual + row_scale * summed)

def run_block(section_weights, inputs):
    return lax.map(partial(mixer, section_weights), inputs)

def reference(tokens, cotangent, norm_gain, w_z, w_x, w_bc, w_dt, conv_x, conv_bc, dt_bias, a_log, skip_d, gate_gain, w_out):
    weights = [member.astype(jnp.float32) for member in (norm_gain, w_z, w_x, w_bc, w_dt, conv_x, conv_bc, dt_bias, a_log, skip_d, gate_gain, w_out)]
    first_weights = tuple((member[0] for member in weights))
    second_weights = tuple((member[1] for member in weights))
    middle, back_first = jax.vjp(run_block, first_weights, tokens.astype(jnp.float32))
    ending, back_second = jax.vjp(run_block, second_weights, middle)
    grads_second, grad_middle = back_second(cotangent.astype(jnp.float32))
    grads_first, grad_tokens = back_first(grad_middle)
    block_outputs = jnp.stack([middle, ending]).astype(jnp.bfloat16)
    input_grads = jnp.stack([grad_tokens, grad_middle]).astype(jnp.bfloat16)
    stacked = [jnp.stack([one_grad, two_grad]) for one_grad, two_grad in zip(grads_first, grads_second)]
    return (block_outputs, input_grads, stacked[0], stacked[1], stacked[2], stacked[3], stacked[4], stacked[5], stacked[6], stacked[7], stacked[8], stacked[9], stacked[10], stacked[11])
```

```python
from functools import partial

import jax
import jax.numpy as jnp
from jax import lax
from jax.experimental import pallas as pl
from jax.experimental.pallas import tpu as pltpu
from jax.sharding import PartitionSpec as P

INNER = 3072
CONV = 4
CHUNK = 128
LANES = 128
ROWS = 256

epsilon = 1e-05
exact = lax.Precision.HIGHEST
f32 = jnp.float32
bf16 = jnp.bfloat16


def dot_nn(left, right, precision=None):
    return lax.dot_general(
        left, right, (((1,), (0,)), ((), ())), precision=precision, preferred_element_type=f32
    )


def dot_nt(left, right, precision=None):
    return lax.dot_general(
        left, right, (((1,), (1,)), ((), ())), precision=precision, preferred_element_type=f32
    )


def dot_tn(left, right):
    return lax.dot_general(left, right, (((0,), (0,)), ((), ())), preferred_element_type=f32)


def silu_parts(values):
    gate = jax.nn.sigmoid(values)
    return gate, values * gate


def silu_slope(values, gate):
    return gate * (1.0 + values * (1.0 - gate))


def head_groups(width, heads):
    head_width = width // heads
    per_group = max(LANES // head_width, 1)
    found = []
    for first in range(0, heads, per_group):
        count = min(per_group, heads - first)
        found.append((first, count, first * head_width, count * head_width))
    return found


def spread(tile, first, count, lanes):
    rows = tile.shape[0]
    head_width = lanes // count
    out = jnp.broadcast_to(tile[:, first : first + 1], (rows, lanes))
    lane = lax.broadcasted_iota(jnp.int32, (rows, lanes), 1)
    for k in range(1, count):
        column = jnp.broadcast_to(tile[:, first + k : first + k + 1], (rows, lanes))
        out = jnp.where(lane >= k * head_width, column, out)
    return out


def own_lanes(tile, k, count):
    if count == 1:
        return tile
    head_width = tile.shape[1] // count
    lane = lax.broadcasted_iota(jnp.int32, tile.shape, 1)
    inside = (lane >= k * head_width) & (lane < (k + 1) * head_width)
    return jnp.where(inside, tile, jnp.zeros_like(tile))


def triangle(keep):
    row = lax.broadcasted_iota(jnp.int32, (CHUNK, CHUNK), 0)
    column = lax.broadcasted_iota(jnp.int32, (CHUNK, CHUNK), 1)
    return keep(row, column)


def conv_kernel(
    heads,
    raw_x,
    raw_bc,
    edge_x,
    edge_bc,
    step_raw,
    dt_bias,
    rate,
    taps_x,
    taps_bc,
    pre_x,
    pre_bc,
    act_x,
    act_bc,
    dt_out,
    run_out,
    end_out,
    total_out,
    ext_x,
    ext_bc,
):
    step = pl.program_id(0)
    groups = head_groups(raw_x.shape[1], heads)
    state = act_bc.shape[1] // 2

    @pl.when(step == 0)
    def _():
        ext_x[0:8] = edge_x[...]
        ext_bc[0:8] = edge_bc[...]
        end_out[...] = jnp.zeros_like(end_out)
        total_out[...] = jnp.zeros_like(total_out)

    @pl.when(step > 0)
    def _():
        ext_x[0:8] = ext_x[ROWS : ROWS + 8]
        ext_bc[0:8] = ext_bc[ROWS : ROWS + 8]

    ext_x[8:] = raw_x[...].astype(f32)
    ext_bc[8:] = raw_bc[...].astype(f32)
    for ext, taps, pre, act in ((ext_x, taps_x, pre_x, act_x), (ext_bc, taps_bc, pre_bc, act_bc)):
        total = ext[5 : 5 + ROWS] * taps[0:1]
        for k in range(1, CONV):
            total = total + ext[5 + k : 5 + k + ROWS] * taps[k : k + 1]
        pre[...] = total.astype(bf16)
        act[...] = silu_parts(total)[1].astype(bf16)
    sizes = jax.nn.softplus(step_raw[...] + dt_bias[...])
    dt_out[...] = sizes
    lower = triangle(lambda t, s: t >= s).astype(f32)
    for sub in range(ROWS // CHUNK):
        at = slice(sub * CHUNK, (sub + 1) * CHUNK)
        dt = sizes[at]
        run = dot_nn(lower, dt * rate[...], exact)
        run_out[at] = run
        last = run[CHUNK - 1 : CHUNK]
        weight = jnp.exp(last - run) * dt
        decay = jnp.exp(last)
        b_turned = act_bc[at, :state].astype(f32).T.astype(bf16)
        for first, count, lane, lanes in groups:
            cols = slice(lane, lane + lanes)
            scaled = act_x[at, cols].astype(f32) * spread(weight, first, count, lanes)
            end_out[:, cols] = spread(decay, first, count, lanes) * end_out[:, cols] + dot_nn(
                b_turned, scaled.astype(bf16)
            )
        total_out[...] += jnp.broadcast_to(last, total_out.shape)


def full(shape):
    return pl.BlockSpec(shape, lambda i: (0,) * len(shape))


def rows_of(width, back=0):
    if back:
        return pl.BlockSpec((ROWS, width), lambda i: (back - 1 - i, 0))
    return pl.BlockSpec((ROWS, width), lambda i: (i, 0))


def params():
    return pltpu.CompilerParams(
        dimension_semantics=("arbitrary",), vmem_limit_bytes=48 * 1024 * 1024
    )


def conv_forward(heads, raw_x, raw_bc, edge_x, edge_bc, step_raw, dt_bias, rate, taps_x, taps_bc):
    count, width = raw_x.shape
    shared = raw_bc.shape[1]
    state = shared // 2
    return pl.pallas_call(
        partial(conv_kernel, heads),
        grid=(count // ROWS,),
        in_specs=[
            rows_of(width),
            rows_of(shared),
            full((8, width)),
            full((8, shared)),
            rows_of(LANES),
            full((1, LANES)),
            full((1, LANES)),
            full((CONV, width)),
            full((CONV, shared)),
        ],
        out_specs=[
            rows_of(width),
            rows_of(shared),
            rows_of(width),
            rows_of(shared),
            rows_of(LANES),
            rows_of(LANES),
            full((state, width)),
            full((8, LANES)),
        ],
        out_shape=[
            jax.ShapeDtypeStruct((count, width), bf16),
            jax.ShapeDtypeStruct((count, shared), bf16),
            jax.ShapeDtypeStruct((count, width), bf16),
            jax.ShapeDtypeStruct((count, shared), bf16),
            jax.ShapeDtypeStruct((count, LANES), f32),
            jax.ShapeDtypeStruct((count, LANES), f32),
            jax.ShapeDtypeStruct((state, width), f32),
            jax.ShapeDtypeStruct((8, LANES), f32),
        ],
        scratch_shapes=[
            pltpu.VMEM((8 + ROWS, width), f32),
            pltpu.VMEM((8 + ROWS, shared), f32),
        ],
        compiler_params=params(),
        cost_estimate=pl.CostEstimate(
            flops=2 * count * width * state,
            bytes_accessed=count * (width + shared) * 6,
            transcendentals=count * (width + shared),
        ),
        name="conv_forward",
    )(raw_x, raw_bc, edge_x, edge_bc, step_raw, dt_bias, rate, taps_x, taps_bc)


def mix_kernel(
    heads,
    act_x,
    act_bc,
    dt_in,
    run_in,
    gate_in,
    start,
    skip,
    gain,
    grad_in,
    mixed_out,
    scaled_out,
    sums_out,
    states_out,
    held,
):
    step = pl.program_id(0)
    groups = head_groups(act_x.shape[1], heads)
    state = act_bc.shape[1] // 2

    @pl.when(step == 0)
    def _():
        held[...] = start[...]

    causal = triangle(lambda t, s: t >= s)
    ones = jnp.ones((8, LANES), f32)
    for sub in range(ROWS // CHUNK):
        at = slice(sub * CHUNK, (sub + 1) * CHUNK)
        dt = dt_in[at]
        run = run_in[at]
        last = run[CHUNK - 1 : CHUNK]
        to_end = jnp.exp(last - run)
        decay = jnp.exp(last)
        turned = run.T
        b_part = act_bc[at, :state]
        c_part = act_bc[at, state:]
        b_turned = b_part.astype(f32).T.astype(bf16)
        product = dot_nt(c_part, b_part)
        states_out[sub] = held[...].astype(bf16)
        squares = jnp.zeros((CHUNK, LANES), f32)
        pairs = jnp.zeros((CHUNK, LANES), f32)
        for first, count, lane, lanes in groups:
            cols = slice(lane, lane + lanes)
            x_part = act_x[at, cols].astype(f32)
            stepped = x_part * spread(dt, first, count, lanes)
            low = stepped.astype(bf16)
            weights = []
            stacked = []
            for k in range(count):
                h = first + k
                gap = jnp.broadcast_to(run[:, h : h + 1], (CHUNK, CHUNK)) - turned[h : h + 1]
                factor = jnp.exp(jnp.where(causal, gap, -jnp.inf))
                weights.append((product * factor).astype(bf16))
                stacked.append(own_lanes(low, k, count))
            mixed = dot_nn(jnp.concatenate(weights, axis=1), jnp.concatenate(stacked, axis=0))
            before = held[:, cols]
            mixed = mixed + jnp.exp(spread(run, first, count, lanes)) * dot_nn(
                c_part, before.astype(bf16)
            )
            mixed = mixed + skip[:, cols] * x_part
            held[:, cols] = spread(decay, first, count, lanes) * before + dot_nn(
                b_turned, (stepped * spread(to_end, first, count, lanes)).astype(bf16)
            )
            gated = mixed * silu_parts(gate_in[at, cols])[1]
            scaled = (gated * gain[:, cols]).astype(bf16)
            mixed_out[at, cols] = mixed.astype(bf16)
            scaled_out[at, cols] = scaled
            square = gated * gated
            pair = scaled.astype(f32) * grad_in[at, cols]
            if lanes < LANES:
                fill = jnp.zeros((CHUNK, LANES - lanes), f32)
                square = jnp.concatenate([square, fill], axis=1)
                pair = jnp.concatenate([pair, fill], axis=1)
            squares = squares + square
            pairs = pairs + pair
        square_row = dot_nt(ones, squares, exact)
        pair_row = dot_nt(ones, pairs, exact)
        row = lax.broadcasted_iota(jnp.int32, (8, CHUNK), 0)
        sums_out[:, at] = jnp.where(row == 0, square_row, pair_row)


def mix_forward(heads, act_x, act_bc, dt, run, gate_in, start, skip, gain, grad_in):
    count, width = act_x.shape
    shared = act_bc.shape[1]
    state = shared // 2
    subs = ROWS // CHUNK
    return pl.pallas_call(
        partial(mix_kernel, heads),
        grid=(count // ROWS,),
        in_specs=[
            rows_of(width),
            rows_of(shared),
            rows_of(LANES),
            rows_of(LANES),
            rows_of(width),
            full((state, width)),
            full((1, width)),
            full((1, width)),
            rows_of(width),
        ],
        out_specs=[
            rows_of(width),
            rows_of(width),
            pl.BlockSpec((8, ROWS), lambda i: (0, i)),
            pl.BlockSpec((subs, state, width), lambda i: (i, 0, 0)),
        ],
        out_shape=[
            jax.ShapeDtypeStruct((count, width), bf16),
            jax.ShapeDtypeStruct((count, width), bf16),
            jax.ShapeDtypeStruct((8, count), f32),
            jax.ShapeDtypeStruct((count // CHUNK, state, width), bf16),
        ],
        scratch_shapes=[pltpu.VMEM((state, width), f32)],
        compiler_params=params(),
        cost_estimate=pl.CostEstimate(
            flops=8 * count * width * state,
            bytes_accessed=count * width * 16,
            transcendentals=count * heads * CHUNK,
        ),
        name="mix_forward",
    )(act_x, act_bc, dt, run, gate_in, start, skip, gain, grad_in)


def gate_kernel(
    heads,
    grad_in,
    scales,
    gate_in,
    mixed_in,
    act_x,
    act_bc,
    run_in,
    gain,
    grad_mixed,
    grad_gate,
    gain_sum,
    skip_sum,
    adjoint,
):
    groups = head_groups(act_x.shape[1], heads)
    state = act_bc.shape[1] // 2

    @pl.when(pl.program_id(0) == 0)
    def _():
        gain_sum[...] = jnp.zeros_like(gain_sum)
        skip_sum[...] = jnp.zeros_like(skip_sum)
        adjoint[...] = jnp.zeros_like(adjoint)

    for sub in reversed(range(ROWS // CHUNK)):
        at = slice(sub * CHUNK, (sub + 1) * CHUNK)
        run = run_in[at]
        grown = jnp.exp(run)
        decay = grown[CHUNK - 1 : CHUNK]
        c_turned = act_bc[at, state:].astype(f32).T.astype(bf16)
        row_scale = scales[at, 0:1]
        row_pull = scales[at, 1:2]
        for first, count, lane, lanes in groups:
            cols = slice(lane, lane + lanes)
            gate = gate_in[at, cols]
            mixed = mixed_in[at, cols].astype(f32)
            share, active = silu_parts(gate)
            gated = mixed * active
            d_scaled = grad_in[at, cols] * row_scale
            d_gated = d_scaled * gain[:, cols] - row_pull * gated
            d_mixed = d_gated * active
            low = d_mixed.astype(bf16)
            grad_mixed[at, cols] = low
            grad_gate[at, cols] = (d_gated * mixed * silu_slope(gate, share)).astype(bf16)
            gain_sum[0:1, cols] += jnp.sum(d_scaled * gated, axis=0, keepdims=True)
            skip_sum[0:1, cols] += jnp.sum(
                d_mixed * act_x[at, cols].astype(f32), axis=0, keepdims=True
            )
            adjoint[:, cols] = spread(decay, first, count, lanes) * adjoint[:, cols] + dot_nn(
                c_turned, (d_mixed * spread(grown, first, count, lanes)).astype(bf16)
            )


def gate_backward(heads, grad_in, scales, gate_in, mixed, act_x, act_bc, run, gain):
    count, width = act_x.shape
    shared = act_bc.shape[1]
    state = shared // 2
    steps = count // ROWS
    return pl.pallas_call(
        partial(gate_kernel, heads),
        grid=(steps,),
        in_specs=[
            rows_of(width, steps),
            rows_of(2, steps),
            rows_of(width, steps),
            rows_of(width, steps),
            rows_of(width, steps),
            rows_of(shared, steps),
            rows_of(LANES, steps),
            full((1, width)),
        ],
        out_specs=[
            rows_of(width, steps),
            rows_of(width, steps),
            full((8, width)),
            full((8, width)),
            full((state, width)),
        ],
        out_shape=[
            jax.ShapeDtypeStruct((count, width), bf16),
            jax.ShapeDtypeStruct((count, width), bf16),
            jax.ShapeDtypeStruct((8, width), f32),
            jax.ShapeDtypeStruct((8, width), f32),
            jax.ShapeDtypeStruct((state, width), f32),
        ],
        compiler_params=params(),
        cost_estimate=pl.CostEstimate(
            flops=2 * count * width * state,
            bytes_accessed=count * width * 16,
            transcendentals=count * width,
        ),
        name="gate_backward",
    )(grad_in, scales, gate_in, mixed, act_x, act_bc, run, gain)


def states_kernel(
    heads,
    grad_mixed,
    act_x,
    act_bc,
    pre_x,
    pre_bc,
    raw_x,
    raw_bc,
    edge_x,
    edge_bc,
    dt_in,
    run_in,
    step_raw,
    dt_bias,
    rate_rows,
    states_in,
    end_in,
    skip,
    taps_x,
    taps_bc,
    members,
    d_raw_x,
    d_raw_bc,
    d_step,
    tail_x,
    tail_bc,
    back_x,
    back_bc,
    tap_sum_x,
    tap_sum_bc,
    rate_sum,
    bias_sum,
    adjoint,
    d_pre_x,
    d_pre_bc,
    rows_ref,
    inside_ref,
    carry_ref,
    square_ref,
):
    step = pl.program_id(0)
    steps = pl.num_programs(0)
    groups = head_groups(act_x.shape[1], heads)
    state = act_bc.shape[1] // 2
    padded = members.shape[0]

    @pl.when(step == 0)
    def _():
        adjoint[...] = end_in[...]
        d_pre_x[8:16] = jnp.zeros((8, d_pre_x.shape[1]), f32)
        d_pre_bc[8:16] = jnp.zeros((8, d_pre_bc.shape[1]), f32)
        tap_sum_x[...] = jnp.zeros_like(tap_sum_x)
        tap_sum_bc[...] = jnp.zeros_like(tap_sum_bc)
        rate_sum[...] = jnp.zeros_like(rate_sum)
        bias_sum[...] = jnp.zeros_like(bias_sum)
        rows_ref[...] = jnp.zeros_like(rows_ref)
        square_ref[...] = jnp.zeros_like(square_ref)

    upto = triangle(lambda s, t: s <= t)
    not_before = triangle(lambda s, t: s >= t).astype(f32)
    before = triangle(lambda s, t: s < t).astype(f32)
    ones = jnp.ones((8, CHUNK), bf16)
    for sub in reversed(range(ROWS // CHUNK)):
        at = slice(sub * CHUNK, (sub + 1) * CHUNK)
        dt = dt_in[at]
        run = run_in[at]
        last = run[CHUNK - 1 : CHUNK]
        grown = jnp.exp(run)
        decay = grown[CHUNK - 1 : CHUNK]
        to_end = jnp.exp(last - run)
        run_turned = run.T
        dt_turned = dt.T[0:padded]
        high = dt_turned.astype(bf16)
        rest = dt_turned - high.astype(f32)
        middle = rest.astype(bf16)
        low_part = (rest - middle.astype(f32)).astype(bf16)
        dt_split = jnp.concatenate([high, middle, low_part], axis=0)
        b_part = act_bc[at, :state]
        c_part = act_bc[at, state:]
        c_turned = c_part.astype(f32).T.astype(bf16)
        product = dot_nt(b_part, c_part)
        d_product = jnp.zeros((CHUNK, CHUNK), f32)
        d_b = jnp.zeros((CHUNK, state), f32)
        d_c = jnp.zeros((CHUNK, state), f32)
        d_pre_x[CHUNK + 8 : CHUNK + 16] = d_pre_x[8:16]
        d_pre_bc[CHUNK + 8 : CHUNK + 16] = d_pre_bc[8:16]
        through = []
        for first, count, lane, lanes in groups:
            cols = slice(lane, lane + lanes)
            x_low = act_x[at, cols]
            x_part = x_low.astype(f32)
            dy_low = grad_mixed[at, cols]
            dy = dy_low.astype(f32)
            dt_wide = spread(dt, first, count, lanes)
            ending = spread(to_end, first, count, lanes)
            growing = spread(grown, first, count, lanes)
            lam = adjoint[:, cols]
            lam_low = lam.astype(bf16)
            held_low = states_in[sub][:, cols]
            weights = []
            stacked = []
            for k in range(count):
                h = first + k
                gap = run_turned[h : h + 1] - jnp.broadcast_to(run[:, h : h + 1], (CHUNK, CHUNK))
                factor = jnp.exp(jnp.where(upto, gap, -jnp.inf))
                weights.append((product * factor).astype(bf16))
                stacked.append(own_lanes(dy_low, k, count))
                paired = dot_nt(own_lanes(x_low, k, count), dy_low) * factor
                d_product = d_product + paired * jnp.broadcast_to(dt[:, h : h + 1], (CHUNK, CHUNK))
                inside = (paired * product).astype(bf16)
                split_rows = dot_nn(dt_split, inside)
                rows_ref[h : h + 1] = (
                    split_rows[h : h + 1]
                    + split_rows[padded + h : padded + h + 1]
                    + split_rows[2 * padded + h : 2 * padded + h + 1]
                )
                inside_ref[h : h + 1] = dot_nt(ones, inside)[0:1]
            d_stepped = dot_nn(jnp.concatenate(weights, axis=1), jnp.concatenate(stacked, axis=0))
            from_end = ending * dot_nn(b_part, lam_low)
            d_x = dt_wide * (d_stepped + from_end) + skip[:, cols] * dy
            dy_grown = dy * growing
            dy_grown_low = dy_grown.astype(bf16)
            carry_ref[0, :, cols] = (x_part * from_end).astype(bf16)
            carry_ref[1, :, cols] = (dy_grown * dot_nn(c_part, held_low)).astype(bf16)
            d_b = d_b + dot_nt((x_part * dt_wide * ending).astype(bf16), lam_low)
            d_c = d_c + dot_nt(dy_grown_low, held_low)
            wide_decay = spread(decay, first, count, lanes)
            lam_decayed = wide_decay * lam
            through.append(
                jnp.sum(lam_decayed * held_low.astype(f32), axis=0, keepdims=True)
            )
            adjoint[:, cols] = lam_decayed + dot_nn(c_turned, dy_grown_low)
            pre = pre_x[at, cols].astype(f32)
            d_pre_x[8 : CHUNK + 8, cols] = d_x * silu_slope(pre, jax.nn.sigmoid(pre))
        member = members[...]
        kept = dot_nt(member, carry_ref[0])
        fed = dot_nt(member, carry_ref[1])
        wide_row = jnp.concatenate(through, axis=1)
        across = dot_nt(member.astype(f32), jnp.broadcast_to(wide_row, (8, wide_row.shape[1])), exact)
        inside_rows = inside_ref[...]
        d_log = (
            dot_nn(rows_ref[...] - dt_turned * inside_rows + fed, not_before, exact)
            + dot_nn(dt_turned * kept, before, exact)
            + across[:, 0:1]
        )
        d_log_rate = d_log * rate_rows[...]
        rate_sum[...] += d_log_rate * dt_turned
        square_ref[0:padded] = d_log_rate + inside_rows + kept
        d_step_exact = square_ref[...].T * jax.nn.sigmoid(step_raw[at] + dt_bias[...])
        bias_sum[0:1] += jnp.sum(d_step_exact, axis=0, keepdims=True)
        d_step[at] = d_step_exact.astype(bf16)
        d_product_low = d_product.astype(bf16)
        d_b = d_b + dot_nn(d_product_low, c_part)
        d_c = d_c + dot_nn(d_product.T.astype(bf16), b_part)
        pre = pre_bc[at].astype(f32)
        slope = silu_slope(pre, jax.nn.sigmoid(pre))
        d_pre_bc[8 : CHUNK + 8, :state] = d_b * slope[:, :state]
        d_pre_bc[8 : CHUNK + 8, state:] = d_c * slope[:, state:]
        for d_pre, raw, taps, d_raw, tap_sum, tail in (
            (d_pre_x, raw_x, taps_x, d_raw_x, tap_sum_x, tail_x),
            (d_pre_bc, raw_bc, taps_bc, d_raw_bc, tap_sum_bc, tail_bc),
        ):
            values = raw[at].astype(f32)
            total = jnp.zeros_like(values)
            for k in range(CONV):
                moved = d_pre[11 - k : 11 - k + CHUNK]
                total = total + moved * taps[k : k + 1]
                tap_sum[k : k + 1] += jnp.sum(values * moved, axis=0, keepdims=True)
            d_raw[at] = total.astype(bf16)
            if sub == ROWS // CHUNK - 1:

                @pl.when(step == 0)
                def _():
                    tail[...] = total[CHUNK - 8 :]

    @pl.when(step == steps - 1)
    def _():
        for d_pre, edge, taps, tap_sum, back in (
            (d_pre_x, edge_x, taps_x, tap_sum_x, back_x),
            (d_pre_bc, edge_bc, taps_bc, tap_sum_bc, back_bc),
        ):
            d_pre[0:8] = jnp.zeros((8, d_pre.shape[1]), f32)
            values = edge[...]
            total = jnp.zeros_like(values)
            for k in range(CONV):
                moved = d_pre[3 - k : 11 - k]
                total = total + moved * taps[k : k + 1]
                tap_sum[k : k + 1] += jnp.sum(values * moved, axis=0, keepdims=True)
            back[...] = total


def states_backward(
    heads,
    grad_mixed,
    act_x,
    act_bc,
    pre_x,
    pre_bc,
    raw_x,
    raw_bc,
    edge_x,
    edge_bc,
    dt,
    run,
    step_raw,
    dt_bias,
    rate,
    states,
    end,
    skip,
    taps_x,
    taps_bc,
):
    count, width = act_x.shape
    shared = act_bc.shape[1]
    state = shared // 2
    steps = count // ROWS
    subs = ROWS // CHUNK
    padded = -(-heads // 16) * 16
    head_of = jnp.arange(width)[None, :] // (width // heads)
    members = (jnp.arange(padded)[:, None] == head_of).astype(bf16)
    rate_rows = jnp.broadcast_to(rate[0, :padded, None], (padded, CHUNK))
    return pl.pallas_call(
        partial(states_kernel, heads),
        grid=(steps,),
        in_specs=[
            rows_of(width, steps),
            rows_of(width, steps),
            rows_of(shared, steps),
            rows_of(width, steps),
            rows_of(shared, steps),
            rows_of(width, steps),
            rows_of(shared, steps),
            full((8, width)),
            full((8, shared)),
            rows_of(LANES, steps),
            rows_of(LANES, steps),
            rows_of(LANES, steps),
            full((1, LANES)),
            full((padded, CHUNK)),
            pl.BlockSpec((subs, state, width), lambda i: (steps - 1 - i, 0, 0)),
            full((state, width)),
            full((1, width)),
            full((CONV, width)),
            full((CONV, shared)),
            full((padded, width)),
        ],
        out_specs=[
            rows_of(width, steps),
            rows_of(shared, steps),
            rows_of(LANES, steps),
            full((8, width)),
            full((8, shared)),
            full((8, width)),
            full((8, shared)),
            full((8, width)),
            full((8, shared)),
            full((padded, CHUNK)),
            full((8, LANES)),
        ],
        out_shape=[
            jax.ShapeDtypeStruct((count, width), bf16),
            jax.ShapeDtypeStruct((count, shared), bf16),
            jax.ShapeDtypeStruct((count, LANES), bf16),
            jax.ShapeDtypeStruct((8, width), f32),
            jax.ShapeDtypeStruct((8, shared), f32),
            jax.ShapeDtypeStruct((8, width), f32),
            jax.ShapeDtypeStruct((8, shared), f32),
            jax.ShapeDtypeStruct((8, width), f32),
            jax.ShapeDtypeStruct((8, shared), f32),
            jax.ShapeDtypeStruct((padded, CHUNK), f32),
            jax.ShapeDtypeStruct((8, LANES), f32),
        ],
        scratch_shapes=[
            pltpu.VMEM((state, width), f32),
            pltpu.VMEM((CHUNK + 16, width), f32),
            pltpu.VMEM((CHUNK + 16, shared), f32),
            pltpu.VMEM((padded, CHUNK), f32),
            pltpu.VMEM((padded, CHUNK), f32),
            pltpu.VMEM((2, CHUNK, width), bf16),
            pltpu.VMEM((CHUNK, CHUNK), f32),
        ],
        compiler_params=params(),
        cost_estimate=pl.CostEstimate(
            flops=20 * count * width * state,
            bytes_accessed=count * width * 16,
            transcendentals=count * heads * CHUNK * 2,
        ),
        name="states_backward",
    )(
        grad_mixed,
        act_x,
        act_bc,
        pre_x,
        pre_bc,
        raw_x,
        raw_bc,
        edge_x,
        edge_bc,
        dt,
        run,
        step_raw,
        dt_bias,
        rate_rows,
        states,
        end,
        skip,
        taps_x,
        taps_bc,
        members,
    )


def moved_along(block, axis, distance):
    size = lax.axis_size(axis)
    route = [(i - distance, i) for i in range(size) if 0 <= i - distance < size]
    return lax.ppermute(block, axis, route)


def swapped(block):
    return lax.ppermute(block, "section", [(0, 1), (1, 0)])


def both_blocks(weight):
    size = lax.axis_size("seq")
    rows = weight.shape[0] // size
    part = lax.dynamic_slice_in_dim(weight, lax.axis_index("seq") * rows, rows, 0)
    return lax.all_gather(part, ("section", "seq"), axis=0, tiled=True).reshape(
        (lax.axis_size("section"),) + weight.shape
    )


def entering(end, total, forward):
    size = lax.axis_size("seq")
    place = lax.axis_index("seq")
    ends = lax.all_gather(end.astype(bf16), "seq")
    totals = lax.all_gather(total, "seq")
    state = jnp.zeros_like(end)
    order = range(size) if forward else reversed(range(size))
    for other in order:
        ahead = other < place if forward else other > place
        new = jnp.exp(totals[other])[None, :] * state + ends[other].astype(f32)
        state = jnp.where(ahead, new, state)
    return state


def padded_edge(edge):
    return jnp.pad(edge.astype(f32), ((8 - edge.shape[0], 0), (0, 0)))


def block_forward(x, rescale, normed, weights, grad_in):
    heads = weights["a_log"].shape[0]
    width = weights["w_x"].shape[1]
    raw_x = dot_nn(normed, weights["w_x"]).astype(bf16)
    raw_bc = dot_nn(normed, weights["w_bc"]).astype(bf16)
    step_raw = dot_nn(normed, weights["w_dt"])
    edge = jnp.concatenate([raw_x[-(CONV - 1) :], raw_bc[-(CONV - 1) :]], axis=1)
    edge = padded_edge(moved_along(edge, "seq", 1))
    edge_x, edge_bc = edge[:, :width], edge[:, width:]
    gate_in = dot_nn(normed, weights["w_z"])
    pre_x, pre_bc, act_x, act_bc, dt, run, end, total = conv_forward(
        heads, raw_x, raw_bc, edge_x, edge_bc, step_raw, weights["dt_bias"], weights["rate"],
        weights["taps_x"], weights["taps_bc"],
    )
    wide_total = jnp.repeat(total[0, :heads], width // heads)
    start = entering(end, wide_total, True)
    mixed, scaled, sums, states = mix_forward(
        heads, act_x, act_bc, dt, run, gate_in, start, weights["skip"], weights["gain"], grad_in
    )
    kept = dict(
        raw_x=raw_x, raw_bc=raw_bc, step_raw=step_raw, edge_x=edge_x, edge_bc=edge_bc,
        gate_in=gate_in, pre_x=pre_x, pre_bc=pre_bc, act_x=act_x, act_bc=act_bc, dt=dt, run=run,
        wide_total=wide_total, mixed=mixed, scaled=scaled, states=states, normed=normed,
        rescale=rescale,
    )
    part = dot_nt(scaled, weights["w_out"]).astype(bf16)
    return part, sums[0:2], kept


def block_backward(grad, grad_in, row_scale, d_row, kept, weights):
    heads = weights["a_log"].shape[0]
    width = weights["w_x"].shape[1]
    count = grad.shape[0]
    pull = d_row * row_scale * row_scale * row_scale / INNER
    grad_mixed, grad_gate, gain_sum, skip_sum, adjoint = gate_backward(
        heads, grad_in, jnp.stack([row_scale, pull], axis=1), kept["gate_in"], kept["mixed"],
        kept["act_x"], kept["act_bc"], kept["run"], weights["gain"],
    )
    end = entering(adjoint, kept["wide_total"], False)
    (
        d_raw_x, d_raw_bc, d_step, tail_x, tail_bc, back_x, back_bc, taps_x, taps_bc, rate_sum,
        bias_sum,
    ) = states_backward(
        heads, grad_mixed, kept["act_x"], kept["act_bc"], kept["pre_x"], kept["pre_bc"],
        kept["raw_x"], kept["raw_bc"], kept["edge_x"], kept["edge_bc"], kept["dt"], kept["run"],
        kept["step_raw"], weights["dt_bias"], weights["rate"], kept["states"], end,
        weights["skip"], weights["taps_x"], weights["taps_bc"],
    )
    back = moved_along(jnp.concatenate([back_x, back_bc], axis=1), "seq", -1)
    d_raw_x = d_raw_x.at[count - 8 :].set((tail_x + back[:, :width]).astype(bf16))
    d_raw_bc = d_raw_bc.at[count - 8 :].set((tail_bc + back[:, width:]).astype(bf16))
    normed = kept["normed"]
    d_summed = (row_scale[:, None] * grad.astype(f32)).astype(bf16)
    grads = dict(
        w_out=dot_tn(d_summed, kept["scaled"]).astype(bf16),
        w_z=dot_tn(normed, grad_gate).astype(bf16),
        w_x=dot_tn(normed, d_raw_x).astype(bf16),
        w_bc=dot_tn(normed, d_raw_bc).astype(bf16),
        w_dt=dot_tn(normed, d_step)[:, :heads].astype(bf16),
        conv_x=taps_x[:CONV],
        conv_bc=taps_bc[:CONV],
        dt_bias=bias_sum[0, :heads],
        a_log=jnp.sum(rate_sum[:heads], axis=1),
        skip=jnp.sum(skip_sum[0].reshape(heads, width // heads), axis=1),
        gain=gain_sum[0],
    )
    part = (
        dot_nt(grad_gate, weights["w_z"])
        + dot_nt(d_raw_x, weights["w_x"])
        + dot_nt(d_step, weights["w_dt"])
    ).astype(bf16)
    return jnp.concatenate([part, d_raw_bc], axis=1), grads


def norm_forward(x, gain):
    rescale = lax.rsqrt(jnp.mean(x * x, axis=-1, keepdims=True) + epsilon)
    return rescale, (x * rescale * gain).astype(bf16)


def norm_backward(share, x, rescale, grad, gain, w_bc):
    width = x.shape[1]
    d_normed = share[:, :width].astype(f32) + dot_nt(share[:, width:], w_bc)
    unit = x * rescale
    h = d_normed * gain
    gain_part = jnp.sum(d_normed * unit, axis=0)
    out = grad + rescale * (h - unit * jnp.mean(h * unit, axis=-1, keepdims=True))
    return out.astype(bf16), gain_part


def shards(
    tokens, cotangent, norm_gain, w_z, w_x, w_bc, w_dt, conv_x, conv_bc, dt_bias, a_log, skip_d,
    gate_gain, w_out,
):
    section = lax.axis_index("section")
    count, model = tokens.shape[1:]
    head_size = lax.axis_size("head")
    head_at = lax.axis_index("head")
    heads = a_log.shape[1]
    width = w_x.shape[2]
    share = model // head_size
    row_share = count // head_size
    gathered = dict(
        w_x=both_blocks(w_x[0]),
        w_bc=both_blocks(w_bc[0]),
        w_dt=both_blocks(jnp.pad(w_dt[0], ((0, 0), (0, LANES - heads)))),
        w_z=both_blocks(w_z[0]),
        w_out=both_blocks(w_out[0]),
    )
    small = lax.all_gather(
        jnp.concatenate(
            [
                norm_gain[0], conv_x[0].T.reshape(-1), conv_bc[0].T.reshape(-1), dt_bias[0],
                a_log[0], skip_d[0], gate_gain[0],
            ]
        ),
        "section",
    )
    weights = []
    for b in range(2):
        block = {name: value[b] for name, value in gathered.items()}
        at = 0

        def take(size):
            nonlocal at
            at += size
            return small[b, at - size : at]

        block["norm"] = take(model)
        block["taps_x"] = take(CONV * width).reshape(CONV, width)
        block["taps_bc"] = take(CONV * w_bc.shape[2]).reshape(CONV, w_bc.shape[2])
        block["dt_bias"] = jnp.pad(take(heads), (0, LANES - heads))[None]
        block["a_log"] = take(heads)
        block["rate"] = jnp.pad(-jnp.exp(block["a_log"]), (0, LANES - heads))[None]
        block["skip"] = jnp.repeat(take(heads), width // heads)[None]
        block["gain"] = take(width)[None]
        weights.append(block)

    def own_rows(array):
        return lax.dynamic_slice_in_dim(array, head_at * row_share, row_share, 0)

    def own_columns(array):
        return lax.dynamic_slice_in_dim(array, head_at * share, share, 1)

    first_low = lax.dynamic_index_in_dim(tokens, section, 0, False)
    last_grad = lax.dynamic_index_in_dim(cotangent, section, 0, False)
    first = first_low.astype(f32)
    rescale, normed = norm_forward(first, weights[0]["norm"])
    nothing = jnp.zeros((count, width), f32)
    part, sums, kept_first = block_forward(first, rescale, normed, weights[0], nothing)
    squares = lax.psum(sums[0], "head")
    scale_first = lax.rsqrt(squares / INNER + epsilon)
    summed = lax.psum_scatter(part, "head", scatter_dimension=0, tiled=True).astype(f32)
    second_share = (own_rows(first) + own_rows(scale_first)[:, None] * summed).astype(bf16)
    second_low = lax.all_gather(second_share, "head", axis=0, tiled=True)
    second = second_low.astype(f32)

    grad_second = dot_nn(last_grad, weights[1]["w_out"])
    rescale, normed = norm_forward(second, weights[1]["norm"])
    part, sums, kept_second = block_forward(second, rescale, normed, weights[1], grad_second)
    squares, d_row = lax.psum(sums, "head")
    scale_second = lax.rsqrt(squares / INNER + epsilon)
    summed = lax.psum_scatter(part, "head", scatter_dimension=1, tiled=True).astype(f32)
    last_share = (own_columns(second) + scale_second[:, None] * summed).astype(bf16)

    part, grads_second = block_backward(
        last_grad, grad_second, scale_second, d_row, kept_second, weights[1]
    )
    part = lax.psum_scatter(part, "head", scatter_dimension=0, tiled=True)
    middle_share, norm_second = norm_backward(
        part, own_rows(second), own_rows(kept_second["rescale"]), own_rows(last_grad).astype(f32),
        weights[1]["norm"], weights[1]["w_bc"],
    )
    middle_grad = lax.all_gather(middle_share, "head", axis=0, tiled=True)

    grad_first = dot_nn(middle_grad, weights[0]["w_out"])
    d_row = jnp.sum(middle_grad.astype(f32) * (second - first), axis=1) / scale_first
    part, grads_first = block_backward(
        middle_grad, grad_first, scale_first, d_row, kept_first, weights[0]
    )
    part = lax.psum_scatter(part, "head", scatter_dimension=0, tiled=True)
    first_share, norm_first = norm_backward(
        part, own_rows(first), own_rows(kept_first["rescale"]), own_rows(middle_grad).astype(f32),
        weights[0]["norm"], weights[0]["w_bc"],
    )

    def to_columns(rows):
        pieces = rows.reshape(row_share, head_size, share).swapaxes(0, 1)
        return lax.all_to_all(pieces, "head", 0, 0).reshape(count, share)

    def by_section(of_first, of_second):
        sent = jnp.where(section == 0, of_second, of_first)
        own = jnp.where(section == 0, of_first, of_second)
        arrived = swapped(sent)
        return jnp.where(
            section == 0, jnp.stack([own, arrived]), jnp.stack([arrived, own])
        )

    block_outputs = by_section(own_columns(second_low), last_share)
    input_grads = by_section(to_columns(first_share), own_columns(middle_grad))

    def summed_rows(name):
        both = jnp.concatenate([grads_first[name], grads_second[name]], axis=0)
        return lax.psum_scatter(both, ("section", "seq"), scatter_dimension=0, tiled=True).astype(
            f32
        )

    shared = [
        lax.psum_scatter(block["w_bc"], "head", scatter_dimension=1, tiled=True)
        for block in (grads_first, grads_second)
    ]
    grads_first["w_bc"], grads_second["w_bc"] = shared
    local = jnp.stack(
        [
            jnp.concatenate(
                [
                    block["conv_x"].reshape(-1), block["dt_bias"], block["a_log"], block["skip"],
                    block["gain"],
                ]
            )
            for block in (grads_first, grads_second)
        ]
    )
    whole = jnp.stack(
        [
            jnp.concatenate([norm, block["conv_bc"].reshape(-1)])
            for norm, block in ((norm_first, grads_first), (norm_second, grads_second))
        ]
    )
    local = lax.dynamic_index_in_dim(lax.psum(local, ("section", "seq")), section, 0, False)
    whole = lax.dynamic_index_in_dim(lax.psum(whole, ("section", "seq", "head")), section, 0, False)
    at = CONV * width
    return (
        block_outputs[None],
        input_grads[None],
        lax.dynamic_slice_in_dim(whole, head_at * share, share, 0)[None],
        summed_rows("w_z")[None],
        summed_rows("w_x")[None],
        summed_rows("w_bc")[None],
        summed_rows("w_dt")[None],
        local[:at].reshape(CONV, width).T[None],
        whole[model:].reshape(CONV, w_bc.shape[2]).T[None],
        local[at : at + heads][None],
        local[at + heads : at + 2 * heads][None],
        local[at + 2 * heads : at + 3 * heads][None],
        local[at + 3 * heads :][None],
        summed_rows("w_out")[None],
    )


def solution(mesh):
    placed = (
        P(None, "seq", None),
        P(None, "seq", None),
        P("section", None),
        P("section", None, "head"),
        P("section", None, "head"),
        P("section", None, None),
        P("section", None, "head"),
        P("section", "head", None),
        P("section", None, None),
        P("section", "head"),
        P("section", "head"),
        P("section", "head"),
        P("section", "head"),
        P("section", None, "head"),
    )
    return jax.shard_map(
        shards,
        mesh=mesh,
        in_specs=placed,
        out_specs=(
            P("section", None, "seq", "head"),
            P("section", None, "seq", "head"),
            P("section", "head"),
            P("section", "seq", "head"),
            P("section", "seq", "head"),
            P("section", "seq", "head"),
            P("section", "seq", "head"),
            P("section", "head", None),
            P("section", None, None),
            P("section", "head"),
            P("section", "head"),
            P("section", "head"),
            P("section", "head"),
            P("section", "seq", "head"),
        ),
        check_vma=False,
    )
```

```python
from functools import partial

import jax
import jax.numpy as jnp
from jax import lax
from jax.experimental import pallas as pl
from jax.experimental.pallas import tpu as pltpu
from jax.sharding import PartitionSpec as P

INNER = 3072
CONV = 4
CHUNK = 128
LANES = 128
ROWS = 256

epsilon = 1e-05
exact = lax.Precision.HIGHEST
f32 = jnp.float32
bf16 = jnp.bfloat16


def dot_nn(left, right, precision=None):
    return lax.dot_general(
        left, right, (((1,), (0,)), ((), ())), precision=precision, preferred_element_type=f32
    )


def dot_nt(left, right, precision=None):
    return lax.dot_general(
        left, right, (((1,), (1,)), ((), ())), precision=precision, preferred_element_type=f32
    )


def dot_tn(left, right):
    return lax.dot_general(left, right, (((0,), (0,)), ((), ())), preferred_element_type=f32)


def silu_parts(values):
    gate = jax.nn.sigmoid(values)
    return gate, values * gate


def silu_slope(values, gate):
    return gate * (1.0 + values * (1.0 - gate))


def weight_fetch(block, sources, held, sem):
    here = lax.axis_index("section") == block
    away = jnp.logical_not(here)

    @pl.when(here)
    def _():
        pltpu.make_async_copy(sources[0], held, sem).start()

    place = lax.axis_index("seq")
    if len(sources) == 3:
        rows = sources[1].shape[1]
        for piece in range(4):
            target = held.at[piece * rows : (piece + 1) * rows]
            for k in range(2):

                @pl.when(away & (lax.rem(place + piece, 2) == k))
                def _():
                    pltpu.make_async_copy(sources[1 + k].at[piece // 2], target, sem).start()

        return
    rows = sources[1].shape[0]
    for piece in range(4):
        target = held.at[piece * rows : (piece + 1) * rows]
        for k, bits in enumerate((0, 2, 1, 3)):
            bit_low = lax.rem(place + piece, 2) == bits % 2
            bit_high = lax.rem(place // 2 + piece // 2, 2) == bits // 2

            @pl.when(away & bit_low & bit_high)
            def _():
                pltpu.make_async_copy(sources[1 + k], target, sem).start()


def weight_wait(sources, held, sem):
    pltpu.make_async_copy(sources[0], held, sem).wait()


def anywhere():
    return pl.BlockSpec(memory_space=pl.ANY)


def weight_scratch(own):
    return [pltpu.VMEM(own.shape, own.dtype), pltpu.SemaphoreType.DMA]


def head_groups(width, heads):
    head_width = width // heads
    per_group = max(LANES // head_width, 1)
    found = []
    for first in range(0, heads, per_group):
        count = min(per_group, heads - first)
        found.append((first, count, first * head_width, count * head_width))
    return found


def spread(tile, first, count, lanes):
    rows = tile.shape[0]
    head_width = lanes // count
    out = jnp.broadcast_to(tile[:, first : first + 1], (rows, lanes))
    lane = lax.broadcasted_iota(jnp.int32, (rows, lanes), 1)
    for k in range(1, count):
        column = jnp.broadcast_to(tile[:, first + k : first + k + 1], (rows, lanes))
        out = jnp.where(lane >= k * head_width, column, out)
    return out


def own_lanes(tile, k, count):
    if count == 1:
        return tile
    head_width = tile.shape[1] // count
    lane = lax.broadcasted_iota(jnp.int32, tile.shape, 1)
    inside = (lane >= k * head_width) & (lane < (k + 1) * head_width)
    return jnp.where(inside, tile, jnp.zeros_like(tile))


def triangle(keep):
    row = lax.broadcasted_iota(jnp.int32, (CHUNK, CHUNK), 0)
    column = lax.broadcasted_iota(jnp.int32, (CHUNK, CHUNK), 1)
    return keep(row, column)


def decay_of(payload, state):
    rows = payload[state : state + 16].astype(f32)
    return jnp.exp(rows[0:1] + rows[8:9] + rows[12:13])


def project_kernel(
    heads,
    block,
    sources,
    x_in,
    x_edge,
    gain,
    *refs,
):
    pack_sources, refs = refs[:sources], refs[sources:]
    (
        dt_bias, rate, taps_x, taps_bc, normed_out, rescale_out, raw_x, raw_bc,
        edge_x, edge_bc, step_raw, pre_x, pre_bc, act_x, act_bc, dt_out,
        run_out, payload, ext_x, ext_bc, end_out, total_out, pack, pack_sem,
    ) = refs
    step = pl.program_id(0)
    groups = head_groups(raw_x.shape[1], heads)
    shared = act_bc.shape[1]
    state = shared // 2

    def normed_of(block):
        x = block.astype(f32)
        rescale = lax.rsqrt(jnp.mean(x * x, axis=-1, keepdims=True) + epsilon)
        return rescale, (x * rescale * gain[...]).astype(bf16)

    @pl.when(step == 0)
    def _():
        weight_fetch(block, pack_sources, pack, pack_sem)
        _, edge = normed_of(x_edge[...])
        weight_wait(pack_sources, pack, pack_sem)
        edge_x[...] = dot_nn(edge, pack[:, shared + LANES :]).astype(bf16).astype(f32)[8:]
        edge_bc[...] = dot_nn(edge, pack[:, :shared]).astype(bf16).astype(f32)[8:]
        ext_x[0:8] = edge_x[...]
        ext_bc[0:8] = edge_bc[...]
        end_out[...] = jnp.zeros_like(end_out)
        total_out[...] = jnp.zeros_like(total_out)

    @pl.when(step > 0)
    def _():
        ext_x[0:8] = ext_x[ROWS : ROWS + 8]
        ext_bc[0:8] = ext_bc[ROWS : ROWS + 8]

    rescale, normed = normed_of(x_in[...])
    rescale_out[...] = rescale
    normed_out[...] = normed
    low = dot_nn(normed, pack[:, :shared]).astype(bf16)
    raw_bc[...] = low
    ext_bc[8:] = low.astype(f32)
    step_in = dot_nn(normed, pack[:, shared : shared + LANES])
    step_raw[...] = step_in
    sizes = jax.nn.softplus(step_in + dt_bias[...])
    dt_out[...] = sizes
    low = dot_nn(normed, pack[:, shared + LANES :]).astype(bf16)
    raw_x[...] = low
    ext_x[8:] = low.astype(f32)
    for ext, taps, pre, act in ((ext_bc, taps_bc, pre_bc, act_bc), (ext_x, taps_x, pre_x, act_x)):
        total = ext[5 : 5 + ROWS] * taps[0:1]
        for k in range(1, CONV):
            total = total + ext[5 + k : 5 + k + ROWS] * taps[k : k + 1]
        pre[...] = total.astype(bf16)
        act[...] = silu_parts(total)[1].astype(bf16)
    lower = triangle(lambda t, s: t >= s).astype(f32)
    for sub in range(ROWS // CHUNK):
        at = slice(sub * CHUNK, (sub + 1) * CHUNK)
        dt = sizes[at]
        run = dot_nn(lower, dt * rate[...], exact)
        run_out[at] = run
        last = run[CHUNK - 1 : CHUNK]
        weight = jnp.exp(last - run) * dt
        decay = jnp.exp(last)
        b_turned = act_bc[at, :state].astype(f32).T.astype(bf16)
        for first, count, lane, lanes in groups:
            cols = slice(lane, lane + lanes)
            scaled = act_x[at, cols].astype(f32) * spread(weight, first, count, lanes)
            end_out[:, cols] = spread(decay, first, count, lanes) * end_out[:, cols] + dot_nn(
                b_turned, scaled.astype(bf16)
            )
        total_out[...] += jnp.broadcast_to(last, total_out.shape)

    @pl.when(step == pl.num_programs(0) - 1)
    def _():
        for first, count, lane, lanes in groups:
            cols = slice(lane, lane + lanes)
            payload[:state, cols] = end_out[:, cols].astype(bf16)
            total = spread(total_out[...], first, count, lanes)
            high = total.astype(bf16).astype(f32)
            middle = (total - high).astype(bf16).astype(f32)
            low = total - high - middle
            row = lax.broadcasted_iota(jnp.int32, (8, lanes), 0)
            rest = jnp.where(row < 4, middle, low)
            payload[state:, cols] = jnp.concatenate([high, rest], axis=0).astype(bf16)


def full(shape):
    return pl.BlockSpec(shape, lambda i: (0,) * len(shape))


def rows_of(width, back=0):
    if back:
        return pl.BlockSpec((ROWS, width), lambda i: (back - 1 - i, 0))
    return pl.BlockSpec((ROWS, width), lambda i: (i, 0))


def pieces_of(pieces, count, model):
    if pieces == 1:
        return rows_of(model), (count, model)
    lanes = model // pieces
    return pl.BlockSpec((pieces, ROWS, lanes), lambda i: (0, i, 0)), (pieces, count, lanes)


def params():
    return pltpu.CompilerParams(
        dimension_semantics=("arbitrary",), vmem_limit_bytes=48 * 1024 * 1024
    )


def project_forward(
    heads, block, x, x_edge, gain, pack, dt_bias, rate, taps_x, taps_bc
):
    count, model = x.shape
    width, shared = taps_x.shape[1], taps_bc.shape[1]
    state = shared // 2
    return pl.pallas_call(
        partial(project_kernel, heads, block, len(pack)),
        grid=(count // ROWS,),
        in_specs=[
            rows_of(model),
            full((16, model)),
            full((1, model)),
            *[anywhere() for _ in pack],
            full((1, LANES)),
            full((1, LANES)),
            full((CONV, width)),
            full((CONV, shared)),
        ],
        out_specs=[
            rows_of(model),
            rows_of(1),
            rows_of(width),
            rows_of(shared),
            full((8, width)),
            full((8, shared)),
            rows_of(LANES),
            rows_of(width),
            rows_of(shared),
            rows_of(width),
            rows_of(shared),
            rows_of(LANES),
            rows_of(LANES),
            full((state + 16, width)),
        ],
        out_shape=[
            jax.ShapeDtypeStruct((count, model), bf16),
            jax.ShapeDtypeStruct((count, 1), f32),
            jax.ShapeDtypeStruct((count, width), bf16),
            jax.ShapeDtypeStruct((count, shared), bf16),
            jax.ShapeDtypeStruct((8, width), f32),
            jax.ShapeDtypeStruct((8, shared), f32),
            jax.ShapeDtypeStruct((count, LANES), f32),
            jax.ShapeDtypeStruct((count, width), bf16),
            jax.ShapeDtypeStruct((count, shared), bf16),
            jax.ShapeDtypeStruct((count, width), bf16),
            jax.ShapeDtypeStruct((count, shared), bf16),
            jax.ShapeDtypeStruct((count, LANES), f32),
            jax.ShapeDtypeStruct((count, LANES), f32),
            jax.ShapeDtypeStruct((state + 16, width), bf16),
        ],
        scratch_shapes=[
            pltpu.VMEM((8 + ROWS, width), f32),
            pltpu.VMEM((8 + ROWS, shared), f32),
            pltpu.VMEM((state, width), f32),
            pltpu.VMEM((8, LANES), f32),
            *weight_scratch(pack[0]),
        ],
        compiler_params=params(),
        cost_estimate=pl.CostEstimate(
            flops=2 * count * model * pack[0].shape[1],
            bytes_accessed=2 * pack[0].size + count * (4 * model + 6 * (width + shared)),
            transcendentals=count * (width + shared),
        ),
        name="project_forward",
    )(x, x_edge, gain, *pack, dt_bias, rate, taps_x, taps_bc)


def inner_kernel(
    heads, block, act_x, act_bc, dt_in, run_in, normed, *refs
):
    *z_sources, gate_out, inner_out, w_z, z_sem = refs

    @pl.when(pl.program_id(0) == 0)
    def _():
        weight_fetch(block, z_sources, w_z, z_sem)
        weight_wait(z_sources, w_z, z_sem)

    groups = head_groups(act_x.shape[1], heads)
    state = act_bc.shape[1] // 2
    gate_out[...] = dot_nn(normed[...], w_z[...])
    causal = triangle(lambda t, s: t >= s)
    for sub in range(ROWS // CHUNK):
        at = slice(sub * CHUNK, (sub + 1) * CHUNK)
        dt = dt_in[at]
        run = run_in[at]
        turned = run.T
        product = dot_nt(act_bc[at, state:], act_bc[at, :state])
        for first, count, lane, lanes in groups:
            cols = slice(lane, lane + lanes)
            stepped = act_x[at, cols].astype(f32) * spread(dt, first, count, lanes)
            low = stepped.astype(bf16)
            weights = []
            stacked = []
            for k in range(count):
                h = first + k
                gap = jnp.broadcast_to(run[:, h : h + 1], (CHUNK, CHUNK)) - turned[h : h + 1]
                factor = jnp.exp(jnp.where(causal, gap, -jnp.inf))
                weights.append((product * factor).astype(bf16))
                stacked.append(own_lanes(low, k, count))
            inner_out[at, cols] = dot_nn(
                jnp.concatenate(weights, axis=1), jnp.concatenate(stacked, axis=0)
            )


def inner_forward(heads, block, act_x, act_bc, dt, run, normed, w_z):
    count, width = act_x.shape
    model = normed.shape[1]
    shared = act_bc.shape[1]
    return pl.pallas_call(
        partial(inner_kernel, heads, block),
        grid=(count // ROWS,),
        in_specs=[
            rows_of(width),
            rows_of(shared),
            rows_of(LANES),
            rows_of(LANES),
            rows_of(model),
            *[anywhere() for _ in w_z],
        ],
        out_specs=[rows_of(width), rows_of(width)],
        out_shape=[
            jax.ShapeDtypeStruct((count, width), f32),
            jax.ShapeDtypeStruct((count, width), f32),
        ],
        scratch_shapes=weight_scratch(w_z[0]),
        compiler_params=params(),
        cost_estimate=pl.CostEstimate(
            flops=2 * count * width * (4 * CHUNK + model),
            bytes_accessed=count * (10 * width + 2 * model) + 2 * w_z[0].size,
            transcendentals=count * heads * CHUNK,
        ),
        name="inner_forward",
    )(act_x, act_bc, dt, run, normed, *w_z)


def outer_kernel(
    heads,
    block,
    sources,
    pieces,
    shards,
    act_x,
    act_bc,
    dt_in,
    run_in,
    gate_in,
    inner_in,
    *refs,
):
    out_sources, refs = refs[:sources], refs[sources:]
    skip, gain, *refs = refs
    arrived, refs = refs[: shards - 1], refs[shards - 1 :]
    grad_in, refs = (refs[0], refs[1:]) if len(refs) == 9 else (None, refs)
    mixed_out, scaled_out, part_out, sums_out, states_out, held, w_out, out_sem = refs
    groups = head_groups(act_x.shape[1], heads)
    state = act_bc.shape[1] // 2

    @pl.when(pl.program_id(0) == 0)
    def _():
        weight_fetch(block, out_sources, w_out, out_sem)
        place = lax.axis_index("seq")
        held[...] = jnp.zeros_like(held)
        for distance in reversed(range(1, shards)):

            @pl.when(place >= distance)
            def _():
                payload = arrived[distance - 1]
                held[...] = decay_of(payload, state) * held[...] + payload[:state].astype(f32)

        weight_wait(out_sources, w_out, out_sem)

    square_rows = []
    ones = jnp.ones((8, LANES), f32)
    for sub in range(ROWS // CHUNK):
        at = slice(sub * CHUNK, (sub + 1) * CHUNK)
        run = run_in[at]
        last = run[CHUNK - 1 : CHUNK]
        weight = jnp.exp(last - run) * dt_in[at]
        decay = jnp.exp(last)
        grown = jnp.exp(run)
        c_part = act_bc[at, state:]
        b_turned = act_bc[at, :state].astype(f32).T.astype(bf16)
        states_out[sub] = held[...].astype(bf16)
        squares = jnp.zeros((CHUNK, LANES), f32)
        for first, count, lane, lanes in groups:
            cols = slice(lane, lane + lanes)
            x_part = act_x[at, cols].astype(f32)
            before = held[:, cols]
            mixed = inner_in[at, cols] + spread(grown, first, count, lanes) * dot_nn(
                c_part, before.astype(bf16)
            )
            mixed = mixed + skip[:, cols] * x_part
            held[:, cols] = spread(decay, first, count, lanes) * before + dot_nn(
                b_turned, (x_part * spread(weight, first, count, lanes)).astype(bf16)
            )
            gated = mixed * silu_parts(gate_in[at, cols])[1]
            mixed_out[at, cols] = mixed.astype(bf16)
            scaled_out[at, cols] = (gated * gain[:, cols]).astype(bf16)
            square = gated * gated
            if lanes < LANES:
                fill = jnp.zeros((CHUNK, LANES - lanes), f32)
                square = jnp.concatenate([square, fill], axis=1)
            squares = squares + square
        square_rows.append(dot_nt(ones, squares, exact))
    part = dot_nt(scaled_out[...], w_out[...])
    if pieces == 1:
        part_out[...] = part.astype(bf16)
    else:
        wide = part.shape[1] // pieces
        for k in range(pieces):
            part_out[k] = part[:, k * wide : (k + 1) * wide].astype(bf16)
    row = lax.broadcasted_iota(jnp.int32, (8, CHUNK), 0)
    for sub in range(ROWS // CHUNK):
        at = slice(sub * CHUNK, (sub + 1) * CHUNK)
        pair_row = jnp.zeros((8, CHUNK), f32)
        if grad_in is not None:
            pairs = jnp.zeros((CHUNK, LANES), f32)
            for lane in range(0, part.shape[1], LANES):
                cols = slice(lane, lane + LANES)
                pairs = pairs + part[at, cols] * grad_in[at, cols].astype(f32)
            pair_row = dot_nt(ones, pairs, exact)
        sums_out[:, at] = jnp.where(row == 0, square_rows[sub], pair_row)


def outer_forward(
    heads, block, pieces, act_x, act_bc, dt, run, gate_in, inner, w_out, skip, gain, arrived, grad_in
):
    count, width = act_x.shape
    model = w_out[0].shape[0]
    part_spec, part_shape = pieces_of(pieces, count, model)
    shared = act_bc.shape[1]
    state = shared // 2
    subs = ROWS // CHUNK
    extra, extra_specs = [], []
    if grad_in is not None:
        extra, extra_specs = [grad_in], [rows_of(model)]
    return pl.pallas_call(
        partial(outer_kernel, heads, block, len(w_out), pieces, len(arrived) + 1),
        grid=(count // ROWS,),
        in_specs=[
            rows_of(width),
            rows_of(shared),
            rows_of(LANES),
            rows_of(LANES),
            rows_of(width),
            rows_of(width),
            *[anywhere() for _ in w_out],
            full((1, width)),
            full((1, width)),
            *[full(payload.shape) for payload in arrived],
            *extra_specs,
        ],
        out_specs=[
            rows_of(width),
            rows_of(width),
            part_spec,
            pl.BlockSpec((8, ROWS), lambda i: (0, i)),
            pl.BlockSpec((subs, state, width), lambda i: (i, 0, 0)),
        ],
        out_shape=[
            jax.ShapeDtypeStruct((count, width), bf16),
            jax.ShapeDtypeStruct((count, width), bf16),
            jax.ShapeDtypeStruct(part_shape, bf16),
            jax.ShapeDtypeStruct((8, count), f32),
            jax.ShapeDtypeStruct((count // CHUNK, state, width), bf16),
        ],
        scratch_shapes=[pltpu.VMEM((state, width), f32), *weight_scratch(w_out[0])],
        compiler_params=params(),
        cost_estimate=pl.CostEstimate(
            flops=2 * count * width * (2 * state + model),
            bytes_accessed=count * width * 18,
            transcendentals=count * width,
        ),
        name="outer_forward",
    )(
        act_x, act_bc, dt, run, gate_in, inner, *w_out, skip, gain, *arrived, *extra
    )


def gate_kernel(
    heads,
    block,
    sources,
    addends,
    between,
    grad,
    gate_in,
    mixed_in,
    scaled_in,
    act_x,
    act_bc,
    run_in,
    gain,
    *refs,
):
    out_sources, refs = refs[:sources], refs[sources:]
    sums, refs = refs[:addends], refs[addends:]
    later, earlier = refs[:2] if between else (None, None)
    refs = refs[2:] if between else refs
    grad_mixed, grad_gate, scaled_out, gain_sum, skip_sum, adjoint_out, *refs = refs
    grad_in, adjoint, scales, w_out, out_sem = refs
    step = pl.program_id(0)
    groups = head_groups(act_x.shape[1], heads)
    state = act_bc.shape[1] // 2

    @pl.when(step == 0)
    def _():
        weight_fetch(block, out_sources, w_out, out_sem)
        gain_sum[...] = jnp.zeros_like(gain_sum)
        skip_sum[...] = jnp.zeros_like(skip_sum)
        adjoint[...] = jnp.zeros_like(adjoint)
        scales[...] = jnp.zeros_like(scales)
        weight_wait(out_sources, w_out, out_sem)

    grad_in[...] = dot_nn(grad[...], w_out[...])
    total = sums[0][...]
    for more in sums[1:]:
        total = total + more[...]
    scale_row = lax.rsqrt(total[0:1] / INNER + epsilon)
    pull_row = total[1:2] * scale_row * scale_row * scale_row / INNER
    for sub in reversed(range(ROWS // CHUNK)):
        at = slice(sub * CHUNK, (sub + 1) * CHUNK)
        run = run_in[at]
        grown = jnp.exp(run)
        decay = grown[CHUNK - 1 : CHUNK]
        c_turned = act_bc[at, state:].astype(f32).T.astype(bf16)
        scales[0:1] = scale_row[:, at]
        scales[1:2] = pull_row[:, at]
        columns = scales[...].T
        row_scale = columns[:, 0:1]
        row_pull = columns[:, 1:2]
        if later is not None:
            moved = later[at].astype(f32) - earlier[at].astype(f32)
            pulled = jnp.sum(grad[at].astype(f32) * moved, axis=1, keepdims=True)
            row_pull = pulled * row_scale * row_scale * (1.0 / INNER)
        for first, count, lane, lanes in groups:
            cols = slice(lane, lane + lanes)
            gate = gate_in[at, cols]
            mixed = mixed_in[at, cols].astype(f32)
            share, active = silu_parts(gate)
            gated = mixed * active
            d_scaled = grad_in[at, cols] * row_scale
            d_gated = d_scaled * gain[:, cols] - row_pull * gated
            d_mixed = d_gated * active
            grad_mixed[at, cols] = d_mixed.astype(bf16)
            grad_gate[at, cols] = (d_gated * mixed * silu_slope(gate, share)).astype(bf16)
            scaled_out[at, cols] = (scaled_in[at, cols].astype(f32) * row_scale).astype(bf16)
            gain_sum[0:1, cols] += jnp.sum(d_scaled * gated, axis=0, keepdims=True)
            skip_sum[0:1, cols] += jnp.sum(
                d_mixed * act_x[at, cols].astype(f32), axis=0, keepdims=True
            )
            adjoint[:, cols] = spread(decay, first, count, lanes) * adjoint[:, cols] + dot_nn(
                c_turned, (d_mixed * spread(grown, first, count, lanes)).astype(bf16)
            )

    @pl.when(step == pl.num_programs(0) - 1)
    def _():
        adjoint_out[...] = adjoint[...].astype(bf16)


def gate_backward(
    heads, block, grad, w_out, gate_in, mixed, scaled, act_x, act_bc, run, gain, sums, ends
):
    count, width = act_x.shape
    model = grad.shape[1]
    shared = act_bc.shape[1]
    state = shared // 2
    steps = count // ROWS
    return pl.pallas_call(
        partial(gate_kernel, heads, block, len(w_out), len(sums), len(ends) > 0),
        grid=(steps,),
        in_specs=[
            rows_of(model, steps),
            rows_of(width, steps),
            rows_of(width, steps),
            rows_of(width, steps),
            rows_of(width, steps),
            rows_of(shared, steps),
            rows_of(LANES, steps),
            full((1, width)),
            *[anywhere() for _ in w_out],
            *[pl.BlockSpec((8, ROWS), lambda i: (0, steps - 1 - i)) for _ in sums],
            *[rows_of(model, steps) for _ in ends],
        ],
        out_specs=[
            rows_of(width, steps),
            rows_of(width, steps),
            rows_of(width, steps),
            full((8, width)),
            full((8, width)),
            full((state, width)),
        ],
        out_shape=[
            jax.ShapeDtypeStruct((count, width), bf16),
            jax.ShapeDtypeStruct((count, width), bf16),
            jax.ShapeDtypeStruct((count, width), bf16),
            jax.ShapeDtypeStruct((8, width), f32),
            jax.ShapeDtypeStruct((8, width), f32),
            jax.ShapeDtypeStruct((state, width), bf16),
        ],
        scratch_shapes=[
            pltpu.VMEM((ROWS, width), f32),
            pltpu.VMEM((state, width), f32),
            pltpu.VMEM((CHUNK, CHUNK), f32),
            *weight_scratch(w_out[0]),
        ],
        compiler_params=params(),
        cost_estimate=pl.CostEstimate(
            flops=2 * count * width * (state + model),
            bytes_accessed=count * width * 16,
            transcendentals=count * width,
        ),
        name="gate_backward",
    )(
        grad, gate_in, mixed, scaled, act_x, act_bc, run, gain, *w_out, *sums, *ends
    )


def states_kernel(
    heads,
    shards,
    grad_mixed,
    act_x,
    act_bc,
    pre_x,
    pre_bc,
    raw_x,
    raw_bc,
    edge_x,
    edge_bc,
    dt_in,
    run_in,
    step_raw,
    dt_bias,
    rate_rows,
    states_in,
    skip,
    taps_x,
    taps_bc,
    members,
    *refs,
):
    arrived, payloads, refs = refs[: shards - 1], refs[shards - 1 : 2 * shards - 2], refs[2 * shards - 2 :]
    packed, tail, back, tap_sum_x, tap_sum_bc, rate_sum, bias_sum, *refs = refs
    adjoint, d_pre_x, d_pre_bc, rows_ref, carry_ref, square_ref = refs
    step = pl.program_id(0)
    steps = pl.num_programs(0)
    groups = head_groups(act_x.shape[1], heads)
    shared = act_bc.shape[1]
    state = shared // 2
    padded = members.shape[0]

    @pl.when(step == 0)
    def _():
        place = lax.axis_index("seq")
        adjoint[...] = jnp.zeros_like(adjoint)
        for distance in reversed(range(1, shards)):

            @pl.when(place + distance < shards)
            def _():
                decay = decay_of(payloads[shards - 1 - distance], state)
                adjoint[...] = decay * adjoint[...] + arrived[distance - 1][...].astype(f32)

        d_pre_x[8:16] = jnp.zeros((8, d_pre_x.shape[1]), f32)
        d_pre_bc[8:16] = jnp.zeros((8, d_pre_bc.shape[1]), f32)
        tap_sum_x[...] = jnp.zeros_like(tap_sum_x)
        tap_sum_bc[...] = jnp.zeros_like(tap_sum_bc)
        rate_sum[...] = jnp.zeros_like(rate_sum)
        bias_sum[...] = jnp.zeros_like(bias_sum)
        rows_ref[...] = jnp.zeros_like(rows_ref)
        square_ref[...] = jnp.zeros_like(square_ref)

    upto = triangle(lambda s, t: s <= t)
    not_before = triangle(lambda s, t: s >= t).astype(f32)
    before = triangle(lambda s, t: s < t).astype(f32)
    head_lane = lax.broadcasted_iota(jnp.int32, (CHUNK, LANES), 1)
    for sub in reversed(range(ROWS // CHUNK)):
        at = slice(sub * CHUNK, (sub + 1) * CHUNK)
        dt = dt_in[at]
        run = run_in[at]
        last = run[CHUNK - 1 : CHUNK]
        grown = jnp.exp(run)
        decay = grown[CHUNK - 1 : CHUNK]
        to_end = jnp.exp(last - run)
        run_turned = run.T
        dt_turned = dt.T[0:padded]
        inside_tile = jnp.zeros((CHUNK, LANES), f32)
        b_part = act_bc[at, :state]
        c_part = act_bc[at, state:]
        c_turned = c_part.astype(f32).T.astype(bf16)
        product = dot_nt(b_part, c_part)
        d_product = jnp.zeros((CHUNK, CHUNK), f32)
        d_b = jnp.zeros((CHUNK, state), f32)
        d_c = jnp.zeros((CHUNK, state), f32)
        d_pre_x[CHUNK + 8 : CHUNK + 16] = d_pre_x[8:16]
        d_pre_bc[CHUNK + 8 : CHUNK + 16] = d_pre_bc[8:16]
        through = []
        for first, count, lane, lanes in groups:
            cols = slice(lane, lane + lanes)
            x_low = act_x[at, cols]
            x_part = x_low.astype(f32)
            dy_low = grad_mixed[at, cols]
            dy = dy_low.astype(f32)
            dt_wide = spread(dt, first, count, lanes)
            ending = spread(to_end, first, count, lanes)
            growing = spread(grown, first, count, lanes)
            lam = adjoint[:, cols]
            lam_low = lam.astype(bf16)
            held_low = states_in[sub][:, cols]
            weights = []
            stacked = []
            for k in range(count):
                h = first + k
                gap = run_turned[h : h + 1] - jnp.broadcast_to(run[:, h : h + 1], (CHUNK, CHUNK))
                factor = jnp.exp(jnp.where(upto, gap, -jnp.inf))
                weights.append((product * factor).astype(bf16))
                stacked.append(own_lanes(dy_low, k, count))
                paired = dot_nt(own_lanes(x_low, k, count), dy_low) * factor
                dt_column = jnp.broadcast_to(dt[:, h : h + 1], (CHUNK, CHUNK))
                d_product = d_product + paired * dt_column
                inside = paired * product
                rows_ref[h : h + 1] = jnp.sum(inside * dt_column, axis=0, keepdims=True)
                inside_tile = jnp.where(
                    head_lane == h, jnp.sum(inside, axis=1, keepdims=True), inside_tile
                )
            d_stepped = dot_nn(jnp.concatenate(weights, axis=1), jnp.concatenate(stacked, axis=0))
            from_end = ending * dot_nn(b_part, lam_low)
            d_x = dt_wide * (d_stepped + from_end) + skip[:, cols] * dy
            dy_grown = dy * growing
            dy_grown_low = dy_grown.astype(bf16)
            carry_ref[0, :, cols] = (x_part * from_end).astype(bf16)
            carry_ref[1, :, cols] = (dy_grown * dot_nn(c_part, held_low)).astype(bf16)
            d_b = d_b + dot_nt((x_part * dt_wide * ending).astype(bf16), lam_low)
            d_c = d_c + dot_nt(dy_grown_low, held_low)
            wide_decay = spread(decay, first, count, lanes)
            lam_decayed = wide_decay * lam
            through.append(
                jnp.sum(lam_decayed * held_low.astype(f32), axis=0, keepdims=True)
            )
            adjoint[:, cols] = lam_decayed + dot_nn(c_turned, dy_grown_low)
            pre = pre_x[at, cols].astype(f32)
            d_pre_x[8 : CHUNK + 8, cols] = d_x * silu_slope(pre, jax.nn.sigmoid(pre))
        member = members[...]
        kept = dot_nt(member, carry_ref[0])
        fed = dot_nt(member, carry_ref[1])
        wide_row = jnp.concatenate(through, axis=1)
        across = dot_nt(member.astype(f32), jnp.broadcast_to(wide_row, (8, wide_row.shape[1])), exact)
        inside_rows = inside_tile.T[0:padded]
        d_log = (
            dot_nn(rows_ref[...] - dt_turned * inside_rows + fed, not_before, exact)
            + dot_nn(dt_turned * kept, before, exact)
            + across[:, 0:1]
        )
        d_log_rate = d_log * rate_rows[...]
        rate_sum[...] += d_log_rate * dt_turned
        square_ref[0:padded] = d_log_rate + inside_rows + kept
        d_step_exact = square_ref[...].T * jax.nn.sigmoid(step_raw[at] + dt_bias[...])
        bias_sum[0:1] += jnp.sum(d_step_exact, axis=0, keepdims=True)
        packed[at, shared : shared + LANES] = d_step_exact.astype(bf16)
        if sub == ROWS // CHUNK - 1:

            @pl.when(step == 0)
            def _():
                tail[:, shared : shared + LANES] = d_step_exact[CHUNK - 16 :]

        d_product_low = d_product.astype(bf16)
        d_b = d_b + dot_nn(d_product_low, c_part)
        d_c = d_c + dot_nn(d_product.T.astype(bf16), b_part)
        pre = pre_bc[at].astype(f32)
        slope = silu_slope(pre, jax.nn.sigmoid(pre))
        d_pre_bc[8 : CHUNK + 8, :state] = d_b * slope[:, :state]
        d_pre_bc[8 : CHUNK + 8, state:] = d_c * slope[:, state:]
        for d_pre, raw, taps, place, tap_sum in (
            (d_pre_x, raw_x, taps_x, slice(shared + LANES, None), tap_sum_x),
            (d_pre_bc, raw_bc, taps_bc, slice(0, shared), tap_sum_bc),
        ):
            values = raw[at].astype(f32)
            total = jnp.zeros_like(values)
            for k in range(CONV):
                moved = d_pre[11 - k : 11 - k + CHUNK]
                total = total + moved * taps[k : k + 1]
                tap_sum[k : k + 1] += jnp.sum(values * moved, axis=0, keepdims=True)
            packed[at, place] = total.astype(bf16)
            if sub == ROWS // CHUNK - 1:

                @pl.when(step == 0)
                def _():
                    tail[:, place] = total[CHUNK - 16 :]

    @pl.when(step == steps - 1)
    def _():
        back[...] = jnp.zeros_like(back)
        for d_pre, edge, taps, tap_sum, place in (
            (d_pre_x, edge_x, taps_x, tap_sum_x, slice(shared + LANES, None)),
            (d_pre_bc, edge_bc, taps_bc, tap_sum_bc, slice(0, shared)),
        ):
            d_pre[0:8] = jnp.zeros((8, d_pre.shape[1]), f32)
            values = edge[...]
            total = jnp.zeros_like(values)
            for k in range(CONV):
                moved = d_pre[3 - k : 11 - k]
                total = total + moved * taps[k : k + 1]
                tap_sum[k : k + 1] += jnp.sum(values * moved, axis=0, keepdims=True)
            back[8:, place] = total


def states_backward(
    heads,
    grad_mixed,
    act_x,
    act_bc,
    pre_x,
    pre_bc,
    raw_x,
    raw_bc,
    edge_x,
    edge_bc,
    dt,
    run,
    step_raw,
    dt_bias,
    rate,
    states,
    skip,
    taps_x,
    taps_bc,
    arrived,
    payloads,
):
    count, width = act_x.shape
    shared = act_bc.shape[1]
    state = shared // 2
    steps = count // ROWS
    subs = ROWS // CHUNK
    padded = -(-heads // 16) * 16
    head_of = jnp.arange(width)[None, :] // (width // heads)
    members = (jnp.arange(padded)[:, None] == head_of).astype(bf16)
    rate_rows = jnp.broadcast_to(rate[0, :padded, None], (padded, CHUNK))
    return pl.pallas_call(
        partial(states_kernel, heads, len(arrived) + 1),
        grid=(steps,),
        in_specs=[
            rows_of(width, steps),
            rows_of(width, steps),
            rows_of(shared, steps),
            rows_of(width, steps),
            rows_of(shared, steps),
            rows_of(width, steps),
            rows_of(shared, steps),
            full((8, width)),
            full((8, shared)),
            rows_of(LANES, steps),
            rows_of(LANES, steps),
            rows_of(LANES, steps),
            full((1, LANES)),
            full((padded, CHUNK)),
            pl.BlockSpec((subs, state, width), lambda i: (steps - 1 - i, 0, 0)),
            full((1, width)),
            full((CONV, width)),
            full((CONV, shared)),
            full((padded, width)),
            *[full(array.shape) for array in (*arrived, *payloads)],
        ],
        out_specs=[
            rows_of(shared + LANES + width, steps),
            full((16, shared + LANES + width)),
            full((16, shared + LANES + width)),
            full((8, width)),
            full((8, shared)),
            full((padded, CHUNK)),
            full((8, LANES)),
        ],
        out_shape=[
            jax.ShapeDtypeStruct((count, shared + LANES + width), bf16),
            jax.ShapeDtypeStruct((16, shared + LANES + width), f32),
            jax.ShapeDtypeStruct((16, shared + LANES + width), f32),
            jax.ShapeDtypeStruct((8, width), f32),
            jax.ShapeDtypeStruct((8, shared), f32),
            jax.ShapeDtypeStruct((padded, CHUNK), f32),
            jax.ShapeDtypeStruct((8, LANES), f32),
        ],
        scratch_shapes=[
            pltpu.VMEM((state, width), f32),
            pltpu.VMEM((CHUNK + 16, width), f32),
            pltpu.VMEM((CHUNK + 16, shared), f32),
            pltpu.VMEM((padded, CHUNK), f32),
            pltpu.VMEM((2, CHUNK, width), bf16),
            pltpu.VMEM((CHUNK, CHUNK), f32),
        ],
        compiler_params=params(),
        cost_estimate=pl.CostEstimate(
            flops=20 * count * width * state,
            bytes_accessed=count * width * 16,
            transcendentals=count * heads * CHUNK * 2,
        ),
        name="states_backward",
    )(
        grad_mixed,
        act_x,
        act_bc,
        pre_x,
        pre_bc,
        raw_x,
        raw_bc,
        edge_x,
        edge_bc,
        dt,
        run,
        step_raw,
        dt_bias,
        rate_rows,
        states,
        skip,
        taps_x,
        taps_bc,
        members,
        *arrived,
        *payloads,
    )


def part_kernel(
    pieces,
    block,
    sources,
    grad_gate,
    packed,
    x_in,
    gain,
    *refs,
):
    z_sources, refs = refs[:sources], refs[sources:]
    *pack_sources, part_out, row_sum, norm_sum, part_ref, w_z, z_sem, pack, pack_sem = refs

    @pl.when(pl.program_id(0) == 0)
    def _():
        weight_fetch(block, z_sources, w_z, z_sem)
        weight_fetch(block, pack_sources, pack, pack_sem)
        weight_wait(z_sources, w_z, z_sem)
        weight_wait(pack_sources, pack, pack_sem)
        norm_sum[...] = jnp.zeros_like(norm_sum)

    x = x_in[...].astype(f32)
    rescale = lax.rsqrt(jnp.mean(x * x, axis=-1, keepdims=True) + epsilon)
    part_ref[...] = dot_nt(grad_gate[...], w_z[...]) + dot_nt(packed[...], pack[...])
    total = jnp.zeros((ROWS, LANES), f32)
    for lane in range(0, x.shape[1], LANES):
        cols = slice(lane, lane + LANES)
        pulled = part_ref[:, cols] * (x_in[:, cols].astype(f32) * rescale)
        norm_sum[0:1, cols] += jnp.sum(pulled, axis=0, keepdims=True)
        total = total + pulled * gain[:, cols]
    row_sum[...] = dot_nt(jnp.ones((8, LANES), f32), total, exact)
    if pieces == 1:
        part_out[...] = part_ref[...].astype(bf16)
    else:
        lanes = x.shape[1] // pieces
        for k in range(pieces):
            part_out[k] = part_ref[:, k * lanes : (k + 1) * lanes].astype(bf16)


def part_backward(
    pieces, block, grad_gate, packed, w_z, pack, x, gain
):
    count, width = grad_gate.shape
    model = x.shape[1]
    part_spec, part_shape = pieces_of(pieces, count, model)
    return pl.pallas_call(
        partial(part_kernel, pieces, block, len(w_z)),
        grid=(count // ROWS,),
        in_specs=[
            rows_of(width),
            rows_of(packed.shape[1]),
            rows_of(model),
            full((1, model)),
            *[anywhere() for _ in (*w_z, *pack)],
        ],
        out_specs=[part_spec, pl.BlockSpec((8, ROWS), lambda i: (0, i)), full((8, model))],
        out_shape=[
            jax.ShapeDtypeStruct(part_shape, bf16),
            jax.ShapeDtypeStruct((8, count), f32),
            jax.ShapeDtypeStruct((8, model), f32),
        ],
        scratch_shapes=[
            pltpu.VMEM((ROWS, model), f32),
            *weight_scratch(w_z[0]),
            *weight_scratch(pack[0]),
        ],
        compiler_params=params(),
        cost_estimate=pl.CostEstimate(
            flops=2 * count * model * (width + packed.shape[1]),
            bytes_accessed=2 * (w_z[0].size + pack[0].size) + 8 * count * model,
            transcendentals=0,
        ),
        name="part_backward",
    )(grad_gate, packed, x, gain, *w_z, *pack)


def weights_kernel(count, low, *refs):
    lefts, rights, out = refs[:count], refs[count : 2 * count], refs[2 * count]
    lane = 0
    for left, right in zip(lefts, rights):
        lanes = right.shape[1]
        out[0, :, lane : lane + lanes] = dot_tn(left[...], right[...]).astype(bf16)
        lane += lanes


def weights_backward(lefts, rights, kept):
    count, model = lefts[0].shape
    rows = model // 4
    lanes = sum(right.shape[1] for right in rights)
    low = lax.rem(lax.axis_index("seq"), 2)
    low = (low if kept else 1 - low).astype(jnp.int32).reshape(1)
    return pl.pallas_call(
        partial(weights_kernel, len(lefts)),
        grid_spec=pltpu.PrefetchScalarGridSpec(
            num_scalar_prefetch=1,
            grid=(2,),
            in_specs=[
                *[pl.BlockSpec((count, rows), lambda i, low: (0, 2 * i + low[0])) for _ in lefts],
                *[pl.BlockSpec(right.shape, lambda i, low: (0, 0)) for right in rights],
            ],
            out_specs=pl.BlockSpec((1, rows, lanes), lambda i, low: (i, 0, 0)),
        ),
        out_shape=jax.ShapeDtypeStruct((2, rows, lanes), bf16),
        compiler_params=params(),
        cost_estimate=pl.CostEstimate(
            flops=count * model * lanes,
            bytes_accessed=2 * (len(lefts) * count * model + count * lanes + model * lanes),
            transcendentals=0,
        ),
        name="weights_backward",
    )(low, *lefts, *rights)


def traded(block, axis, bit):
    return lax.ppermute(block, axis, [(i, i ^ bit) for i in range(lax.axis_size(axis))])


def rotated(block, axis, distance):
    size = lax.axis_size(axis)
    return lax.ppermute(block, axis, [(i, (i + distance) % size) for i in range(size)])


def others(block, axis, sign):
    return [rotated(block, axis, sign * d) for d in range(1, lax.axis_size(axis))]


def bits_of(axis):
    bit = 1
    while bit < lax.axis_size(axis):
        yield bit
        bit *= 2


def butterfly(block, axis):
    for bit in bits_of(axis):
        block = block + traded(block, axis, bit)
    return block


def halved(pieces, axis, bit):
    pairs = pieces.reshape((pieces.shape[0] // 2, 2) + pieces.shape[1:])
    mine = lax.rem(lax.axis_index(axis) // bit, 2)
    kept = lax.dynamic_index_in_dim(pairs, mine, 1, False)
    sent = lax.dynamic_index_in_dim(pairs, 1 - mine, 1, False)
    return kept + traded(sent, axis, bit)


def core_sum(kept, arrived, earlier):
    high = lax.axis_index("seq") // 2

    def summed(at):
        own = lax.dynamic_index_in_dim(kept, at, 0, False)
        return after(own + lax.dynamic_index_in_dim(arrived, at, 0, False), earlier)

    return summed(1 - high), summed(high)


def after(value, earlier):
    return value + (0.0 * earlier.reshape(-1)[0].astype(f32)).astype(value.dtype)


def moved_along(block, axis, distance):
    size, place = lax.axis_size(axis), lax.axis_index(axis)
    arrived = rotated(block, axis, distance)
    outside = (place < distance) | (place >= size + distance)
    return jnp.where(outside, jnp.zeros_like(arrived), arrived)


def tied(*values):
    return lax.optimization_barrier(values)


def block_forward(
    block, x, x_edge, weights, grad, pieces, mixed_inside=lambda inner, payloads: (inner, payloads)
):
    heads = weights["heads"]
    (
        normed, rescale, raw_x, raw_bc, edge_x, edge_bc, step_raw, pre_x, pre_bc, act_x, act_bc,
        dt, run, payload,
    ) = project_forward(
        heads, block, x, x_edge, weights["norm"], weights["pack"], weights["dt_bias"],
        weights["rate"], weights["taps_x"], weights["taps_bc"],
    )
    payloads = others(payload, "seq", 1)
    gate_in, inner = inner_forward(
        heads, block, act_x, act_bc, dt, run, normed, weights["w_z"]
    )
    inner, payloads = mixed_inside(inner, payloads)
    mixed, scaled, part, sums, states = outer_forward(
        heads, block, pieces, act_x, act_bc, dt, run, gate_in, inner, weights["w_out"],
        weights["skip"], weights["gain"], payloads, grad,
    )
    kept = dict(
        raw_x=raw_x, raw_bc=raw_bc, step_raw=step_raw, edge_x=edge_x, edge_bc=edge_bc,
        gate_in=gate_in, pre_x=pre_x, pre_bc=pre_bc, act_x=act_x, act_bc=act_bc, dt=dt, run=run,
        payloads=payloads, mixed=mixed, scaled=scaled, states=states, normed=normed,
        rescale=rescale,
    )
    return part, sums, kept


def gate_step(block, grad, sums, ends, kept, weights):
    return gate_backward(
        weights["heads"], block, grad, weights["w_out"], kept["gate_in"], kept["mixed"],
        kept["scaled"], kept["act_x"], kept["act_bc"], kept["run"], weights["gain"], sums, ends,
    )


def states_step(grad_mixed, arrived, kept, weights):
    return states_backward(
        weights["heads"], grad_mixed, kept["act_x"], kept["act_bc"], kept["pre_x"],
        kept["pre_bc"], kept["raw_x"], kept["raw_bc"], kept["edge_x"], kept["edge_bc"],
        kept["dt"], kept["run"], kept["step_raw"], weights["dt_bias"], weights["rate"],
        kept["states"], weights["skip"], weights["taps_x"], weights["taps_bc"], arrived,
        kept["payloads"],
    )


def fixed_tail(packed, tail, back):
    rows = tail + moved_along(back, "seq", -1)
    return packed.at[packed.shape[0] - 16 :].set(rows.astype(bf16))


def vectors_of(heads, taps_x, gain_sum, skip_sum, bias_sum, rate_sum, norm_sum, taps_bc):
    return (
        jnp.concatenate(
            [
                taps_x[:CONV].reshape(-1), gain_sum[0], skip_sum[0], bias_sum[0, :heads],
                jnp.sum(rate_sum[:heads], axis=1),
            ]
        ),
        jnp.concatenate([norm_sum[0], taps_bc[:CONV].reshape(-1)]),
    )


def norm_backward(d_normed, row_sum, x, rescale, grad, gain, model):
    unit = x.astype(f32) * rescale
    h = d_normed.astype(f32) * gain
    out = grad.astype(f32) + rescale * (h - unit * (row_sum / model)[:, None])
    return out.astype(bf16)


def shards(
    tokens, cotangent, norm_gain, w_z, w_x, w_bc, w_dt, conv_x, conv_bc, dt_bias, a_log, skip_d,
    gate_gain, w_out,
):
    section = lax.axis_index("section")
    seq_at = lax.axis_index("seq")
    seq_size = lax.axis_size("seq")
    count, model = tokens.shape[1:]
    head_size = lax.axis_size("head")
    head_at = lax.axis_index("head")
    heads = a_log.shape[1]
    width = w_x.shape[2]
    shared = w_bc.shape[2]
    share = model // head_size
    row_share = count // head_size
    quarter = model // seq_size

    def mine_first(of_first, of_second):
        return (
            jnp.where(section == 0, of_first, of_second),
            jnp.where(section == 0, of_second, of_first),
        )

    def quarter_of(weight):
        return lax.dynamic_slice_in_dim(weight, seq_at * quarter, quarter, 0)

    def half_of(weight):
        pairs = weight.reshape(2, 2, quarter, weight.shape[1])
        return lax.dynamic_index_in_dim(pairs, lax.rem(seq_at, 2), 1, False)

    def own_rows(array):
        return lax.dynamic_slice_in_dim(array, head_at * row_share, row_share, 0)

    def own_columns(array):
        return lax.dynamic_slice_in_dim(array, head_at * share, share, 1)

    def edge_of(x):
        return jnp.pad(moved_along(x[count - (CONV - 1) :], "seq", 1), ((16 - (CONV - 1), 0), (0, 0)))

    def section_sum(of_first, of_second, earlier=None):
        mine, other = mine_first(of_first, of_second)
        arrived = traded(other, "section", 1)
        if earlier is not None:
            arrived = after(arrived, earlier)
        return mine.astype(f32) + arrived.astype(f32)

    def both_sequences(of_first, of_second, earlier=None):
        mine, other = mine_first(of_first, of_second)
        arrived = traded(other, "section", 1)
        if earlier is not None:
            arrived = after(arrived, earlier)
        return jnp.stack(mine_first(mine, arrived))

    padded_dt = jnp.pad(w_dt[0], ((0, 0), (0, LANES - heads)))
    got_pack = traded(
        jnp.concatenate([quarter_of(w) for w in (w_bc[0], padded_dt, w_x[0])], axis=1),
        "section", 1,
    )
    pack = jnp.concatenate([w_bc[0], padded_dt, w_x[0]], axis=1)
    vector = jnp.concatenate(
        [
            norm_gain[0], conv_x[0].T.reshape(-1), conv_bc[0].T.reshape(-1), dt_bias[0], a_log[0],
            skip_d[0], gate_gain[0],
        ]
    )
    got_pack, part_z, vector = tied(got_pack, half_of(w_z[0]), vector)
    vectors = mine_first(vector, traded(vector, "section", 1))
    first = lax.dynamic_index_in_dim(tokens, section, 0, False)
    first_edge = edge_of(first)
    got_z = traded(part_z, "section", 1)
    far_pack = traded(got_pack, "seq", 2)
    far_pack, got_z, part_out, pack, first, first_edge, *vectors = tied(
        far_pack, got_z, half_of(w_out[0]), pack, first, first_edge, *vectors
    )
    got_out = traded(part_out, "section", 1)
    sources_pack = (got_pack, far_pack, traded(got_pack, "seq", 1), traded(far_pack, "seq", 1))
    sources = dict(
        pack=(pack, *sources_pack), w_z=(w_z[0], got_z, traded(got_z, "seq", 1)), w_out=[w_out[0]]
    )
    weights = []
    for b in range(2):
        at = 0

        def take(size):
            nonlocal at
            at += size
            return vectors[b][at - size : at]

        block = dict(heads=heads, **sources)
        block["norm"] = take(model)[None]
        block["taps_x"] = take(CONV * width).reshape(CONV, width)
        block["taps_bc"] = take(CONV * shared).reshape(CONV, shared)
        block["dt_bias"] = jnp.pad(take(heads), (0, LANES - heads))[None]
        block["rate"] = jnp.pad(-jnp.exp(take(heads)), (0, LANES - heads))[None]
        block["skip"] = jnp.repeat(take(heads), width // heads)[None]
        block["gain"] = take(width)[None]
        weights.append(block)

    last_grad = lax.dynamic_index_in_dim(cotangent, section, 0, False)

    def fetch_out(inner, payloads):
        inner, part, *payloads = tied(inner, got_out, *payloads)
        sources["w_out"] += [part, traded(part, "seq", 1)]
        return inner, payloads

    part, sums, kept_first = block_forward(
        0, first, first_edge, weights[0], None, 1, fetch_out
    )
    summed = lax.psum_scatter(part, "head", scatter_dimension=0, tiled=True).astype(f32)
    sums_first = [sums, *others(sums, "head", 1)]
    scale_first = lax.rsqrt(sum(part[0] for part in sums_first) / INNER + epsilon)
    second_share = own_rows(first).astype(f32) + own_rows(scale_first)[:, None] * summed
    second = lax.all_gather(second_share.astype(bf16), "head", axis=0, tiled=True)

    outward, sums, kept_second = block_forward(
        1, second, edge_of(second), weights[1], last_grad, head_size
    )
    sums_second = [sums, *others(sums, "head", 1)]
    bits = list(bits_of("head"))

    grad_mixed, grad_gate, scaled, gain_sum, skip_sum, adjoint = gate_step(
        1, last_grad, sums_second, (), kept_second, weights[1]
    )
    normed = kept_second["normed"]
    early_sent = weights_backward([last_grad, normed], [scaled, grad_gate], False)
    grad_mixed, early_sent, outward, *arrived = tied(
        grad_mixed, early_sent, outward, *others(adjoint, "seq", -1)
    )
    packed, tail, back, taps_x, taps_bc, rate_sum, bias_sum = states_step(
        grad_mixed, arrived, kept_second, weights[1]
    )
    outward = after(halved(outward, "head", bits[0]), tail)
    packed, outward = tied(fixed_tail(packed, tail, back), outward)
    part, row_sum, norm_sum = part_backward(
        1, 1, grad_gate, packed, weights[1]["w_z"], weights[1]["pack"], second,
        weights[1]["norm"],
    )
    norm_sum, taps_x, gain_sum, skip_sum, bias_sum, rate_sum, taps_bc = tied(
        norm_sum, taps_x, gain_sum, skip_sum, bias_sum, rate_sum, taps_bc
    )
    local_second, whole_second = vectors_of(
        heads, taps_x, gain_sum, skip_sum, bias_sum, rate_sum, norm_sum, taps_bc
    )
    part, packed, scaled, grad_gate = tied(part, packed, scaled, grad_gate)
    rows_part = lax.psum_scatter(part, "head", scatter_dimension=0, tiled=True)
    row_sums = [row_sum, *others(row_sum, "head", 1)]
    row_sum = sum(part[0] for part in row_sums)
    kept = weights_backward([last_grad, normed], [scaled, grad_gate], True)
    early_sent, early = core_sum(kept, traded(early_sent, "seq", 1), norm_sum)
    late_sent = weights_backward([normed], [packed], False)
    kept = weights_backward([normed], [packed], True)
    late_sent, late = core_sum(kept, traded(late_sent, "seq", 1), norm_sum)
    rows_part, early_sent, late_sent = tied(rows_part, early_sent, late_sent)
    early = early + traded(early_sent, "seq", 2)
    late = late + traded(late_sent, "seq", 2)
    middle_share = norm_backward(
        rows_part, own_rows(row_sum), own_rows(second), own_rows(kept_second["rescale"]),
        own_rows(last_grad), weights[1]["norm"], model,
    )
    middle_grad = lax.all_gather(middle_share, "head", axis=0, tiled=True)
    middle_grad, early_second, late_second, outward = tied(middle_grad, early, late, outward)

    grad_mixed, grad_gate, scaled, gain_sum, skip_sum, adjoint = gate_step(
        0, middle_grad, sums_first, (second, first), kept_first, weights[0]
    )
    normed = kept_first["normed"]
    early_sent = weights_backward([middle_grad, normed], [scaled, grad_gate], False)
    grad_mixed, early_sent, outward, *arrived = tied(
        grad_mixed, early_sent, outward, *others(adjoint, "seq", -1)
    )
    packed, tail, back, taps_x, taps_bc, rate_sum, bias_sum = states_step(
        grad_mixed, arrived, kept_first, weights[0]
    )
    for bit in bits[1:]:
        outward = after(halved(outward, "head", bit), tail)
    packed, outward = tied(fixed_tail(packed, tail, back), outward)
    late_sent = weights_backward([normed], [packed], False)
    kept = weights_backward([normed], [packed], True)
    late_sent, late = core_sum(kept, traded(late_sent, "seq", 1), tail)
    packed, late_sent, late = tied(packed, late_sent, late)
    part, row_sum, norm_sum = part_backward(
        head_size, 0, grad_gate, packed, weights[0]["w_z"], weights[0]["pack"], first,
        weights[0]["norm"],
    )
    norm_sum, scaled, grad_gate, outward, *sums_second = tied(
        norm_sum, scaled, grad_gate, outward, *sums_second
    )
    columns_part = lax.psum_scatter(part, "head", scatter_dimension=0, tiled=True)[0]
    row_sums = [row_sum, *others(row_sum, "head", 1)]
    row_sum = sum(part[0] for part in row_sums)
    kept = weights_backward([middle_grad, normed], [scaled, grad_gate], True)
    sent, early = core_sum(kept, traded(early_sent, "seq", 1), norm_sum)
    sent, late_arrived = tied(sent, traded(late_sent, "seq", 2))
    late = late + late_arrived
    late, sent, norm_sum, taps_x, gain_sum, skip_sum, bias_sum, rate_sum, taps_bc = tied(
        late, sent, norm_sum, taps_x, gain_sum, skip_sum, bias_sum, rate_sum, taps_bc
    )
    local_first, whole_first = vectors_of(
        heads, taps_x, gain_sum, skip_sum, bias_sum, rate_sum, norm_sum, taps_bc
    )
    vector = jnp.stack(
        [
            jnp.concatenate([whole_first, local_first]),
            jnp.concatenate([whole_second, local_second]),
        ]
    )
    vector = butterfly(vector, "seq")
    first_share = norm_backward(
        columns_part, row_sum, own_columns(first), kept_first["rescale"],
        own_columns(middle_grad), own_columns(weights[0]["norm"]), model,
    )
    vector = section_sum(vector[0], vector[1], first_share)
    late = section_sum(late, late_second, first_share)
    early = section_sum(early + traded(sent, "seq", 2), early_second, first_share)
    whole = butterfly(vector[: whole_first.shape[0]], "head")
    local = vector[whole_first.shape[0] :]
    last_share = lax.rsqrt(sum(part[0] for part in sums_second) / INNER + epsilon)
    last_share = last_share[:, None] * outward[0].astype(f32)
    last_share = (own_columns(second).astype(f32) + last_share).astype(bf16)
    block_outputs = both_sequences(own_columns(second), last_share, first_share)
    grad_w_bc = late[:, :shared].astype(bf16).reshape(quarter, head_size, shared // head_size)
    grad_w_bc = grad_w_bc.swapaxes(0, 1)
    for bit in bits:
        grad_w_bc = halved(grad_w_bc, "head", bit)
    input_grads = both_sequences(first_share, own_columns(middle_grad))
    at = 0

    def taken(size):
        nonlocal at
        at += size
        return local[at - size : at]

    grad_norm = lax.dynamic_slice_in_dim(whole, head_at * share, share, 0)
    grad_conv_bc = whole[model:].reshape(CONV, shared).T
    grad_conv_x = taken(CONV * width).reshape(CONV, width).T
    grad_gain = taken(width)
    grad_skip = jnp.sum(taken(width).reshape(heads, width // heads), axis=1)
    grad_bias = taken(heads)
    grad_rate = taken(heads)
    return (
        block_outputs[None],
        input_grads[None],
        grad_norm[None],
        early[None, :, width:],
        late[None, :, shared + LANES :],
        grad_w_bc.astype(f32),
        late[None, :, shared : shared + heads],
        grad_conv_x[None],
        grad_conv_bc[None],
        grad_bias[None],
        grad_rate[None],
        grad_skip[None],
        grad_gain[None],
        early[None, :, :width],
    )


def solution(mesh):
    placed = (
        P(None, "seq", None),
        P(None, "seq", None),
        P("section", None),
        P("section", None, "head"),
        P("section", None, "head"),
        P("section", None, None),
        P("section", None, "head"),
        P("section", "head", None),
        P("section", None, None),
        P("section", "head"),
        P("section", "head"),
        P("section", "head"),
        P("section", "head"),
        P("section", None, "head"),
    )
    return jax.shard_map(
        shards,
        mesh=mesh,
        in_specs=placed,
        out_specs=(
            P("section", None, "seq", "head"),
            P("section", None, "seq", "head"),
            P("section", "head"),
            P("section", "seq", "head"),
            P("section", "seq", "head"),
            P("section", "seq", "head"),
            P("section", "seq", "head"),
            P("section", "head", None),
            P("section", None, None),
            P("section", "head"),
            P("section", "head"),
            P("section", "head"),
            P("section", "head"),
            P("section", "seq", "head"),
        ),
        check_vma=False,
    )
```

```python
from functools import partial

import jax
import jax.numpy as jnp
from jax import lax
from jax.experimental import pallas as pl
from jax.experimental.pallas import tpu as pltpu
from jax.sharding import PartitionSpec as P

INNER = 3072
CONV = 4
CHUNK = 128
LANES = 128
ROWS = 256

epsilon = 1e-05
exact = lax.Precision.HIGHEST
f32 = jnp.float32
bf16 = jnp.bfloat16


def dot_nn(left, right, precision=None):
    return lax.dot_general(
        left, right, (((1,), (0,)), ((), ())), precision=precision, preferred_element_type=f32
    )


def dot_nt(left, right, precision=None):
    return lax.dot_general(
        left, right, (((1,), (1,)), ((), ())), precision=precision, preferred_element_type=f32
    )


def dot_tn(left, right):
    return lax.dot_general(left, right, (((0,), (0,)), ((), ())), preferred_element_type=f32)


def three_parts(values):
    high = values.astype(bf16)
    rest = values - high.astype(f32)
    middle = rest.astype(bf16)
    return high, middle, (rest - middle.astype(f32)).astype(bf16)


def lane_sums(values):
    ones = jnp.ones((8, values.shape[1]), bf16)
    return sum(dot_nt(ones, part) for part in three_parts(values))


def times_mask(values, mask):
    rows = values.shape[0]
    product = dot_nn(jnp.concatenate(three_parts(values), axis=0), mask)
    return product[:rows] + product[rows : 2 * rows] + product[2 * rows :]


def mask_times(mask, values):
    columns = values.shape[1]
    product = dot_nn(mask, jnp.concatenate(three_parts(values), axis=1))
    return product[:, :columns] + product[:, columns : 2 * columns] + product[:, 2 * columns :]


def silu_parts(values):
    gate = jax.nn.sigmoid(values)
    return gate, values * gate


def silu_slope(values, gate):
    return gate * (1.0 + values * (1.0 - gate))


def weight_fetch(block, sources, held, sem):
    here = lax.axis_index("section") == block
    away = jnp.logical_not(here)

    @pl.when(here)
    def _():
        pltpu.make_async_copy(sources[0], held, sem).start()

    place = lax.axis_index("seq")
    if len(sources) == 3:
        rows = sources[1].shape[1]
        for piece in range(4):
            target = held.at[piece * rows : (piece + 1) * rows]
            for k in range(2):

                @pl.when(away & (lax.rem(place + piece, 2) == k))
                def _():
                    pltpu.make_async_copy(sources[1 + k].at[piece // 2], target, sem).start()

        return
    rows = sources[1].shape[0]
    for piece in range(4):
        target = held.at[piece * rows : (piece + 1) * rows]
        for k, bits in enumerate((0, 2, 1, 3)):
            bit_low = lax.rem(place + piece, 2) == bits % 2
            bit_high = lax.rem(place // 2 + piece // 2, 2) == bits // 2

            @pl.when(away & bit_low & bit_high)
            def _():
                pltpu.make_async_copy(sources[1 + k], target, sem).start()


def weight_wait(sources, held, sem):
    pltpu.make_async_copy(sources[0], held, sem).wait()


def anywhere():
    return pl.BlockSpec(memory_space=pl.ANY)


def weight_scratch(own):
    return [pltpu.VMEM(own.shape, own.dtype), pltpu.SemaphoreType.DMA]


def head_groups(width, heads):
    head_width = width // heads
    per_group = max(LANES // head_width, 1)
    found = []
    for first in range(0, heads, per_group):
        count = min(per_group, heads - first)
        found.append((first, count, first * head_width, count * head_width))
    return found


def spread(tile, first, count, lanes):
    rows = tile.shape[0]
    head_width = lanes // count
    out = jnp.broadcast_to(tile[:, first : first + 1], (rows, lanes))
    lane = lax.broadcasted_iota(jnp.int32, (rows, lanes), 1)
    for k in range(1, count):
        column = jnp.broadcast_to(tile[:, first + k : first + k + 1], (rows, lanes))
        out = jnp.where(lane >= k * head_width, column, out)
    return out


def own_lanes(tile, k, count):
    if count == 1:
        return tile
    head_width = tile.shape[1] // count
    lane = lax.broadcasted_iota(jnp.int32, tile.shape, 1)
    inside = (lane >= k * head_width) & (lane < (k + 1) * head_width)
    return jnp.where(inside, tile, jnp.zeros_like(tile))


def triangle(keep):
    row = lax.broadcasted_iota(jnp.int32, (CHUNK, CHUNK), 0)
    column = lax.broadcasted_iota(jnp.int32, (CHUNK, CHUNK), 1)
    return keep(row, column)


def decay_of(payload, state):
    rows = payload[state : state + 16].astype(f32)
    return jnp.exp(rows[0:1] + rows[8:9] + rows[12:13])


def project_kernel(
    heads,
    block,
    sources,
    x_in,
    x_edge,
    gain,
    *refs,
):
    pack_sources, refs = refs[:sources], refs[sources:]
    (
        dt_bias, rate, taps_x, taps_bc, normed_out, rescale_out, raw_x, raw_bc,
        edge_x, edge_bc, step_raw, pre_x, pre_bc, act_x, act_bc, dt_out,
        run_out, payload, ext_x, ext_bc, end_out, total_out, pack, pack_sem,
    ) = refs
    step = pl.program_id(0)
    groups = head_groups(raw_x.shape[1], heads)
    shared = act_bc.shape[1]
    state = shared // 2

    def normed_of(block):
        x = block.astype(f32)
        rescale = lax.rsqrt(jnp.mean(x * x, axis=-1, keepdims=True) + epsilon)
        return rescale, (x * rescale * gain[...]).astype(bf16)

    @pl.when(step == 0)
    def _():
        weight_fetch(block, pack_sources, pack, pack_sem)
        _, edge = normed_of(x_edge[...])
        weight_wait(pack_sources, pack, pack_sem)
        edge_x[...] = dot_nn(edge, pack[:, shared + LANES :]).astype(bf16).astype(f32)[8:]
        edge_bc[...] = dot_nn(edge, pack[:, :shared]).astype(bf16).astype(f32)[8:]
        ext_x[0:8] = edge_x[...]
        ext_bc[0:8] = edge_bc[...]
        end_out[...] = jnp.zeros_like(end_out)
        total_out[...] = jnp.zeros_like(total_out)

    @pl.when(step > 0)
    def _():
        ext_x[0:8] = ext_x[ROWS : ROWS + 8]
        ext_bc[0:8] = ext_bc[ROWS : ROWS + 8]

    rescale, normed = normed_of(x_in[...])
    rescale_out[...] = rescale
    normed_out[...] = normed
    low = dot_nn(normed, pack[:, :shared]).astype(bf16)
    raw_bc[...] = low
    ext_bc[8:] = low.astype(f32)
    step_in = dot_nn(normed, pack[:, shared : shared + LANES])
    step_raw[...] = step_in
    sizes = jax.nn.softplus(step_in + dt_bias[...])
    dt_out[...] = sizes
    low = dot_nn(normed, pack[:, shared + LANES :]).astype(bf16)
    raw_x[...] = low
    ext_x[8:] = low.astype(f32)
    for ext, taps, pre, act in ((ext_bc, taps_bc, pre_bc, act_bc), (ext_x, taps_x, pre_x, act_x)):
        total = ext[5 : 5 + ROWS] * taps[0:1]
        for k in range(1, CONV):
            total = total + ext[5 + k : 5 + k + ROWS] * taps[k : k + 1]
        pre[...] = total.astype(bf16)
        act[...] = silu_parts(total)[1].astype(bf16)
    lower = triangle(lambda t, s: t >= s).astype(bf16)
    for sub in range(ROWS // CHUNK):
        at = slice(sub * CHUNK, (sub + 1) * CHUNK)
        dt = sizes[at]
        run = mask_times(lower, dt * rate[...])
        run_out[at] = run
        last = run[CHUNK - 1 : CHUNK]
        weight = jnp.exp(last - run) * dt
        decay = jnp.exp(last)
        b_turned = act_bc[at, :state].astype(f32).T.astype(bf16)
        for first, count, lane, lanes in groups:
            cols = slice(lane, lane + lanes)
            scaled = act_x[at, cols].astype(f32) * spread(weight, first, count, lanes)
            end_out[:, cols] = spread(decay, first, count, lanes) * end_out[:, cols] + dot_nn(
                b_turned, scaled.astype(bf16)
            )
        total_out[...] += jnp.broadcast_to(last, total_out.shape)

    @pl.when(step == pl.num_programs(0) - 1)
    def _():
        for first, count, lane, lanes in groups:
            cols = slice(lane, lane + lanes)
            payload[:state, cols] = end_out[:, cols].astype(bf16)
            total = spread(total_out[...], first, count, lanes)
            high = total.astype(bf16).astype(f32)
            middle = (total - high).astype(bf16).astype(f32)
            low = total - high - middle
            row = lax.broadcasted_iota(jnp.int32, (8, lanes), 0)
            rest = jnp.where(row < 4, middle, low)
            payload[state:, cols] = jnp.concatenate([high, rest], axis=0).astype(bf16)


def full(shape):
    return pl.BlockSpec(shape, lambda i: (0,) * len(shape))


def rows_of(width, back=0):
    if back:
        return pl.BlockSpec((ROWS, width), lambda i: (back - 1 - i, 0))
    return pl.BlockSpec((ROWS, width), lambda i: (i, 0))


def pieces_of(pieces, count, model):
    if pieces == 1:
        return rows_of(model), (count, model)
    lanes = model // pieces
    return pl.BlockSpec((pieces, ROWS, lanes), lambda i: (0, i, 0)), (pieces, count, lanes)


def params():
    return pltpu.CompilerParams(
        dimension_semantics=("arbitrary",), vmem_limit_bytes=60 * 1024 * 1024
    )


def project_forward(
    heads, block, x, x_edge, gain, pack, dt_bias, rate, taps_x, taps_bc
):
    count, model = x.shape
    width, shared = taps_x.shape[1], taps_bc.shape[1]
    state = shared // 2
    return pl.pallas_call(
        partial(project_kernel, heads, block, len(pack)),
        grid=(count // ROWS,),
        in_specs=[
            rows_of(model),
            full((16, model)),
            full((1, model)),
            *[anywhere() for _ in pack],
            full((1, LANES)),
            full((1, LANES)),
            full((CONV, width)),
            full((CONV, shared)),
        ],
        out_specs=[
            rows_of(model),
            rows_of(1),
            rows_of(width),
            rows_of(shared),
            full((8, width)),
            full((8, shared)),
            rows_of(LANES),
            rows_of(width),
            rows_of(shared),
            rows_of(width),
            rows_of(shared),
            rows_of(LANES),
            rows_of(LANES),
            full((state + 16, width)),
        ],
        out_shape=[
            jax.ShapeDtypeStruct((count, model), bf16),
            jax.ShapeDtypeStruct((count, 1), f32),
            jax.ShapeDtypeStruct((count, width), bf16),
            jax.ShapeDtypeStruct((count, shared), bf16),
            jax.ShapeDtypeStruct((8, width), f32),
            jax.ShapeDtypeStruct((8, shared), f32),
            jax.ShapeDtypeStruct((count, LANES), f32),
            jax.ShapeDtypeStruct((count, width), bf16),
            jax.ShapeDtypeStruct((count, shared), bf16),
            jax.ShapeDtypeStruct((count, width), bf16),
            jax.ShapeDtypeStruct((count, shared), bf16),
            jax.ShapeDtypeStruct((count, LANES), f32),
            jax.ShapeDtypeStruct((count, LANES), f32),
            jax.ShapeDtypeStruct((state + 16, width), bf16),
        ],
        scratch_shapes=[
            pltpu.VMEM((8 + ROWS, width), f32),
            pltpu.VMEM((8 + ROWS, shared), f32),
            pltpu.VMEM((state, width), f32),
            pltpu.VMEM((8, LANES), f32),
            *weight_scratch(pack[0]),
        ],
        compiler_params=params(),
        cost_estimate=pl.CostEstimate(
            flops=2 * count * model * pack[0].shape[1],
            bytes_accessed=2 * pack[0].size + count * (4 * model + 6 * (width + shared)),
            transcendentals=count * (width + shared),
        ),
        name="project_forward",
    )(x, x_edge, gain, *pack, dt_bias, rate, taps_x, taps_bc)


def inner_kernel(
    heads, block, act_x, act_bc, dt_in, run_in, normed, *refs
):
    *z_sources, gate_out, inner_out, w_z, z_sem = refs

    @pl.when(pl.program_id(0) == 0)
    def _():
        weight_fetch(block, z_sources, w_z, z_sem)
        weight_wait(z_sources, w_z, z_sem)

    groups = head_groups(act_x.shape[1], heads)
    state = act_bc.shape[1] // 2
    gate_out[...] = dot_nn(normed[...], w_z[...])
    causal = triangle(lambda t, s: t >= s)
    for sub in range(ROWS // CHUNK):
        at = slice(sub * CHUNK, (sub + 1) * CHUNK)
        dt = dt_in[at]
        run = run_in[at]
        turned = run.T
        product = dot_nt(act_bc[at, state:], act_bc[at, :state])
        for first, count, lane, lanes in groups:
            cols = slice(lane, lane + lanes)
            stepped = act_x[at, cols].astype(f32) * spread(dt, first, count, lanes)
            low = stepped.astype(bf16)
            weights = []
            stacked = []
            for k in range(count):
                h = first + k
                gap = jnp.broadcast_to(run[:, h : h + 1], (CHUNK, CHUNK)) - turned[h : h + 1]
                factor = jnp.exp(jnp.where(causal, gap, -jnp.inf))
                weights.append((product * factor).astype(bf16))
                stacked.append(own_lanes(low, k, count))
            inner_out[at, cols] = dot_nn(
                jnp.concatenate(weights, axis=1), jnp.concatenate(stacked, axis=0)
            )


def inner_forward(heads, block, act_x, act_bc, dt, run, normed, w_z):
    count, width = act_x.shape
    model = normed.shape[1]
    shared = act_bc.shape[1]
    return pl.pallas_call(
        partial(inner_kernel, heads, block),
        grid=(count // ROWS,),
        in_specs=[
            rows_of(width),
            rows_of(shared),
            rows_of(LANES),
            rows_of(LANES),
            rows_of(model),
            *[anywhere() for _ in w_z],
        ],
        out_specs=[rows_of(width), rows_of(width)],
        out_shape=[
            jax.ShapeDtypeStruct((count, width), f32),
            jax.ShapeDtypeStruct((count, width), f32),
        ],
        scratch_shapes=weight_scratch(w_z[0]),
        compiler_params=params(),
        cost_estimate=pl.CostEstimate(
            flops=2 * count * width * (4 * CHUNK + model),
            bytes_accessed=count * (10 * width + 2 * model) + 2 * w_z[0].size,
            transcendentals=count * heads * CHUNK,
        ),
        name="inner_forward",
    )(act_x, act_bc, dt, run, normed, *w_z)


def outer_kernel(
    heads,
    block,
    sources,
    pieces,
    shards,
    act_x,
    act_bc,
    dt_in,
    run_in,
    gate_in,
    inner_in,
    *refs,
):
    out_sources, refs = refs[:sources], refs[sources:]
    skip, gain, *refs = refs
    arrived, refs = refs[: shards - 1], refs[shards - 1 :]
    grad_in, refs = (refs[0], refs[1:]) if len(refs) == 9 else (None, refs)
    mixed_out, scaled_out, part_out, sums_out, states_out, held, w_out, out_sem = refs
    groups = head_groups(act_x.shape[1], heads)
    state = act_bc.shape[1] // 2

    @pl.when(pl.program_id(0) == 0)
    def _():
        weight_fetch(block, out_sources, w_out, out_sem)
        place = lax.axis_index("seq")
        held[...] = jnp.zeros_like(held)
        for distance in reversed(range(1, shards)):

            @pl.when(place >= distance)
            def _():
                payload = arrived[distance - 1]
                held[...] = decay_of(payload, state) * held[...] + payload[:state].astype(f32)

        weight_wait(out_sources, w_out, out_sem)

    square_rows = []
    ones = jnp.ones((8, LANES), f32)
    for sub in range(ROWS // CHUNK):
        at = slice(sub * CHUNK, (sub + 1) * CHUNK)
        run = run_in[at]
        last = run[CHUNK - 1 : CHUNK]
        weight = jnp.exp(last - run) * dt_in[at]
        decay = jnp.exp(last)
        grown = jnp.exp(run)
        c_part = act_bc[at, state:]
        b_turned = act_bc[at, :state].astype(f32).T.astype(bf16)
        states_out[sub] = held[...].astype(bf16)
        squares = jnp.zeros((CHUNK, LANES), f32)
        for first, count, lane, lanes in groups:
            cols = slice(lane, lane + lanes)
            x_part = act_x[at, cols].astype(f32)
            before = held[:, cols]
            mixed = inner_in[at, cols] + spread(grown, first, count, lanes) * dot_nn(
                c_part, before.astype(bf16)
            )
            mixed = mixed + skip[:, cols] * x_part
            held[:, cols] = spread(decay, first, count, lanes) * before + dot_nn(
                b_turned, (x_part * spread(weight, first, count, lanes)).astype(bf16)
            )
            gated = mixed * silu_parts(gate_in[at, cols])[1]
            mixed_out[at, cols] = mixed.astype(bf16)
            scaled_out[at, cols] = (gated * gain[:, cols]).astype(bf16)
            square = gated * gated
            if lanes < LANES:
                fill = jnp.zeros((CHUNK, LANES - lanes), f32)
                square = jnp.concatenate([square, fill], axis=1)
            squares = squares + square
        square_rows.append(lane_sums(squares))
    part = dot_nt(scaled_out[...], w_out[...])
    if pieces == 1:
        part_out[...] = part.astype(bf16)
    else:
        wide = part.shape[1] // pieces
        for k in range(pieces):
            part_out[k] = part[:, k * wide : (k + 1) * wide].astype(bf16)
    row = lax.broadcasted_iota(jnp.int32, (8, CHUNK), 0)
    for sub in range(ROWS // CHUNK):
        at = slice(sub * CHUNK, (sub + 1) * CHUNK)
        pair_row = jnp.zeros((8, CHUNK), f32)
        if grad_in is not None:
            pairs = jnp.zeros((CHUNK, LANES), f32)
            for lane in range(0, part.shape[1], LANES):
                cols = slice(lane, lane + LANES)
                pairs = pairs + part[at, cols] * grad_in[at, cols].astype(f32)
            pair_row = lane_sums(pairs)
        sums_out[:, at] = jnp.where(row == 0, square_rows[sub], pair_row)


def outer_forward(
    heads, block, pieces, act_x, act_bc, dt, run, gate_in, inner, w_out, skip, gain, arrived, grad_in
):
    count, width = act_x.shape
    model = w_out[0].shape[0]
    part_spec, part_shape = pieces_of(pieces, count, model)
    shared = act_bc.shape[1]
    state = shared // 2
    subs = ROWS // CHUNK
    extra, extra_specs = [], []
    if grad_in is not None:
        extra, extra_specs = [grad_in], [rows_of(model)]
    return pl.pallas_call(
        partial(outer_kernel, heads, block, len(w_out), pieces, len(arrived) + 1),
        grid=(count // ROWS,),
        in_specs=[
            rows_of(width),
            rows_of(shared),
            rows_of(LANES),
            rows_of(LANES),
            rows_of(width),
            rows_of(width),
            *[anywhere() for _ in w_out],
            full((1, width)),
            full((1, width)),
            *[full(payload.shape) for payload in arrived],
            *extra_specs,
        ],
        out_specs=[
            rows_of(width),
            rows_of(width),
            part_spec,
            pl.BlockSpec((8, ROWS), lambda i: (0, i)),
            pl.BlockSpec((subs, state, width), lambda i: (i, 0, 0)),
        ],
        out_shape=[
            jax.ShapeDtypeStruct((count, width), bf16),
            jax.ShapeDtypeStruct((count, width), bf16),
            jax.ShapeDtypeStruct(part_shape, bf16),
            jax.ShapeDtypeStruct((8, count), f32),
            jax.ShapeDtypeStruct((count // CHUNK, state, width), bf16),
        ],
        scratch_shapes=[pltpu.VMEM((state, width), f32), *weight_scratch(w_out[0])],
        compiler_params=params(),
        cost_estimate=pl.CostEstimate(
            flops=2 * count * width * (2 * state + model),
            bytes_accessed=count * width * 18,
            transcendentals=count * width,
        ),
        name="outer_forward",
    )(
        act_x, act_bc, dt, run, gate_in, inner, *w_out, skip, gain, *arrived, *extra
    )


def gate_kernel(
    heads,
    block,
    sources,
    addends,
    between,
    grad,
    gate_in,
    mixed_in,
    scaled_in,
    act_x,
    act_bc,
    run_in,
    gain,
    *refs,
):
    out_sources, refs = refs[:sources], refs[sources:]
    sums, refs = refs[:addends], refs[addends:]
    later, earlier = refs[:2] if between else (None, None)
    refs = refs[2:] if between else refs
    grad_mixed, grad_gate, scaled_out, gain_sum, skip_sum, adjoint_out, *refs = refs
    grad_in, adjoint, scales, w_out, out_sem = refs
    step = pl.program_id(0)
    groups = head_groups(act_x.shape[1], heads)
    state = act_bc.shape[1] // 2

    @pl.when(step == 0)
    def _():
        weight_fetch(block, out_sources, w_out, out_sem)
        gain_sum[...] = jnp.zeros_like(gain_sum)
        skip_sum[...] = jnp.zeros_like(skip_sum)
        adjoint[...] = jnp.zeros_like(adjoint)
        scales[...] = jnp.zeros_like(scales)
        weight_wait(out_sources, w_out, out_sem)

    grad_in[...] = dot_nn(grad[...], w_out[...])
    total = sums[0][...]
    for more in sums[1:]:
        total = total + more[...]
    scale_row = lax.rsqrt(total[0:1] / INNER + epsilon)
    pull_row = total[1:2] * scale_row * scale_row * scale_row / INNER
    for sub in reversed(range(ROWS // CHUNK)):
        at = slice(sub * CHUNK, (sub + 1) * CHUNK)
        run = run_in[at]
        grown = jnp.exp(run)
        decay = grown[CHUNK - 1 : CHUNK]
        c_turned = act_bc[at, state:].astype(f32).T.astype(bf16)
        scales[0:1] = scale_row[:, at]
        scales[1:2] = pull_row[:, at]
        columns = scales[...].T
        row_scale = columns[:, 0:1]
        row_pull = columns[:, 1:2]
        if later is not None:
            moved = later[at].astype(f32) - earlier[at].astype(f32)
            pulled = jnp.sum(grad[at].astype(f32) * moved, axis=1, keepdims=True)
            row_pull = pulled * row_scale * row_scale * (1.0 / INNER)
        for first, count, lane, lanes in groups:
            cols = slice(lane, lane + lanes)
            gate = gate_in[at, cols]
            mixed = mixed_in[at, cols].astype(f32)
            share, active = silu_parts(gate)
            gated = mixed * active
            d_scaled = grad_in[at, cols] * row_scale
            d_gated = d_scaled * gain[:, cols] - row_pull * gated
            d_mixed = d_gated * active
            grad_mixed[at, cols] = d_mixed.astype(bf16)
            grad_gate[at, cols] = (d_gated * mixed * silu_slope(gate, share)).astype(bf16)
            scaled_out[at, cols] = (scaled_in[at, cols].astype(f32) * row_scale).astype(bf16)
            gain_sum[0:1, cols] += jnp.sum(d_scaled * gated, axis=0, keepdims=True)
            skip_sum[0:1, cols] += jnp.sum(
                d_mixed * act_x[at, cols].astype(f32), axis=0, keepdims=True
            )
            adjoint[:, cols] = spread(decay, first, count, lanes) * adjoint[:, cols] + dot_nn(
                c_turned, (d_mixed * spread(grown, first, count, lanes)).astype(bf16)
            )

    @pl.when(step == pl.num_programs(0) - 1)
    def _():
        adjoint_out[...] = adjoint[...].astype(bf16)


def gate_backward(
    heads, block, grad, w_out, gate_in, mixed, scaled, act_x, act_bc, run, gain, sums, ends
):
    count, width = act_x.shape
    model = grad.shape[1]
    shared = act_bc.shape[1]
    state = shared // 2
    steps = count // ROWS
    return pl.pallas_call(
        partial(gate_kernel, heads, block, len(w_out), len(sums), len(ends) > 0),
        grid=(steps,),
        in_specs=[
            rows_of(model, steps),
            rows_of(width, steps),
            rows_of(width, steps),
            rows_of(width, steps),
            rows_of(width, steps),
            rows_of(shared, steps),
            rows_of(LANES, steps),
            full((1, width)),
            *[anywhere() for _ in w_out],
            *[pl.BlockSpec((8, ROWS), lambda i: (0, steps - 1 - i)) for _ in sums],
            *[rows_of(model, steps) for _ in ends],
        ],
        out_specs=[
            rows_of(width, steps),
            rows_of(width, steps),
            rows_of(width, steps),
            full((8, width)),
            full((8, width)),
            full((state, width)),
        ],
        out_shape=[
            jax.ShapeDtypeStruct((count, width), bf16),
            jax.ShapeDtypeStruct((count, width), bf16),
            jax.ShapeDtypeStruct((count, width), bf16),
            jax.ShapeDtypeStruct((8, width), f32),
            jax.ShapeDtypeStruct((8, width), f32),
            jax.ShapeDtypeStruct((state, width), bf16),
        ],
        scratch_shapes=[
            pltpu.VMEM((ROWS, width), f32),
            pltpu.VMEM((state, width), f32),
            pltpu.VMEM((CHUNK, CHUNK), f32),
            *weight_scratch(w_out[0]),
        ],
        compiler_params=params(),
        cost_estimate=pl.CostEstimate(
            flops=2 * count * width * (state + model),
            bytes_accessed=count * width * 16,
            transcendentals=count * width,
        ),
        name="gate_backward",
    )(
        grad, gate_in, mixed, scaled, act_x, act_bc, run, gain, *w_out, *sums, *ends
    )


def states_kernel(
    heads,
    shards,
    grad_mixed,
    act_x,
    act_bc,
    pre_x,
    pre_bc,
    raw_x,
    raw_bc,
    edge_x,
    edge_bc,
    dt_in,
    run_in,
    step_raw,
    dt_bias,
    rate_rows,
    states_in,
    skip,
    taps_x,
    taps_bc,
    members,
    *refs,
):
    arrived, payloads, refs = refs[: shards - 1], refs[shards - 1 : 2 * shards - 2], refs[2 * shards - 2 :]
    packed, tail, back, tap_sum_x, tap_sum_bc, rate_sum, bias_sum, *refs = refs
    adjoint, d_pre_x, d_pre_bc, rows_ref, carry_ref, square_ref = refs
    step = pl.program_id(0)
    steps = pl.num_programs(0)
    groups = head_groups(act_x.shape[1], heads)
    shared = act_bc.shape[1]
    state = shared // 2
    padded = members.shape[0]

    @pl.when(step == 0)
    def _():
        place = lax.axis_index("seq")
        adjoint[...] = jnp.zeros_like(adjoint)
        for distance in reversed(range(1, shards)):

            @pl.when(place + distance < shards)
            def _():
                decay = decay_of(payloads[shards - 1 - distance], state)
                adjoint[...] = decay * adjoint[...] + arrived[distance - 1][...].astype(f32)

        d_pre_x[8:16] = jnp.zeros((8, d_pre_x.shape[1]), f32)
        d_pre_bc[8:16] = jnp.zeros((8, d_pre_bc.shape[1]), f32)
        tap_sum_x[...] = jnp.zeros_like(tap_sum_x)
        tap_sum_bc[...] = jnp.zeros_like(tap_sum_bc)
        rate_sum[...] = jnp.zeros_like(rate_sum)
        bias_sum[...] = jnp.zeros_like(bias_sum)
        rows_ref[...] = jnp.zeros_like(rows_ref)
        square_ref[...] = jnp.zeros_like(square_ref)

    upto = triangle(lambda s, t: s <= t)
    not_before = triangle(lambda s, t: s >= t).astype(bf16)
    before = triangle(lambda s, t: s < t).astype(bf16)
    head_lane = lax.broadcasted_iota(jnp.int32, (CHUNK, LANES), 1)
    for sub in reversed(range(ROWS // CHUNK)):
        at = slice(sub * CHUNK, (sub + 1) * CHUNK)
        dt = dt_in[at]
        run = run_in[at]
        last = run[CHUNK - 1 : CHUNK]
        grown = jnp.exp(run)
        decay = grown[CHUNK - 1 : CHUNK]
        to_end = jnp.exp(last - run)
        run_turned = run.T
        dt_turned = dt.T[0:padded]
        inside_tile = jnp.zeros((CHUNK, LANES), f32)
        b_part = act_bc[at, :state]
        c_part = act_bc[at, state:]
        c_turned = c_part.astype(f32).T.astype(bf16)
        product = dot_nt(b_part, c_part)
        d_product = jnp.zeros((CHUNK, CHUNK), f32)
        d_b = jnp.zeros((CHUNK, state), f32)
        d_c = jnp.zeros((CHUNK, state), f32)
        d_pre_x[CHUNK + 8 : CHUNK + 16] = d_pre_x[8:16]
        d_pre_bc[CHUNK + 8 : CHUNK + 16] = d_pre_bc[8:16]
        through = []
        for first, count, lane, lanes in groups:
            cols = slice(lane, lane + lanes)
            x_low = act_x[at, cols]
            x_part = x_low.astype(f32)
            dy_low = grad_mixed[at, cols]
            dy = dy_low.astype(f32)
            dt_wide = spread(dt, first, count, lanes)
            ending = spread(to_end, first, count, lanes)
            growing = spread(grown, first, count, lanes)
            lam = adjoint[:, cols]
            lam_low = lam.astype(bf16)
            held_low = states_in[sub][:, cols]
            weights = []
            stacked = []
            for k in range(count):
                h = first + k
                gap = run_turned[h : h + 1] - jnp.broadcast_to(run[:, h : h + 1], (CHUNK, CHUNK))
                factor = jnp.exp(jnp.where(upto, gap, -jnp.inf))
                weights.append((product * factor).astype(bf16))
                stacked.append(own_lanes(dy_low, k, count))
                paired = dot_nt(own_lanes(x_low, k, count), dy_low) * factor
                dt_column = jnp.broadcast_to(dt[:, h : h + 1], (CHUNK, CHUNK))
                d_product = d_product + paired * dt_column
                inside = paired * product
                rows_ref[h : h + 1] = jnp.sum(inside * dt_column, axis=0, keepdims=True)
                inside_tile = jnp.where(
                    head_lane == h, jnp.sum(inside, axis=1, keepdims=True), inside_tile
                )
            d_stepped = dot_nn(jnp.concatenate(weights, axis=1), jnp.concatenate(stacked, axis=0))
            from_end = ending * dot_nn(b_part, lam_low)
            d_x = dt_wide * (d_stepped + from_end) + skip[:, cols] * dy
            dy_grown = dy * growing
            dy_grown_low = dy_grown.astype(bf16)
            carry_ref[0, :, cols] = (x_part * from_end).astype(bf16)
            carry_ref[1, :, cols] = (dy_grown * dot_nn(c_part, held_low)).astype(bf16)
            d_b = d_b + dot_nt((x_part * dt_wide * ending).astype(bf16), lam_low)
            d_c = d_c + dot_nt(dy_grown_low, held_low)
            wide_decay = spread(decay, first, count, lanes)
            lam_decayed = wide_decay * lam
            through.append(
                jnp.sum(lam_decayed * held_low.astype(f32), axis=0, keepdims=True)
            )
            adjoint[:, cols] = lam_decayed + dot_nn(c_turned, dy_grown_low)
            pre = pre_x[at, cols].astype(f32)
            d_pre_x[8 : CHUNK + 8, cols] = d_x * silu_slope(pre, jax.nn.sigmoid(pre))
        member = members[...]
        kept = dot_nt(member, carry_ref[0])
        fed = dot_nt(member, carry_ref[1])
        wide_row = jnp.concatenate(through, axis=1)
        across = jnp.sum(member.astype(f32) * wide_row, axis=1, keepdims=True)
        inside_rows = inside_tile.T[0:padded]
        d_log = (
            times_mask(rows_ref[...] - dt_turned * inside_rows + fed, not_before)
            + times_mask(dt_turned * kept, before)
            + across
        )
        d_log_rate = d_log * rate_rows[...]
        rate_sum[...] += d_log_rate * dt_turned
        square_ref[0:padded] = d_log_rate + inside_rows + kept
        d_step_exact = square_ref[...].T * jax.nn.sigmoid(step_raw[at] + dt_bias[...])
        bias_sum[0:1] += jnp.sum(d_step_exact, axis=0, keepdims=True)
        packed[at, shared : shared + LANES] = d_step_exact.astype(bf16)
        if sub == ROWS // CHUNK - 1:

            @pl.when(step == 0)
            def _():
                tail[:, shared : shared + LANES] = d_step_exact[CHUNK - 16 :]

        d_product_low = d_product.astype(bf16)
        d_b = d_b + dot_nn(d_product_low, c_part)
        d_c = d_c + dot_nn(d_product.T.astype(bf16), b_part)
        pre = pre_bc[at].astype(f32)
        slope = silu_slope(pre, jax.nn.sigmoid(pre))
        d_pre_bc[8 : CHUNK + 8, :state] = d_b * slope[:, :state]
        d_pre_bc[8 : CHUNK + 8, state:] = d_c * slope[:, state:]
        for d_pre, raw, taps, place, tap_sum in (
            (d_pre_x, raw_x, taps_x, slice(shared + LANES, None), tap_sum_x),
            (d_pre_bc, raw_bc, taps_bc, slice(0, shared), tap_sum_bc),
        ):
            values = raw[at].astype(f32)
            total = jnp.zeros_like(values)
            for k in range(CONV):
                moved = d_pre[11 - k : 11 - k + CHUNK]
                total = total + moved * taps[k : k + 1]
                tap_sum[k : k + 1] += jnp.sum(values * moved, axis=0, keepdims=True)
            packed[at, place] = total.astype(bf16)
            if sub == ROWS // CHUNK - 1:

                @pl.when(step == 0)
                def _():
                    tail[:, place] = total[CHUNK - 16 :]

    @pl.when(step == steps - 1)
    def _():
        back[...] = jnp.zeros_like(back)
        for d_pre, edge, taps, tap_sum, place in (
            (d_pre_x, edge_x, taps_x, tap_sum_x, slice(shared + LANES, None)),
            (d_pre_bc, edge_bc, taps_bc, tap_sum_bc, slice(0, shared)),
        ):
            d_pre[0:8] = jnp.zeros((8, d_pre.shape[1]), f32)
            values = edge[...]
            total = jnp.zeros_like(values)
            for k in range(CONV):
                moved = d_pre[3 - k : 11 - k]
                total = total + moved * taps[k : k + 1]
                tap_sum[k : k + 1] += jnp.sum(values * moved, axis=0, keepdims=True)
            back[8:, place] = total


def states_backward(
    heads,
    grad_mixed,
    act_x,
    act_bc,
    pre_x,
    pre_bc,
    raw_x,
    raw_bc,
    edge_x,
    edge_bc,
    dt,
    run,
    step_raw,
    dt_bias,
    rate,
    states,
    skip,
    taps_x,
    taps_bc,
    arrived,
    payloads,
):
    count, width = act_x.shape
    shared = act_bc.shape[1]
    state = shared // 2
    steps = count // ROWS
    subs = ROWS // CHUNK
    padded = -(-heads // 16) * 16
    head_of = jnp.arange(width)[None, :] // (width // heads)
    members = (jnp.arange(padded)[:, None] == head_of).astype(bf16)
    rate_rows = jnp.broadcast_to(rate[0, :padded, None], (padded, CHUNK))
    return pl.pallas_call(
        partial(states_kernel, heads, len(arrived) + 1),
        grid=(steps,),
        in_specs=[
            rows_of(width, steps),
            rows_of(width, steps),
            rows_of(shared, steps),
            rows_of(width, steps),
            rows_of(shared, steps),
            rows_of(width, steps),
            rows_of(shared, steps),
            full((8, width)),
            full((8, shared)),
            rows_of(LANES, steps),
            rows_of(LANES, steps),
            rows_of(LANES, steps),
            full((1, LANES)),
            full((padded, CHUNK)),
            pl.BlockSpec((subs, state, width), lambda i: (steps - 1 - i, 0, 0)),
            full((1, width)),
            full((CONV, width)),
            full((CONV, shared)),
            full((padded, width)),
            *[full(array.shape) for array in (*arrived, *payloads)],
        ],
        out_specs=[
            rows_of(shared + LANES + width, steps),
            full((16, shared + LANES + width)),
            full((16, shared + LANES + width)),
            full((8, width)),
            full((8, shared)),
            full((padded, CHUNK)),
            full((8, LANES)),
        ],
        out_shape=[
            jax.ShapeDtypeStruct((count, shared + LANES + width), bf16),
            jax.ShapeDtypeStruct((16, shared + LANES + width), f32),
            jax.ShapeDtypeStruct((16, shared + LANES + width), f32),
            jax.ShapeDtypeStruct((8, width), f32),
            jax.ShapeDtypeStruct((8, shared), f32),
            jax.ShapeDtypeStruct((padded, CHUNK), f32),
            jax.ShapeDtypeStruct((8, LANES), f32),
        ],
        scratch_shapes=[
            pltpu.VMEM((state, width), f32),
            pltpu.VMEM((CHUNK + 16, width), f32),
            pltpu.VMEM((CHUNK + 16, shared), f32),
            pltpu.VMEM((padded, CHUNK), f32),
            pltpu.VMEM((2, CHUNK, width), bf16),
            pltpu.VMEM((CHUNK, CHUNK), f32),
        ],
        compiler_params=params(),
        cost_estimate=pl.CostEstimate(
            flops=20 * count * width * state,
            bytes_accessed=count * width * 16,
            transcendentals=count * heads * CHUNK * 2,
        ),
        name="states_backward",
    )(
        grad_mixed,
        act_x,
        act_bc,
        pre_x,
        pre_bc,
        raw_x,
        raw_bc,
        edge_x,
        edge_bc,
        dt,
        run,
        step_raw,
        dt_bias,
        rate_rows,
        states,
        skip,
        taps_x,
        taps_bc,
        members,
        *arrived,
        *payloads,
    )


def part_kernel(
    pieces,
    block,
    sources,
    grad_gate,
    packed,
    x_in,
    gain,
    *refs,
):
    z_sources, refs = refs[:sources], refs[sources:]
    *pack_sources, part_out, row_sum, norm_sum, part_ref, w_z, z_sem, pack, pack_sem = refs

    @pl.when(pl.program_id(0) == 0)
    def _():
        weight_fetch(block, z_sources, w_z, z_sem)
        weight_fetch(block, pack_sources, pack, pack_sem)
        weight_wait(z_sources, w_z, z_sem)
        weight_wait(pack_sources, pack, pack_sem)
        norm_sum[...] = jnp.zeros_like(norm_sum)

    x = x_in[...].astype(f32)
    rescale = lax.rsqrt(jnp.mean(x * x, axis=-1, keepdims=True) + epsilon)
    part_ref[...] = dot_nt(grad_gate[...], w_z[...]) + dot_nt(packed[...], pack[...])
    total = jnp.zeros((ROWS, LANES), f32)
    for lane in range(0, x.shape[1], LANES):
        cols = slice(lane, lane + LANES)
        pulled = part_ref[:, cols] * (x_in[:, cols].astype(f32) * rescale)
        norm_sum[0:1, cols] += jnp.sum(pulled, axis=0, keepdims=True)
        total = total + pulled * gain[:, cols]
    row_sum[...] = lane_sums(total)
    if pieces == 1:
        part_out[...] = part_ref[...].astype(bf16)
    else:
        lanes = x.shape[1] // pieces
        for k in range(pieces):
            part_out[k] = part_ref[:, k * lanes : (k + 1) * lanes].astype(bf16)


def part_backward(
    pieces, block, grad_gate, packed, w_z, pack, x, gain
):
    count, width = grad_gate.shape
    model = x.shape[1]
    part_spec, part_shape = pieces_of(pieces, count, model)
    return pl.pallas_call(
        partial(part_kernel, pieces, block, len(w_z)),
        grid=(count // ROWS,),
        in_specs=[
            rows_of(width),
            rows_of(packed.shape[1]),
            rows_of(model),
            full((1, model)),
            *[anywhere() for _ in (*w_z, *pack)],
        ],
        out_specs=[part_spec, pl.BlockSpec((8, ROWS), lambda i: (0, i)), full((8, model))],
        out_shape=[
            jax.ShapeDtypeStruct(part_shape, bf16),
            jax.ShapeDtypeStruct((8, count), f32),
            jax.ShapeDtypeStruct((8, model), f32),
        ],
        scratch_shapes=[
            pltpu.VMEM((ROWS, model), f32),
            *weight_scratch(w_z[0]),
            *weight_scratch(pack[0]),
        ],
        compiler_params=params(),
        cost_estimate=pl.CostEstimate(
            flops=2 * count * model * (width + packed.shape[1]),
            bytes_accessed=2 * (w_z[0].size + pack[0].size) + 8 * count * model,
            transcendentals=0,
        ),
        name="part_backward",
    )(grad_gate, packed, x, gain, *w_z, *pack)


def weights_kernel(count, low, *refs):
    lefts, rights, out = refs[:count], refs[count : 2 * count], refs[2 * count]
    lane = 0
    for left, right in zip(lefts, rights):
        lanes = right.shape[1]
        out[0, :, lane : lane + lanes] = dot_tn(left[...], right[...]).astype(bf16)
        lane += lanes


def weights_backward(lefts, rights, kept):
    count, model = lefts[0].shape
    rows = model // 4
    lanes = sum(right.shape[1] for right in rights)
    low = lax.rem(lax.axis_index("seq"), 2)
    low = (low if kept else 1 - low).astype(jnp.int32).reshape(1)
    return pl.pallas_call(
        partial(weights_kernel, len(lefts)),
        grid_spec=pltpu.PrefetchScalarGridSpec(
            num_scalar_prefetch=1,
            grid=(2,),
            in_specs=[
                *[pl.BlockSpec((count, rows), lambda i, low: (0, 2 * i + low[0])) for _ in lefts],
                *[pl.BlockSpec(right.shape, lambda i, low: (0, 0)) for right in rights],
            ],
            out_specs=pl.BlockSpec((1, rows, lanes), lambda i, low: (i, 0, 0)),
        ),
        out_shape=jax.ShapeDtypeStruct((2, rows, lanes), bf16),
        compiler_params=params(),
        cost_estimate=pl.CostEstimate(
            flops=count * model * lanes,
            bytes_accessed=2 * (len(lefts) * count * model + count * lanes + model * lanes),
            transcendentals=0,
        ),
        name="weights_backward",
    )(low, *lefts, *rights)


def traded(block, axis, bit):
    return lax.ppermute(block, axis, [(i, i ^ bit) for i in range(lax.axis_size(axis))])


def rotated(block, axis, distance):
    size = lax.axis_size(axis)
    return lax.ppermute(block, axis, [(i, (i + distance) % size) for i in range(size)])


def others(block, axis, sign):
    return [rotated(block, axis, sign * d) for d in range(1, lax.axis_size(axis))]


def bits_of(axis):
    bit = 1
    while bit < lax.axis_size(axis):
        yield bit
        bit *= 2


def butterfly(block, axis):
    for bit in bits_of(axis):
        block = block + traded(block, axis, bit)
    return block


def parted(pieces, axis, bit):
    pairs = pieces.reshape((pieces.shape[0] // 2, 2) + pieces.shape[1:])
    mine = lax.rem(lax.axis_index(axis) // bit, 2)
    return (
        lax.dynamic_index_in_dim(pairs, mine, 1, False),
        lax.dynamic_index_in_dim(pairs, 1 - mine, 1, False),
    )


def halved(pieces, axis, bit):
    kept, sent = parted(pieces, axis, bit)
    return kept + traded(sent, axis, bit)


def core_sum(kept, arrived, earlier):
    high = lax.axis_index("seq") // 2

    def summed(at):
        own = lax.dynamic_index_in_dim(kept, at, 0, False)
        return after(own + lax.dynamic_index_in_dim(arrived, at, 0, False), earlier)

    return summed(1 - high), summed(high)


def after(value, earlier):
    return value + (0.0 * earlier.reshape(-1)[0].astype(f32)).astype(value.dtype)


def moved_along(block, axis, distance):
    size, place = lax.axis_size(axis), lax.axis_index(axis)
    arrived = rotated(block, axis, distance)
    outside = (place < distance) | (place >= size + distance)
    return jnp.where(outside, jnp.zeros_like(arrived), arrived)


def tied(*values):
    return lax.optimization_barrier(values)


def block_forward(
    block, x, x_edge, weights, grad, pieces, mixed_inside=lambda inner, payloads: (inner, payloads)
):
    heads = weights["heads"]
    (
        normed, rescale, raw_x, raw_bc, edge_x, edge_bc, step_raw, pre_x, pre_bc, act_x, act_bc,
        dt, run, payload,
    ) = project_forward(
        heads, block, x, x_edge, weights["norm"], weights["pack"], weights["dt_bias"],
        weights["rate"], weights["taps_x"], weights["taps_bc"],
    )
    payloads = others(payload, "seq", 1)
    gate_in, inner = inner_forward(
        heads, block, act_x, act_bc, dt, run, normed, weights["w_z"]
    )
    inner, payloads = mixed_inside(inner, payloads)
    mixed, scaled, part, sums, states = outer_forward(
        heads, block, pieces, act_x, act_bc, dt, run, gate_in, inner, weights["w_out"],
        weights["skip"], weights["gain"], payloads, grad,
    )
    kept = dict(
        raw_x=raw_x, raw_bc=raw_bc, step_raw=step_raw, edge_x=edge_x, edge_bc=edge_bc,
        gate_in=gate_in, pre_x=pre_x, pre_bc=pre_bc, act_x=act_x, act_bc=act_bc, dt=dt, run=run,
        payloads=payloads, mixed=mixed, scaled=scaled, states=states, normed=normed,
        rescale=rescale,
    )
    return part, sums, kept


def gate_step(block, grad, sums, ends, kept, weights):
    return gate_backward(
        weights["heads"], block, grad, weights["w_out"], kept["gate_in"], kept["mixed"],
        kept["scaled"], kept["act_x"], kept["act_bc"], kept["run"], weights["gain"], sums, ends,
    )


def states_step(grad_mixed, arrived, kept, weights):
    return states_backward(
        weights["heads"], grad_mixed, kept["act_x"], kept["act_bc"], kept["pre_x"],
        kept["pre_bc"], kept["raw_x"], kept["raw_bc"], kept["edge_x"], kept["edge_bc"],
        kept["dt"], kept["run"], kept["step_raw"], weights["dt_bias"], weights["rate"],
        kept["states"], weights["skip"], weights["taps_x"], weights["taps_bc"], arrived,
        kept["payloads"],
    )


def fixed_tail(packed, tail, back):
    rows = tail + moved_along(back, "seq", -1)
    return packed.at[packed.shape[0] - 16 :].set(rows.astype(bf16))


def vectors_of(heads, taps_x, gain_sum, skip_sum, bias_sum, rate_sum, norm_sum, taps_bc):
    return (
        jnp.concatenate(
            [
                taps_x[:CONV].reshape(-1), gain_sum[0], skip_sum[0], bias_sum[0, :heads],
                jnp.sum(rate_sum[:heads], axis=1),
            ]
        ),
        jnp.concatenate([norm_sum[0], taps_bc[:CONV].reshape(-1)]),
    )


def norm_backward(d_normed, row_sum, x, rescale, grad, gain, model):
    unit = x.astype(f32) * rescale
    h = d_normed.astype(f32) * gain
    out = grad.astype(f32) + rescale * (h - unit * (row_sum / model)[:, None])
    return out.astype(bf16)


def shards(
    tokens, cotangent, norm_gain, w_z, w_x, w_bc, w_dt, conv_x, conv_bc, dt_bias, a_log, skip_d,
    gate_gain, w_out,
):
    section = lax.axis_index("section")
    seq_at = lax.axis_index("seq")
    seq_size = lax.axis_size("seq")
    count, model = tokens.shape[1:]
    head_size = lax.axis_size("head")
    head_at = lax.axis_index("head")
    heads = a_log.shape[1]
    width = w_x.shape[2]
    shared = w_bc.shape[2]
    share = model // head_size
    row_share = count // head_size
    quarter = model // seq_size

    def mine_first(of_first, of_second):
        return (
            jnp.where(section == 0, of_first, of_second),
            jnp.where(section == 0, of_second, of_first),
        )

    def quarter_of(weight):
        return lax.dynamic_slice_in_dim(weight, seq_at * quarter, quarter, 0)

    def half_of(weight):
        pairs = weight.reshape(2, 2, quarter, weight.shape[1])
        return lax.dynamic_index_in_dim(pairs, lax.rem(seq_at, 2), 1, False)

    def own_rows(array):
        return lax.dynamic_slice_in_dim(array, head_at * row_share, row_share, 0)

    def own_columns(array):
        return lax.dynamic_slice_in_dim(array, head_at * share, share, 1)

    def edge_of(x):
        return jnp.pad(moved_along(x[count - (CONV - 1) :], "seq", 1), ((16 - (CONV - 1), 0), (0, 0)))

    def section_sum(of_first, of_second, earlier=None):
        mine, other = mine_first(of_first, of_second)
        arrived = traded(other, "section", 1)
        if earlier is not None:
            arrived = after(arrived, earlier)
        return mine.astype(f32) + arrived.astype(f32)

    def both_sequences(of_first, of_second, earlier=None):
        mine, other = mine_first(of_first, of_second)
        arrived = traded(other, "section", 1)
        if earlier is not None:
            arrived = after(arrived, earlier)
        return jnp.stack(mine_first(mine, arrived))

    padded_dt = jnp.pad(w_dt[0], ((0, 0), (0, LANES - heads)))
    got_pack = traded(
        jnp.concatenate([quarter_of(w) for w in (w_bc[0], padded_dt, w_x[0])], axis=1),
        "section", 1,
    )
    pack = jnp.concatenate([w_bc[0], padded_dt, w_x[0]], axis=1)
    vector = jnp.concatenate(
        [
            norm_gain[0], conv_x[0].T.reshape(-1), conv_bc[0].T.reshape(-1), dt_bias[0], a_log[0],
            skip_d[0], gate_gain[0],
        ]
    )
    got_pack, part_z, vector = tied(got_pack, half_of(w_z[0]), vector)
    vectors = mine_first(vector, traded(vector, "section", 1))
    first = lax.dynamic_index_in_dim(tokens, section, 0, False)
    first_edge = edge_of(first)
    got_z = traded(part_z, "section", 1)
    far_pack = traded(got_pack, "seq", 2)
    far_pack, got_z, part_out, pack, first, first_edge, *vectors = tied(
        far_pack, got_z, half_of(w_out[0]), pack, first, first_edge, *vectors
    )
    got_out = traded(part_out, "section", 1)
    sources_pack = (got_pack, far_pack, traded(got_pack, "seq", 1), traded(far_pack, "seq", 1))
    sources = dict(
        pack=(pack, *sources_pack), w_z=(w_z[0], got_z, traded(got_z, "seq", 1)), w_out=[w_out[0]]
    )
    weights = []
    for b in range(2):
        at = 0

        def take(size):
            nonlocal at
            at += size
            return vectors[b][at - size : at]

        block = dict(heads=heads, **sources)
        block["norm"] = take(model)[None]
        block["taps_x"] = take(CONV * width).reshape(CONV, width)
        block["taps_bc"] = take(CONV * shared).reshape(CONV, shared)
        block["dt_bias"] = jnp.pad(take(heads), (0, LANES - heads))[None]
        block["rate"] = jnp.pad(-jnp.exp(take(heads)), (0, LANES - heads))[None]
        block["skip"] = jnp.repeat(take(heads), width // heads)[None]
        block["gain"] = take(width)[None]
        weights.append(block)

    last_grad = lax.dynamic_index_in_dim(cotangent, section, 0, False)

    def fetch_out(inner, payloads):
        inner, part, *payloads = tied(inner, got_out, *payloads)
        sources["w_out"] += [part, traded(part, "seq", 1)]
        return inner, payloads

    part, sums, kept_first = block_forward(
        0, first, first_edge, weights[0], None, 1, fetch_out
    )
    summed = lax.psum_scatter(part, "head", scatter_dimension=0, tiled=True).astype(f32)
    sums_first = [sums, *others(sums, "head", 1)]
    scale_first = lax.rsqrt(sum(part[0] for part in sums_first) / INNER + epsilon)
    second_share = own_rows(first).astype(f32) + own_rows(scale_first)[:, None] * summed
    second = lax.all_gather(second_share.astype(bf16), "head", axis=0, tiled=True)

    outward, sums, kept_second = block_forward(
        1, second, edge_of(second), weights[1], last_grad, head_size
    )
    sums_second = [sums, *others(sums, "head", 1)]
    bits = list(bits_of("head"))

    grad_mixed, grad_gate, scaled, gain_sum, skip_sum, adjoint = gate_step(
        1, last_grad, sums_second, (), kept_second, weights[1]
    )
    normed = kept_second["normed"]
    early_sent = weights_backward([last_grad, normed], [scaled, grad_gate], False)
    grad_mixed, early_sent, outward, *arrived = tied(
        grad_mixed, early_sent, outward, *others(adjoint, "seq", -1)
    )
    packed, tail, back, taps_x, taps_bc, rate_sum, bias_sum = states_step(
        grad_mixed, arrived, kept_second, weights[1]
    )
    kept, sent = parted(outward, "head", bits[0])
    packed, kept, arrived = tied(
        fixed_tail(packed, tail, back), kept, traded(sent, "head", bits[0])
    )
    part, row_sum, norm_sum = part_backward(
        1, 1, grad_gate, packed, weights[1]["w_z"], weights[1]["pack"], second,
        weights[1]["norm"],
    )
    norm_sum, kept, taps_x, gain_sum, skip_sum, bias_sum, rate_sum, taps_bc = tied(
        norm_sum, kept, taps_x, gain_sum, skip_sum, bias_sum, rate_sum, taps_bc
    )
    outward = kept + arrived
    local_second, whole_second = vectors_of(
        heads, taps_x, gain_sum, skip_sum, bias_sum, rate_sum, norm_sum, taps_bc
    )
    part, packed, scaled, grad_gate = tied(part, packed, scaled, grad_gate)
    rows_part = lax.psum_scatter(part, "head", scatter_dimension=0, tiled=True)
    row_sums = [row_sum, *others(row_sum, "head", 1)]
    row_sum = sum(part[0] for part in row_sums)
    kept = weights_backward([last_grad, normed], [scaled, grad_gate], True)
    early_sent, early = core_sum(kept, traded(early_sent, "seq", 1), norm_sum)
    late_sent = weights_backward([normed], [packed], False)
    kept = weights_backward([normed], [packed], True)
    late_sent, late = core_sum(kept, traded(late_sent, "seq", 1), norm_sum)
    rows_part, early_sent, late_sent = tied(rows_part, early_sent, late_sent)
    early = early + traded(early_sent, "seq", 2)
    late = late + traded(late_sent, "seq", 2)
    middle_share = norm_backward(
        rows_part, own_rows(row_sum), own_rows(second), own_rows(kept_second["rescale"]),
        own_rows(last_grad), weights[1]["norm"], model,
    )
    middle_grad = lax.all_gather(middle_share, "head", axis=0, tiled=True)
    middle_grad, early_second, late_second, outward, local_second, whole_second = tied(
        middle_grad, early, late, outward, local_second, whole_second
    )
    for bit in bits[1:-1]:
        outward = halved(outward, "head", bit)
    out_kept, out_sent = parted(outward, "head", bits[-1])

    grad_mixed, grad_gate, scaled, gain_sum, skip_sum, adjoint = gate_step(
        0, middle_grad, sums_first, (second, first), kept_first, weights[0]
    )
    normed = kept_first["normed"]
    early_sent = weights_backward([middle_grad, normed], [scaled, grad_gate], False)
    grad_mixed, early_sent, out_sent, *arrived = tied(
        grad_mixed, early_sent, out_sent, *others(adjoint, "seq", -1)
    )
    packed, tail, back, taps_x, taps_bc, rate_sum, bias_sum = states_step(
        grad_mixed, arrived, kept_first, weights[0]
    )
    packed, out_arrived = tied(
        fixed_tail(packed, tail, back), traded(out_sent, "head", bits[-1])
    )
    late_sent = weights_backward([normed], [packed], False)
    kept = weights_backward([normed], [packed], True)
    late_sent, late = core_sum(kept, traded(late_sent, "seq", 1), tail)
    packed, late_sent, late = tied(packed, late_sent, late)
    part, row_sum, norm_sum = part_backward(
        head_size, 0, grad_gate, packed, weights[0]["w_z"], weights[0]["pack"], first,
        weights[0]["norm"],
    )
    norm_sum, scaled, grad_gate, out_kept, *sums_second = tied(
        norm_sum, scaled, grad_gate, out_kept, *sums_second
    )
    outward = out_kept + out_arrived
    columns_part = lax.psum_scatter(part, "head", scatter_dimension=0, tiled=True)[0]
    row_sums = [row_sum, *others(row_sum, "head", 1)]
    row_sum = sum(part[0] for part in row_sums)
    kept = weights_backward([middle_grad, normed], [scaled, grad_gate], True)
    sent, early = core_sum(kept, traded(early_sent, "seq", 1), norm_sum)
    sent, late_arrived = tied(sent, traded(late_sent, "seq", 2))
    late = late + late_arrived
    late, sent, norm_sum, taps_x, gain_sum, skip_sum, bias_sum, rate_sum, taps_bc = tied(
        late, sent, norm_sum, taps_x, gain_sum, skip_sum, bias_sum, rate_sum, taps_bc
    )
    local_first, whole_first = vectors_of(
        heads, taps_x, gain_sum, skip_sum, bias_sum, rate_sum, norm_sum, taps_bc
    )
    vector = jnp.stack(
        [
            jnp.concatenate([whole_first, local_first]),
            jnp.concatenate([whole_second, local_second]),
        ]
    )
    vector = butterfly(vector, "seq")
    first_share = norm_backward(
        columns_part, row_sum, own_columns(first), kept_first["rescale"],
        own_columns(middle_grad), own_columns(weights[0]["norm"]), model,
    )
    vector = section_sum(vector[0], vector[1], first_share)
    late = section_sum(late, late_second, first_share)
    early = section_sum(early + traded(sent, "seq", 2), early_second, first_share)
    whole = butterfly(vector[: whole_first.shape[0]], "head")
    local = vector[whole_first.shape[0] :]
    last_share = lax.rsqrt(sum(part[0] for part in sums_second) / INNER + epsilon)
    last_share = last_share[:, None] * outward[0].astype(f32)
    last_share = (own_columns(second).astype(f32) + last_share).astype(bf16)
    block_outputs = both_sequences(own_columns(second), last_share, first_share)
    grad_w_bc = late[:, :shared].astype(bf16).reshape(quarter, head_size, shared // head_size)
    grad_w_bc = grad_w_bc.swapaxes(0, 1)
    for bit in bits:
        grad_w_bc = halved(grad_w_bc, "head", bit)
    input_grads = both_sequences(first_share, own_columns(middle_grad))
    at = 0

    def taken(size):
        nonlocal at
        at += size
        return local[at - size : at]

    grad_norm = lax.dynamic_slice_in_dim(whole, head_at * share, share, 0)
    grad_conv_bc = whole[model:].reshape(CONV, shared).T
    grad_conv_x = taken(CONV * width).reshape(CONV, width).T
    grad_gain = taken(width)
    grad_skip = jnp.sum(taken(width).reshape(heads, width // heads), axis=1)
    grad_bias = taken(heads)
    grad_rate = taken(heads)
    return (
        block_outputs[None],
        input_grads[None],
        grad_norm[None],
        early[None, :, width:],
        late[None, :, shared + LANES :],
        grad_w_bc.astype(f32),
        late[None, :, shared : shared + heads],
        grad_conv_x[None],
        grad_conv_bc[None],
        grad_bias[None],
        grad_rate[None],
        grad_skip[None],
        grad_gain[None],
        early[None, :, :width],
    )


def solution(mesh):
    placed = (
        P(None, "seq", None),
        P(None, "seq", None),
        P("section", None),
        P("section", None, "head"),
        P("section", None, "head"),
        P("section", None, None),
        P("section", None, "head"),
        P("section", "head", None),
        P("section", None, None),
        P("section", "head"),
        P("section", "head"),
        P("section", "head"),
        P("section", "head"),
        P("section", None, "head"),
    )
    return jax.shard_map(
        shards,
        mesh=mesh,
        in_specs=placed,
        out_specs=(
            P("section", None, "seq", "head"),
            P("section", None, "seq", "head"),
            P("section", "head"),
            P("section", "seq", "head"),
            P("section", "seq", "head"),
            P("section", "seq", "head"),
            P("section", "seq", "head"),
            P("section", "head", None),
            P("section", None, None),
            P("section", "head"),
            P("section", "head"),
            P("section", "head"),
            P("section", "head"),
            P("section", "seq", "head"),
        ),
        check_vma=False,
    )
```

```python
from functools import partial

import jax
import jax.numpy as jnp
from jax import lax
from jax.experimental import pallas as pl
from jax.experimental.pallas import tpu as pltpu
from jax.sharding import PartitionSpec as P

INNER = 3072
CONV = 4
CHUNK = 128
LANES = 128
ROWS = 256

epsilon = 1e-05
exact = lax.Precision.HIGHEST
f32 = jnp.float32
bf16 = jnp.bfloat16


def dot_nn(left, right, precision=None):
    return lax.dot_general(
        left, right, (((1,), (0,)), ((), ())), precision=precision, preferred_element_type=f32
    )


def dot_nt(left, right, precision=None):
    return lax.dot_general(
        left, right, (((1,), (1,)), ((), ())), precision=precision, preferred_element_type=f32
    )


def dot_tn(left, right):
    return lax.dot_general(left, right, (((0,), (0,)), ((), ())), preferred_element_type=f32)


def three_parts(values):
    high = values.astype(bf16)
    rest = values - high.astype(f32)
    middle = rest.astype(bf16)
    return high, middle, (rest - middle.astype(f32)).astype(bf16)


def lane_sums(values):
    ones = jnp.ones((8, values.shape[1]), bf16)
    return sum(dot_nt(ones, part) for part in three_parts(values))


def times_mask(values, mask):
    rows = values.shape[0]
    product = dot_nn(jnp.concatenate(three_parts(values), axis=0), mask)
    return product[:rows] + product[rows : 2 * rows] + product[2 * rows :]


def mask_times(mask, values):
    columns = values.shape[1]
    product = dot_nn(mask, jnp.concatenate(three_parts(values), axis=1))
    return product[:, :columns] + product[:, columns : 2 * columns] + product[:, 2 * columns :]


def sigmoid(values):
    return 0.5 * jnp.tanh(0.5 * values) + 0.5


def silu_parts(values):
    gate = sigmoid(values)
    return gate, values * gate


def silu_slope(values, gate):
    return gate * (1.0 + values * (1.0 - gate))


def weight_fetch(block, sources, held, sem):
    here = lax.axis_index("section") == block
    away = jnp.logical_not(here)

    @pl.when(here)
    def _():
        pltpu.make_async_copy(sources[0], held, sem).start()

    place = lax.axis_index("seq")
    if len(sources) == 3:
        rows = sources[1].shape[1]
        for piece in range(4):
            target = held.at[piece * rows : (piece + 1) * rows]
            for k in range(2):

                @pl.when(away & (lax.rem(place + piece, 2) == k))
                def _():
                    pltpu.make_async_copy(sources[1 + k].at[piece // 2], target, sem).start()

        return
    rows = sources[1].shape[0]
    for piece in range(4):
        target = held.at[piece * rows : (piece + 1) * rows]
        for k, bits in enumerate((0, 2, 1, 3)):
            bit_low = lax.rem(place + piece, 2) == bits % 2
            bit_high = lax.rem(place // 2 + piece // 2, 2) == bits // 2

            @pl.when(away & bit_low & bit_high)
            def _():
                pltpu.make_async_copy(sources[1 + k], target, sem).start()


def weight_wait(sources, held, sem):
    pltpu.make_async_copy(sources[0], held, sem).wait()


def anywhere():
    return pl.BlockSpec(memory_space=pl.ANY)


def weight_scratch(own):
    return [pltpu.VMEM(own.shape, own.dtype), pltpu.SemaphoreType.DMA]


def head_groups(width, heads):
    head_width = width // heads
    per_group = max(LANES // head_width, 1)
    found = []
    for first in range(0, heads, per_group):
        count = min(per_group, heads - first)
        found.append((first, count, first * head_width, count * head_width))
    return found


def spread(tile, first, count, lanes):
    rows = tile.shape[0]
    head_width = lanes // count
    out = jnp.broadcast_to(tile[:, first : first + 1], (rows, lanes))
    lane = lax.broadcasted_iota(jnp.int32, (rows, lanes), 1)
    for k in range(1, count):
        column = jnp.broadcast_to(tile[:, first + k : first + k + 1], (rows, lanes))
        out = jnp.where(lane >= k * head_width, column, out)
    return out


def own_lanes(tile, k, count):
    if count == 1:
        return tile
    head_width = tile.shape[1] // count
    lane = lax.broadcasted_iota(jnp.int32, tile.shape, 1)
    inside = (lane >= k * head_width) & (lane < (k + 1) * head_width)
    return jnp.where(inside, tile, jnp.zeros_like(tile))


def triangle(keep):
    row = lax.broadcasted_iota(jnp.int32, (CHUNK, CHUNK), 0)
    column = lax.broadcasted_iota(jnp.int32, (CHUNK, CHUNK), 1)
    return keep(row, column)


def decay_of(payload, state):
    rows = payload[state : state + 16].astype(f32)
    return jnp.exp(rows[0:1] + rows[8:9] + rows[12:13])


def project_kernel(
    heads,
    block,
    sources,
    x_in,
    x_edge,
    gain,
    *refs,
):
    pack_sources, refs = refs[:sources], refs[sources:]
    (
        dt_bias, rate, taps_x, taps_bc, normed_out, rescale_out, raw_x, raw_bc,
        edge_x, edge_bc, step_raw, pre_x, pre_bc, act_x, act_bc, dt_out,
        run_out, payload, ext_x, ext_bc, end_out, total_out, pack, pack_sem,
    ) = refs
    step = pl.program_id(0)
    groups = head_groups(raw_x.shape[1], heads)
    shared = act_bc.shape[1]
    state = shared // 2

    def normed_of(block):
        x = block.astype(f32)
        rescale = lax.rsqrt(jnp.mean(x * x, axis=-1, keepdims=True) + epsilon)
        return rescale, (x * rescale * gain[...]).astype(bf16)

    @pl.when(step == 0)
    def _():
        weight_fetch(block, pack_sources, pack, pack_sem)
        _, edge = normed_of(x_edge[...])
        weight_wait(pack_sources, pack, pack_sem)
        edge_x[...] = dot_nn(edge, pack[:, shared + LANES :]).astype(bf16).astype(f32)[8:]
        edge_bc[...] = dot_nn(edge, pack[:, :shared]).astype(bf16).astype(f32)[8:]
        ext_x[0:8] = edge_x[...]
        ext_bc[0:8] = edge_bc[...]
        end_out[...] = jnp.zeros_like(end_out)
        total_out[...] = jnp.zeros_like(total_out)

    @pl.when(step > 0)
    def _():
        ext_x[0:8] = ext_x[ROWS : ROWS + 8]
        ext_bc[0:8] = ext_bc[ROWS : ROWS + 8]

    rescale, normed = normed_of(x_in[...])
    rescale_out[...] = rescale
    normed_out[...] = normed
    low = dot_nn(normed, pack[:, :shared]).astype(bf16)
    raw_bc[...] = low
    ext_bc[8:] = low.astype(f32)
    step_in = dot_nn(normed, pack[:, shared : shared + LANES])
    step_raw[...] = step_in
    sizes = jax.nn.softplus(step_in + dt_bias[...])
    dt_out[...] = sizes
    low = dot_nn(normed, pack[:, shared + LANES :]).astype(bf16)
    raw_x[...] = low
    ext_x[8:] = low.astype(f32)
    for ext, taps, pre, act in ((ext_bc, taps_bc, pre_bc, act_bc), (ext_x, taps_x, pre_x, act_x)):
        total = ext[5 : 5 + ROWS] * taps[0:1]
        for k in range(1, CONV):
            total = total + ext[5 + k : 5 + k + ROWS] * taps[k : k + 1]
        pre[...] = total.astype(bf16)
        act[...] = silu_parts(total)[1].astype(bf16)
    lower = triangle(lambda t, s: t >= s).astype(bf16)
    for sub in range(ROWS // CHUNK):
        at = slice(sub * CHUNK, (sub + 1) * CHUNK)
        dt = sizes[at]
        run = mask_times(lower, dt * rate[...])
        run_out[at] = run
        last = run[CHUNK - 1 : CHUNK]
        weight = jnp.exp(last - run) * dt
        decay = jnp.exp(last)
        b_turned = act_bc[at, :state].astype(f32).T.astype(bf16)
        for first, count, lane, lanes in groups:
            cols = slice(lane, lane + lanes)
            scaled = act_x[at, cols].astype(f32) * spread(weight, first, count, lanes)
            end_out[:, cols] = spread(decay, first, count, lanes) * end_out[:, cols] + dot_nn(
                b_turned, scaled.astype(bf16)
            )
        total_out[...] += jnp.broadcast_to(last, total_out.shape)

    @pl.when(step == pl.num_programs(0) - 1)
    def _():
        for first, count, lane, lanes in groups:
            cols = slice(lane, lane + lanes)
            payload[:state, cols] = end_out[:, cols].astype(bf16)
            total = spread(total_out[...], first, count, lanes)
            high = total.astype(bf16).astype(f32)
            middle = (total - high).astype(bf16).astype(f32)
            low = total - high - middle
            row = lax.broadcasted_iota(jnp.int32, (8, lanes), 0)
            rest = jnp.where(row < 4, middle, low)
            payload[state:, cols] = jnp.concatenate([high, rest], axis=0).astype(bf16)


def full(shape):
    return pl.BlockSpec(shape, lambda i: (0,) * len(shape))


def rows_of(width, back=0):
    if back:
        return pl.BlockSpec((ROWS, width), lambda i: (back - 1 - i, 0))
    return pl.BlockSpec((ROWS, width), lambda i: (i, 0))


def pieces_of(pieces, count, model):
    if pieces == 1:
        return rows_of(model), (count, model)
    lanes = model // pieces
    return pl.BlockSpec((pieces, ROWS, lanes), lambda i: (0, i, 0)), (pieces, count, lanes)


def params():
    return pltpu.CompilerParams(
        dimension_semantics=("arbitrary",), vmem_limit_bytes=60 * 1024 * 1024
    )


def project_forward(
    heads, block, x, x_edge, gain, pack, dt_bias, rate, taps_x, taps_bc
):
    count, model = x.shape
    width, shared = taps_x.shape[1], taps_bc.shape[1]
    state = shared // 2
    return pl.pallas_call(
        partial(project_kernel, heads, block, len(pack)),
        grid=(count // ROWS,),
        in_specs=[
            rows_of(model),
            full((16, model)),
            full((1, model)),
            *[anywhere() for _ in pack],
            full((1, LANES)),
            full((1, LANES)),
            full((CONV, width)),
            full((CONV, shared)),
        ],
        out_specs=[
            rows_of(model),
            rows_of(1),
            rows_of(width),
            rows_of(shared),
            full((8, width)),
            full((8, shared)),
            rows_of(LANES),
            rows_of(width),
            rows_of(shared),
            rows_of(width),
            rows_of(shared),
            rows_of(LANES),
            rows_of(LANES),
            full((state + 16, width)),
        ],
        out_shape=[
            jax.ShapeDtypeStruct((count, model), bf16),
            jax.ShapeDtypeStruct((count, 1), f32),
            jax.ShapeDtypeStruct((count, width), bf16),
            jax.ShapeDtypeStruct((count, shared), bf16),
            jax.ShapeDtypeStruct((8, width), f32),
            jax.ShapeDtypeStruct((8, shared), f32),
            jax.ShapeDtypeStruct((count, LANES), f32),
            jax.ShapeDtypeStruct((count, width), bf16),
            jax.ShapeDtypeStruct((count, shared), bf16),
            jax.ShapeDtypeStruct((count, width), bf16),
            jax.ShapeDtypeStruct((count, shared), bf16),
            jax.ShapeDtypeStruct((count, LANES), f32),
            jax.ShapeDtypeStruct((count, LANES), f32),
            jax.ShapeDtypeStruct((state + 16, width), bf16),
        ],
        scratch_shapes=[
            pltpu.VMEM((8 + ROWS, width), f32),
            pltpu.VMEM((8 + ROWS, shared), f32),
            pltpu.VMEM((state, width), f32),
            pltpu.VMEM((8, LANES), f32),
            *weight_scratch(pack[0]),
        ],
        compiler_params=params(),
        cost_estimate=pl.CostEstimate(
            flops=2 * count * model * pack[0].shape[1],
            bytes_accessed=2 * pack[0].size + count * (4 * model + 6 * (width + shared)),
            transcendentals=count * (width + shared),
        ),
        name="project_forward",
    )(x, x_edge, gain, *pack, dt_bias, rate, taps_x, taps_bc)


def inner_kernel(
    heads, block, act_x, act_bc, dt_in, run_in, normed, *refs
):
    *z_sources, gate_out, inner_out, w_z, z_sem = refs

    @pl.when(pl.program_id(0) == 0)
    def _():
        weight_fetch(block, z_sources, w_z, z_sem)
        weight_wait(z_sources, w_z, z_sem)

    groups = head_groups(act_x.shape[1], heads)
    state = act_bc.shape[1] // 2
    gate_out[...] = dot_nn(normed[...], w_z[...])
    causal = triangle(lambda t, s: t >= s)
    for sub in range(ROWS // CHUNK):
        at = slice(sub * CHUNK, (sub + 1) * CHUNK)
        dt = dt_in[at]
        run = run_in[at]
        turned = run.T
        product = dot_nt(act_bc[at, state:], act_bc[at, :state])
        for first, count, lane, lanes in groups:
            cols = slice(lane, lane + lanes)
            stepped = act_x[at, cols].astype(f32) * spread(dt, first, count, lanes)
            low = stepped.astype(bf16)
            weights = []
            stacked = []
            for k in range(count):
                h = first + k
                gap = jnp.broadcast_to(run[:, h : h + 1], (CHUNK, CHUNK)) - turned[h : h + 1]
                factor = jnp.exp(jnp.where(causal, gap, -jnp.inf))
                weights.append((product * factor).astype(bf16))
                stacked.append(own_lanes(low, k, count))
            inner_out[at, cols] = dot_nn(
                jnp.concatenate(weights, axis=1), jnp.concatenate(stacked, axis=0)
            )


def inner_forward(heads, block, act_x, act_bc, dt, run, normed, w_z):
    count, width = act_x.shape
    model = normed.shape[1]
    shared = act_bc.shape[1]
    return pl.pallas_call(
        partial(inner_kernel, heads, block),
        grid=(count // ROWS,),
        in_specs=[
            rows_of(width),
            rows_of(shared),
            rows_of(LANES),
            rows_of(LANES),
            rows_of(model),
            *[anywhere() for _ in w_z],
        ],
        out_specs=[rows_of(width), rows_of(width)],
        out_shape=[
            jax.ShapeDtypeStruct((count, width), f32),
            jax.ShapeDtypeStruct((count, width), f32),
        ],
        scratch_shapes=weight_scratch(w_z[0]),
        compiler_params=params(),
        cost_estimate=pl.CostEstimate(
            flops=2 * count * width * (4 * CHUNK + model),
            bytes_accessed=count * (10 * width + 2 * model) + 2 * w_z[0].size,
            transcendentals=count * heads * CHUNK,
        ),
        name="inner_forward",
    )(act_x, act_bc, dt, run, normed, *w_z)


def outer_kernel(
    heads,
    block,
    sources,
    pieces,
    shards,
    act_x,
    act_bc,
    dt_in,
    run_in,
    gate_in,
    inner_in,
    *refs,
):
    out_sources, refs = refs[:sources], refs[sources:]
    skip, gain, *refs = refs
    arrived, refs = refs[: shards - 1], refs[shards - 1 :]
    grad_in, refs = (refs[0], refs[1:]) if len(refs) == 9 else (None, refs)
    mixed_out, scaled_out, part_out, sums_out, states_out, held, w_out, out_sem = refs
    groups = head_groups(act_x.shape[1], heads)
    state = act_bc.shape[1] // 2

    @pl.when(pl.program_id(0) == 0)
    def _():
        weight_fetch(block, out_sources, w_out, out_sem)
        place = lax.axis_index("seq")
        held[...] = jnp.zeros_like(held)
        for distance in reversed(range(1, shards)):

            @pl.when(place >= distance)
            def _():
                payload = arrived[distance - 1]
                held[...] = decay_of(payload, state) * held[...] + payload[:state].astype(f32)

    square_rows = []
    ones = jnp.ones((8, LANES), f32)
    for sub in range(ROWS // CHUNK):
        at = slice(sub * CHUNK, (sub + 1) * CHUNK)
        run = run_in[at]
        last = run[CHUNK - 1 : CHUNK]
        weight = jnp.exp(last - run) * dt_in[at]
        decay = jnp.exp(last)
        grown = jnp.exp(run)
        c_part = act_bc[at, state:]
        b_turned = act_bc[at, :state].astype(f32).T.astype(bf16)
        states_out[sub] = held[...].astype(bf16)
        squares = jnp.zeros((CHUNK, LANES), f32)
        for first, count, lane, lanes in groups:
            cols = slice(lane, lane + lanes)
            x_part = act_x[at, cols].astype(f32)
            before = held[:, cols]
            mixed = inner_in[at, cols] + spread(grown, first, count, lanes) * dot_nn(
                c_part, before.astype(bf16)
            )
            mixed = mixed + skip[:, cols] * x_part
            held[:, cols] = spread(decay, first, count, lanes) * before + dot_nn(
                b_turned, (x_part * spread(weight, first, count, lanes)).astype(bf16)
            )
            gated = mixed * silu_parts(gate_in[at, cols])[1]
            mixed_out[at, cols] = mixed.astype(bf16)
            scaled_out[at, cols] = (gated * gain[:, cols]).astype(bf16)
            square = gated * gated
            if lanes < LANES:
                fill = jnp.zeros((CHUNK, LANES - lanes), f32)
                square = jnp.concatenate([square, fill], axis=1)
            squares = squares + square
        square_rows.append(lane_sums(squares))

    @pl.when(pl.program_id(0) == 0)
    def _():
        weight_wait(out_sources, w_out, out_sem)

    part = dot_nt(scaled_out[...], w_out[...])
    if pieces == 1:
        part_out[...] = part.astype(bf16)
    else:
        wide = part.shape[1] // pieces
        for k in range(pieces):
            part_out[k] = part[:, k * wide : (k + 1) * wide].astype(bf16)
    row = lax.broadcasted_iota(jnp.int32, (8, CHUNK), 0)
    for sub in range(ROWS // CHUNK):
        at = slice(sub * CHUNK, (sub + 1) * CHUNK)
        pair_row = jnp.zeros((8, CHUNK), f32)
        if grad_in is not None:
            pairs = jnp.zeros((CHUNK, LANES), f32)
            for lane in range(0, part.shape[1], LANES):
                cols = slice(lane, lane + LANES)
                pairs = pairs + part[at, cols] * grad_in[at, cols].astype(f32)
            pair_row = lane_sums(pairs)
        sums_out[:, at] = jnp.where(row == 0, square_rows[sub], pair_row)


def outer_forward(
    heads, block, pieces, act_x, act_bc, dt, run, gate_in, inner, w_out, skip, gain, arrived, grad_in
):
    count, width = act_x.shape
    model = w_out[0].shape[0]
    part_spec, part_shape = pieces_of(pieces, count, model)
    shared = act_bc.shape[1]
    state = shared // 2
    subs = ROWS // CHUNK
    extra, extra_specs = [], []
    if grad_in is not None:
        extra, extra_specs = [grad_in], [rows_of(model)]
    return pl.pallas_call(
        partial(outer_kernel, heads, block, len(w_out), pieces, len(arrived) + 1),
        grid=(count // ROWS,),
        in_specs=[
            rows_of(width),
            rows_of(shared),
            rows_of(LANES),
            rows_of(LANES),
            rows_of(width),
            rows_of(width),
            *[anywhere() for _ in w_out],
            full((1, width)),
            full((1, width)),
            *[full(payload.shape) for payload in arrived],
            *extra_specs,
        ],
        out_specs=[
            rows_of(width),
            rows_of(width),
            part_spec,
            pl.BlockSpec((8, ROWS), lambda i: (0, i)),
            pl.BlockSpec((subs, state, width), lambda i: (i, 0, 0)),
        ],
        out_shape=[
            jax.ShapeDtypeStruct((count, width), bf16),
            jax.ShapeDtypeStruct((count, width), bf16),
            jax.ShapeDtypeStruct(part_shape, bf16),
            jax.ShapeDtypeStruct((8, count), f32),
            jax.ShapeDtypeStruct((count // CHUNK, state, width), bf16),
        ],
        scratch_shapes=[pltpu.VMEM((state, width), f32), *weight_scratch(w_out[0])],
        compiler_params=params(),
        cost_estimate=pl.CostEstimate(
            flops=2 * count * width * (2 * state + model),
            bytes_accessed=count * width * 18,
            transcendentals=count * width,
        ),
        name="outer_forward",
    )(
        act_x, act_bc, dt, run, gate_in, inner, *w_out, skip, gain, *arrived, *extra
    )


def gate_kernel(
    heads,
    block,
    sources,
    addends,
    between,
    grad,
    gate_in,
    mixed_in,
    scaled_in,
    act_x,
    act_bc,
    run_in,
    gain,
    *refs,
):
    out_sources, refs = refs[:sources], refs[sources:]
    sums, refs = refs[:addends], refs[addends:]
    later, earlier = refs[:2] if between else (None, None)
    refs = refs[2:] if between else refs
    grad_mixed, grad_gate, scaled_out, gain_sum, skip_sum, adjoint_out, *refs = refs
    grad_in, adjoint, scales, w_out, out_sem = refs
    step = pl.program_id(0)
    groups = head_groups(act_x.shape[1], heads)
    state = act_bc.shape[1] // 2

    @pl.when(step == 0)
    def _():
        weight_fetch(block, out_sources, w_out, out_sem)
        gain_sum[...] = jnp.zeros_like(gain_sum)
        skip_sum[...] = jnp.zeros_like(skip_sum)
        adjoint[...] = jnp.zeros_like(adjoint)
        scales[...] = jnp.zeros_like(scales)
        weight_wait(out_sources, w_out, out_sem)

    grad_in[...] = dot_nn(grad[...], w_out[...])
    total = sums[0][...]
    for more in sums[1:]:
        total = total + more[...]
    scale_row = lax.rsqrt(total[0:1] / INNER + epsilon)
    pull_row = total[1:2] * scale_row * scale_row * scale_row / INNER
    for sub in reversed(range(ROWS // CHUNK)):
        at = slice(sub * CHUNK, (sub + 1) * CHUNK)
        run = run_in[at]
        grown = jnp.exp(run)
        decay = grown[CHUNK - 1 : CHUNK]
        c_turned = act_bc[at, state:].astype(f32).T.astype(bf16)
        scales[0:1] = scale_row[:, at]
        scales[1:2] = pull_row[:, at]
        columns = scales[...].T
        row_scale = columns[:, 0:1]
        row_pull = columns[:, 1:2]
        if later is not None:
            moved = later[at].astype(f32) - earlier[at].astype(f32)
            pulled = jnp.sum(grad[at].astype(f32) * moved, axis=1, keepdims=True)
            row_pull = pulled * row_scale * row_scale * (1.0 / INNER)
        for first, count, lane, lanes in groups:
            cols = slice(lane, lane + lanes)
            gate = gate_in[at, cols]
            mixed = mixed_in[at, cols].astype(f32)
            share, active = silu_parts(gate)
            gated = mixed * active
            d_scaled = grad_in[at, cols] * row_scale
            d_gated = d_scaled * gain[:, cols] - row_pull * gated
            d_mixed = d_gated * active
            grad_mixed[at, cols] = d_mixed.astype(bf16)
            grad_gate[at, cols] = (d_gated * mixed * silu_slope(gate, share)).astype(bf16)
            scaled_out[at, cols] = (scaled_in[at, cols].astype(f32) * row_scale).astype(bf16)
            gain_sum[0:1, cols] += jnp.sum(d_scaled * gated, axis=0, keepdims=True)
            skip_sum[0:1, cols] += jnp.sum(
                d_mixed * act_x[at, cols].astype(f32), axis=0, keepdims=True
            )
            adjoint[:, cols] = spread(decay, first, count, lanes) * adjoint[:, cols] + dot_nn(
                c_turned, (d_mixed * spread(grown, first, count, lanes)).astype(bf16)
            )

    @pl.when(step == pl.num_programs(0) - 1)
    def _():
        adjoint_out[...] = adjoint[...].astype(bf16)


def gate_backward(
    heads, block, grad, w_out, gate_in, mixed, scaled, act_x, act_bc, run, gain, sums, ends
):
    count, width = act_x.shape
    model = grad.shape[1]
    shared = act_bc.shape[1]
    state = shared // 2
    steps = count // ROWS
    return pl.pallas_call(
        partial(gate_kernel, heads, block, len(w_out), len(sums), len(ends) > 0),
        grid=(steps,),
        in_specs=[
            rows_of(model, steps),
            rows_of(width, steps),
            rows_of(width, steps),
            rows_of(width, steps),
            rows_of(width, steps),
            rows_of(shared, steps),
            rows_of(LANES, steps),
            full((1, width)),
            *[anywhere() for _ in w_out],
            *[pl.BlockSpec((8, ROWS), lambda i: (0, steps - 1 - i)) for _ in sums],
            *[rows_of(model, steps) for _ in ends],
        ],
        out_specs=[
            rows_of(width, steps),
            rows_of(width, steps),
            rows_of(width, steps),
            full((8, width)),
            full((8, width)),
            full((state, width)),
        ],
        out_shape=[
            jax.ShapeDtypeStruct((count, width), bf16),
            jax.ShapeDtypeStruct((count, width), bf16),
            jax.ShapeDtypeStruct((count, width), bf16),
            jax.ShapeDtypeStruct((8, width), f32),
            jax.ShapeDtypeStruct((8, width), f32),
            jax.ShapeDtypeStruct((state, width), bf16),
        ],
        scratch_shapes=[
            pltpu.VMEM((ROWS, width), f32),
            pltpu.VMEM((state, width), f32),
            pltpu.VMEM((CHUNK, CHUNK), f32),
            *weight_scratch(w_out[0]),
        ],
        compiler_params=params(),
        cost_estimate=pl.CostEstimate(
            flops=2 * count * width * (state + model),
            bytes_accessed=count * width * 16,
            transcendentals=count * width,
        ),
        name="gate_backward",
    )(
        grad, gate_in, mixed, scaled, act_x, act_bc, run, gain, *w_out, *sums, *ends
    )


def states_kernel(
    heads,
    shards,
    grad_mixed,
    act_x,
    act_bc,
    pre_x,
    pre_bc,
    raw_x,
    raw_bc,
    edge_x,
    edge_bc,
    dt_in,
    run_in,
    step_raw,
    dt_bias,
    rate_rows,
    states_in,
    skip,
    taps_x,
    taps_bc,
    members,
    *refs,
):
    arrived, payloads, refs = refs[: shards - 1], refs[shards - 1 : 2 * shards - 2], refs[2 * shards - 2 :]
    packed, tail, back, tap_sum_x, tap_sum_bc, rate_sum, bias_sum, *refs = refs
    adjoint, d_pre_x, d_pre_bc, rows_ref, carry_ref, square_ref = refs
    step = pl.program_id(0)
    steps = pl.num_programs(0)
    groups = head_groups(act_x.shape[1], heads)
    shared = act_bc.shape[1]
    state = shared // 2
    padded = members.shape[0]

    @pl.when(step == 0)
    def _():
        place = lax.axis_index("seq")
        adjoint[...] = jnp.zeros_like(adjoint)
        for distance in reversed(range(1, shards)):

            @pl.when(place + distance < shards)
            def _():
                decay = decay_of(payloads[shards - 1 - distance], state)
                adjoint[...] = decay * adjoint[...] + arrived[distance - 1][...].astype(f32)

        d_pre_x[8:16] = jnp.zeros((8, d_pre_x.shape[1]), f32)
        d_pre_bc[8:16] = jnp.zeros((8, d_pre_bc.shape[1]), f32)
        tap_sum_x[...] = jnp.zeros_like(tap_sum_x)
        tap_sum_bc[...] = jnp.zeros_like(tap_sum_bc)
        rate_sum[...] = jnp.zeros_like(rate_sum)
        bias_sum[...] = jnp.zeros_like(bias_sum)
        rows_ref[...] = jnp.zeros_like(rows_ref)
        square_ref[...] = jnp.zeros_like(square_ref)

    upto = triangle(lambda s, t: s <= t)
    not_before = triangle(lambda s, t: s >= t).astype(bf16)
    before = triangle(lambda s, t: s < t).astype(bf16)
    head_lane = lax.broadcasted_iota(jnp.int32, (CHUNK, LANES), 1)
    for sub in reversed(range(ROWS // CHUNK)):
        at = slice(sub * CHUNK, (sub + 1) * CHUNK)
        dt = dt_in[at]
        run = run_in[at]
        last = run[CHUNK - 1 : CHUNK]
        grown = jnp.exp(run)
        decay = grown[CHUNK - 1 : CHUNK]
        to_end = jnp.exp(last - run)
        run_turned = run.T
        dt_turned = dt.T[0:padded]
        inside_tile = jnp.zeros((CHUNK, LANES), f32)
        b_part = act_bc[at, :state]
        c_part = act_bc[at, state:]
        c_turned = c_part.astype(f32).T.astype(bf16)
        product = dot_nt(b_part, c_part)
        d_product = jnp.zeros((CHUNK, CHUNK), f32)
        d_b = jnp.zeros((CHUNK, state), f32)
        d_c = jnp.zeros((CHUNK, state), f32)
        d_pre_x[CHUNK + 8 : CHUNK + 16] = d_pre_x[8:16]
        d_pre_bc[CHUNK + 8 : CHUNK + 16] = d_pre_bc[8:16]
        through = []
        for first, count, lane, lanes in groups:
            cols = slice(lane, lane + lanes)
            x_low = act_x[at, cols]
            x_part = x_low.astype(f32)
            dy_low = grad_mixed[at, cols]
            dy = dy_low.astype(f32)
            dt_wide = spread(dt, first, count, lanes)
            ending = spread(to_end, first, count, lanes)
            growing = spread(grown, first, count, lanes)
            lam = adjoint[:, cols]
            lam_low = lam.astype(bf16)
            held_low = states_in[sub][:, cols]
            weights = []
            stacked = []
            for k in range(count):
                h = first + k
                gap = run_turned[h : h + 1] - jnp.broadcast_to(run[:, h : h + 1], (CHUNK, CHUNK))
                factor = jnp.exp(jnp.where(upto, gap, -jnp.inf))
                weights.append((product * factor).astype(bf16))
                stacked.append(own_lanes(dy_low, k, count))
                paired = dot_nt(own_lanes(x_low, k, count), dy_low) * factor
                dt_column = jnp.broadcast_to(dt[:, h : h + 1], (CHUNK, CHUNK))
                d_product = d_product + paired * dt_column
                inside = paired * product
                rows_ref[h : h + 1] = jnp.sum(inside * dt_column, axis=0, keepdims=True)
                inside_tile = jnp.where(
                    head_lane == h, jnp.sum(inside, axis=1, keepdims=True), inside_tile
                )
            d_stepped = dot_nn(jnp.concatenate(weights, axis=1), jnp.concatenate(stacked, axis=0))
            from_end = ending * dot_nn(b_part, lam_low)
            d_x = dt_wide * (d_stepped + from_end) + skip[:, cols] * dy
            dy_grown = dy * growing
            dy_grown_low = dy_grown.astype(bf16)
            carry_ref[0, :, cols] = (x_part * from_end).astype(bf16)
            carry_ref[1, :, cols] = (dy_grown * dot_nn(c_part, held_low)).astype(bf16)
            d_b = d_b + dot_nt((x_part * dt_wide * ending).astype(bf16), lam_low)
            d_c = d_c + dot_nt(dy_grown_low, held_low)
            wide_decay = spread(decay, first, count, lanes)
            lam_decayed = wide_decay * lam
            through.append(
                jnp.sum(lam_decayed * held_low.astype(f32), axis=0, keepdims=True)
            )
            adjoint[:, cols] = lam_decayed + dot_nn(c_turned, dy_grown_low)
            pre = pre_x[at, cols].astype(f32)
            d_pre_x[8 : CHUNK + 8, cols] = d_x * silu_slope(pre, sigmoid(pre))
        member = members[...]
        kept = dot_nt(member, carry_ref[0])
        fed = dot_nt(member, carry_ref[1])
        wide_row = jnp.concatenate(through, axis=1)
        across = jnp.sum(member.astype(f32) * wide_row, axis=1, keepdims=True)
        inside_rows = inside_tile.T[0:padded]
        d_log = (
            times_mask(rows_ref[...] - dt_turned * inside_rows + fed, not_before)
            + times_mask(dt_turned * kept, before)
            + across
        )
        d_log_rate = d_log * rate_rows[...]
        rate_sum[...] += d_log_rate * dt_turned
        square_ref[0:padded] = d_log_rate + inside_rows + kept
        d_step_exact = square_ref[...].T * sigmoid(step_raw[at] + dt_bias[...])
        bias_sum[0:1] += jnp.sum(d_step_exact, axis=0, keepdims=True)
        packed[at, shared : shared + LANES] = d_step_exact.astype(bf16)
        if sub == ROWS // CHUNK - 1:

            @pl.when(step == 0)
            def _():
                tail[:, shared : shared + LANES] = d_step_exact[CHUNK - 16 :]

        d_product_low = d_product.astype(bf16)
        d_b = d_b + dot_nn(d_product_low, c_part)
        d_c = d_c + dot_nn(d_product.T.astype(bf16), b_part)
        pre = pre_bc[at].astype(f32)
        slope = silu_slope(pre, sigmoid(pre))
        d_pre_bc[8 : CHUNK + 8, :state] = d_b * slope[:, :state]
        d_pre_bc[8 : CHUNK + 8, state:] = d_c * slope[:, state:]
        for d_pre, raw, taps, place, tap_sum in (
            (d_pre_x, raw_x, taps_x, slice(shared + LANES, None), tap_sum_x),
            (d_pre_bc, raw_bc, taps_bc, slice(0, shared), tap_sum_bc),
        ):
            values = raw[at].astype(f32)
            total = jnp.zeros_like(values)
            for k in range(CONV):
                moved = d_pre[11 - k : 11 - k + CHUNK]
                total = total + moved * taps[k : k + 1]
                tap_sum[k : k + 1] += jnp.sum(values * moved, axis=0, keepdims=True)
            packed[at, place] = total.astype(bf16)
            if sub == ROWS // CHUNK - 1:

                @pl.when(step == 0)
                def _():
                    tail[:, place] = total[CHUNK - 16 :]

    @pl.when(step == steps - 1)
    def _():
        back[...] = jnp.zeros_like(back)
        for d_pre, edge, taps, tap_sum, place in (
            (d_pre_x, edge_x, taps_x, tap_sum_x, slice(shared + LANES, None)),
            (d_pre_bc, edge_bc, taps_bc, tap_sum_bc, slice(0, shared)),
        ):
            d_pre[0:8] = jnp.zeros((8, d_pre.shape[1]), f32)
            values = edge[...]
            total = jnp.zeros_like(values)
            for k in range(CONV):
                moved = d_pre[3 - k : 11 - k]
                total = total + moved * taps[k : k + 1]
                tap_sum[k : k + 1] += jnp.sum(values * moved, axis=0, keepdims=True)
            back[8:, place] = total


def states_backward(
    heads,
    grad_mixed,
    act_x,
    act_bc,
    pre_x,
    pre_bc,
    raw_x,
    raw_bc,
    edge_x,
    edge_bc,
    dt,
    run,
    step_raw,
    dt_bias,
    rate,
    states,
    skip,
    taps_x,
    taps_bc,
    arrived,
    payloads,
):
    count, width = act_x.shape
    shared = act_bc.shape[1]
    state = shared // 2
    steps = count // ROWS
    subs = ROWS // CHUNK
    padded = -(-heads // 16) * 16
    head_of = jnp.arange(width)[None, :] // (width // heads)
    members = (jnp.arange(padded)[:, None] == head_of).astype(bf16)
    rate_rows = jnp.broadcast_to(rate[0, :padded, None], (padded, CHUNK))
    return pl.pallas_call(
        partial(states_kernel, heads, len(arrived) + 1),
        grid=(steps,),
        in_specs=[
            rows_of(width, steps),
            rows_of(width, steps),
            rows_of(shared, steps),
            rows_of(width, steps),
            rows_of(shared, steps),
            rows_of(width, steps),
            rows_of(shared, steps),
            full((8, width)),
            full((8, shared)),
            rows_of(LANES, steps),
            rows_of(LANES, steps),
            rows_of(LANES, steps),
            full((1, LANES)),
            full((padded, CHUNK)),
            pl.BlockSpec((subs, state, width), lambda i: (steps - 1 - i, 0, 0)),
            full((1, width)),
            full((CONV, width)),
            full((CONV, shared)),
            full((padded, width)),
            *[full(array.shape) for array in (*arrived, *payloads)],
        ],
        out_specs=[
            rows_of(shared + LANES + width, steps),
            full((16, shared + LANES + width)),
            full((16, shared + LANES + width)),
            full((8, width)),
            full((8, shared)),
            full((padded, CHUNK)),
            full((8, LANES)),
        ],
        out_shape=[
            jax.ShapeDtypeStruct((count, shared + LANES + width), bf16),
            jax.ShapeDtypeStruct((16, shared + LANES + width), f32),
            jax.ShapeDtypeStruct((16, shared + LANES + width), f32),
            jax.ShapeDtypeStruct((8, width), f32),
            jax.ShapeDtypeStruct((8, shared), f32),
            jax.ShapeDtypeStruct((padded, CHUNK), f32),
            jax.ShapeDtypeStruct((8, LANES), f32),
        ],
        scratch_shapes=[
            pltpu.VMEM((state, width), f32),
            pltpu.VMEM((CHUNK + 16, width), f32),
            pltpu.VMEM((CHUNK + 16, shared), f32),
            pltpu.VMEM((padded, CHUNK), f32),
            pltpu.VMEM((2, CHUNK, width), bf16),
            pltpu.VMEM((CHUNK, CHUNK), f32),
        ],
        compiler_params=params(),
        cost_estimate=pl.CostEstimate(
            flops=20 * count * width * state,
            bytes_accessed=count * width * 16,
            transcendentals=count * heads * CHUNK * 2,
        ),
        name="states_backward",
    )(
        grad_mixed,
        act_x,
        act_bc,
        pre_x,
        pre_bc,
        raw_x,
        raw_bc,
        edge_x,
        edge_bc,
        dt,
        run,
        step_raw,
        dt_bias,
        rate_rows,
        states,
        skip,
        taps_x,
        taps_bc,
        members,
        *arrived,
        *payloads,
    )


def part_kernel(
    pieces,
    block,
    sources,
    grad_gate,
    packed,
    x_in,
    gain,
    *refs,
):
    z_sources, refs = refs[:sources], refs[sources:]
    *pack_sources, part_out, row_sum, norm_sum, part_ref, w_z, z_sem, pack, pack_sem = refs

    @pl.when(pl.program_id(0) == 0)
    def _():
        weight_fetch(block, z_sources, w_z, z_sem)
        weight_fetch(block, pack_sources, pack, pack_sem)
        weight_wait(z_sources, w_z, z_sem)
        weight_wait(pack_sources, pack, pack_sem)
        norm_sum[...] = jnp.zeros_like(norm_sum)

    x = x_in[...].astype(f32)
    rescale = lax.rsqrt(jnp.mean(x * x, axis=-1, keepdims=True) + epsilon)
    part_ref[...] = dot_nt(grad_gate[...], w_z[...]) + dot_nt(packed[...], pack[...])
    total = jnp.zeros((ROWS, LANES), f32)
    for lane in range(0, x.shape[1], LANES):
        cols = slice(lane, lane + LANES)
        pulled = part_ref[:, cols] * (x_in[:, cols].astype(f32) * rescale)
        norm_sum[0:1, cols] += jnp.sum(pulled, axis=0, keepdims=True)
        total = total + pulled * gain[:, cols]
    row_sum[...] = lane_sums(total)
    if pieces == 1:
        part_out[...] = part_ref[...].astype(bf16)
    else:
        lanes = x.shape[1] // pieces
        for k in range(pieces):
            part_out[k] = part_ref[:, k * lanes : (k + 1) * lanes].astype(bf16)


def part_backward(
    pieces, block, grad_gate, packed, w_z, pack, x, gain
):
    count, width = grad_gate.shape
    model = x.shape[1]
    part_spec, part_shape = pieces_of(pieces, count, model)
    return pl.pallas_call(
        partial(part_kernel, pieces, block, len(w_z)),
        grid=(count // ROWS,),
        in_specs=[
            rows_of(width),
            rows_of(packed.shape[1]),
            rows_of(model),
            full((1, model)),
            *[anywhere() for _ in (*w_z, *pack)],
        ],
        out_specs=[part_spec, pl.BlockSpec((8, ROWS), lambda i: (0, i)), full((8, model))],
        out_shape=[
            jax.ShapeDtypeStruct(part_shape, bf16),
            jax.ShapeDtypeStruct((8, count), f32),
            jax.ShapeDtypeStruct((8, model), f32),
        ],
        scratch_shapes=[
            pltpu.VMEM((ROWS, model), f32),
            *weight_scratch(w_z[0]),
            *weight_scratch(pack[0]),
        ],
        compiler_params=params(),
        cost_estimate=pl.CostEstimate(
            flops=2 * count * model * (width + packed.shape[1]),
            bytes_accessed=2 * (w_z[0].size + pack[0].size) + 8 * count * model,
            transcendentals=0,
        ),
        name="part_backward",
    )(grad_gate, packed, x, gain, *w_z, *pack)


def weights_kernel(count, low, *refs):
    lefts, rights, out = refs[:count], refs[count : 2 * count], refs[2 * count]
    lane = 0
    for left, right in zip(lefts, rights):
        lanes = right.shape[1]
        out[0, :, lane : lane + lanes] = dot_tn(left[...], right[...]).astype(bf16)
        lane += lanes


def weights_backward(lefts, rights, kept):
    count, model = lefts[0].shape
    rows = model // 4
    lanes = sum(right.shape[1] for right in rights)
    low = lax.rem(lax.axis_index("seq"), 2)
    low = (low if kept else 1 - low).astype(jnp.int32).reshape(1)
    return pl.pallas_call(
        partial(weights_kernel, len(lefts)),
        grid_spec=pltpu.PrefetchScalarGridSpec(
            num_scalar_prefetch=1,
            grid=(2,),
            in_specs=[
                *[pl.BlockSpec((count, rows), lambda i, low: (0, 2 * i + low[0])) for _ in lefts],
                *[pl.BlockSpec(right.shape, lambda i, low: (0, 0)) for right in rights],
            ],
            out_specs=pl.BlockSpec((1, rows, lanes), lambda i, low: (i, 0, 0)),
        ),
        out_shape=jax.ShapeDtypeStruct((2, rows, lanes), bf16),
        compiler_params=params(),
        cost_estimate=pl.CostEstimate(
            flops=count * model * lanes,
            bytes_accessed=2 * (len(lefts) * count * model + count * lanes + model * lanes),
            transcendentals=0,
        ),
        name="weights_backward",
    )(low, *lefts, *rights)


def traded(block, axis, bit):
    return lax.ppermute(block, axis, [(i, i ^ bit) for i in range(lax.axis_size(axis))])


def rotated(block, axis, distance):
    size = lax.axis_size(axis)
    return lax.ppermute(block, axis, [(i, (i + distance) % size) for i in range(size)])


def others(block, axis, sign):
    return [rotated(block, axis, sign * d) for d in range(1, lax.axis_size(axis))]


def bits_of(axis):
    bit = 1
    while bit < lax.axis_size(axis):
        yield bit
        bit *= 2


def butterfly(block, axis):
    for bit in bits_of(axis):
        block = block + traded(block, axis, bit)
    return block


def parted(pieces, axis, bit):
    pairs = pieces.reshape((pieces.shape[0] // 2, 2) + pieces.shape[1:])
    mine = lax.rem(lax.axis_index(axis) // bit, 2)
    return (
        lax.dynamic_index_in_dim(pairs, mine, 1, False),
        lax.dynamic_index_in_dim(pairs, 1 - mine, 1, False),
    )


def halved(pieces, axis, bit):
    kept, sent = parted(pieces, axis, bit)
    return kept + traded(sent, axis, bit)


def core_sum(kept, arrived, earlier):
    high = lax.axis_index("seq") // 2

    def summed(at):
        own = lax.dynamic_index_in_dim(kept, at, 0, False)
        both = own + lax.dynamic_index_in_dim(arrived, at, 0, False)
        return both if earlier is None else after(both, earlier)

    return summed(1 - high), summed(high)


def after(value, earlier):
    return value + (0.0 * earlier.reshape(-1)[0].astype(f32)).astype(value.dtype)


def moved_along(block, axis, distance):
    size, place = lax.axis_size(axis), lax.axis_index(axis)
    arrived = rotated(block, axis, distance)
    outside = (place < distance) | (place >= size + distance)
    return jnp.where(outside, jnp.zeros_like(arrived), arrived)


def tied(*values):
    return lax.optimization_barrier(values)


def block_forward(
    block, x, x_edge, weights, grad, pieces, mixed_inside=lambda inner, payloads: (inner, payloads)
):
    heads = weights["heads"]
    (
        normed, rescale, raw_x, raw_bc, edge_x, edge_bc, step_raw, pre_x, pre_bc, act_x, act_bc,
        dt, run, payload,
    ) = project_forward(
        heads, block, x, x_edge, weights["norm"], weights["pack"], weights["dt_bias"],
        weights["rate"], weights["taps_x"], weights["taps_bc"],
    )
    payloads = others(payload, "seq", 1)
    gate_in, inner = inner_forward(
        heads, block, act_x, act_bc, dt, run, normed, weights["w_z"]
    )
    inner, payloads = mixed_inside(inner, payloads)
    mixed, scaled, part, sums, states = outer_forward(
        heads, block, pieces, act_x, act_bc, dt, run, gate_in, inner, weights["w_out"],
        weights["skip"], weights["gain"], payloads, grad,
    )
    kept = dict(
        raw_x=raw_x, raw_bc=raw_bc, step_raw=step_raw, edge_x=edge_x, edge_bc=edge_bc,
        gate_in=gate_in, pre_x=pre_x, pre_bc=pre_bc, act_x=act_x, act_bc=act_bc, dt=dt, run=run,
        payloads=payloads, mixed=mixed, scaled=scaled, states=states, normed=normed,
        rescale=rescale,
    )
    return part, sums, kept


def gate_step(block, grad, sums, ends, kept, weights):
    return gate_backward(
        weights["heads"], block, grad, weights["w_out"], kept["gate_in"], kept["mixed"],
        kept["scaled"], kept["act_x"], kept["act_bc"], kept["run"], weights["gain"], sums, ends,
    )


def states_step(grad_mixed, arrived, kept, weights):
    return states_backward(
        weights["heads"], grad_mixed, kept["act_x"], kept["act_bc"], kept["pre_x"],
        kept["pre_bc"], kept["raw_x"], kept["raw_bc"], kept["edge_x"], kept["edge_bc"],
        kept["dt"], kept["run"], kept["step_raw"], weights["dt_bias"], weights["rate"],
        kept["states"], weights["skip"], weights["taps_x"], weights["taps_bc"], arrived,
        kept["payloads"],
    )


def fixed_tail(packed, tail, back):
    rows = tail + moved_along(back, "seq", -1)
    return packed.at[packed.shape[0] - 16 :].set(rows.astype(bf16))


def vectors_of(heads, taps_x, gain_sum, skip_sum, bias_sum, rate_sum, norm_sum, taps_bc):
    return (
        jnp.concatenate(
            [
                taps_x[:CONV].reshape(-1), gain_sum[0], skip_sum[0], bias_sum[0, :heads],
                jnp.sum(rate_sum[:heads], axis=1),
            ]
        ),
        jnp.concatenate([norm_sum[0], taps_bc[:CONV].reshape(-1)]),
    )


def norm_backward(d_normed, row_sum, x, rescale, grad, gain, model):
    unit = x.astype(f32) * rescale
    h = d_normed.astype(f32) * gain
    out = grad.astype(f32) + rescale * (h - unit * (row_sum / model)[:, None])
    return out.astype(bf16)


def shards(
    tokens, cotangent, norm_gain, w_z, w_x, w_bc, w_dt, conv_x, conv_bc, dt_bias, a_log, skip_d,
    gate_gain, w_out,
):
    section = lax.axis_index("section")
    seq_at = lax.axis_index("seq")
    seq_size = lax.axis_size("seq")
    count, model = tokens.shape[1:]
    head_size = lax.axis_size("head")
    head_at = lax.axis_index("head")
    heads = a_log.shape[1]
    width = w_x.shape[2]
    shared = w_bc.shape[2]
    share = model // head_size
    row_share = count // head_size
    quarter = model // seq_size

    def mine_first(of_first, of_second):
        return (
            jnp.where(section == 0, of_first, of_second),
            jnp.where(section == 0, of_second, of_first),
        )

    def quarter_of(weight):
        return lax.dynamic_slice_in_dim(weight, seq_at * quarter, quarter, 0)

    def half_of(weight):
        pairs = weight.reshape(2, 2, quarter, weight.shape[1])
        return lax.dynamic_index_in_dim(pairs, lax.rem(seq_at, 2), 1, False)

    def own_rows(array):
        return lax.dynamic_slice_in_dim(array, head_at * row_share, row_share, 0)

    def own_columns(array):
        return lax.dynamic_slice_in_dim(array, head_at * share, share, 1)

    def edge_of(x):
        return jnp.pad(moved_along(x[count - (CONV - 1) :], "seq", 1), ((16 - (CONV - 1), 0), (0, 0)))

    def section_sum(of_first, of_second, earlier=None):
        mine, other = mine_first(of_first, of_second)
        arrived = traded(other, "section", 1)
        if earlier is not None:
            arrived = after(arrived, earlier)
        return mine.astype(f32) + arrived.astype(f32)

    def both_sequences(of_first, of_second, earlier=None):
        mine, other = mine_first(of_first, of_second)
        arrived = traded(other, "section", 1)
        if earlier is not None:
            arrived = after(arrived, earlier)
        return jnp.stack(mine_first(mine, arrived))

    padded_dt = jnp.pad(w_dt[0], ((0, 0), (0, LANES - heads)))
    got_pack = traded(
        jnp.concatenate([quarter_of(w) for w in (w_bc[0], padded_dt, w_x[0])], axis=1),
        "section", 1,
    )
    pack = jnp.concatenate([w_bc[0], padded_dt, w_x[0]], axis=1)
    vector = jnp.concatenate(
        [
            norm_gain[0], conv_x[0].T.reshape(-1), conv_bc[0].T.reshape(-1), dt_bias[0], a_log[0],
            skip_d[0], gate_gain[0],
        ]
    )
    got_pack, part_z, vector = tied(got_pack, half_of(w_z[0]), vector)
    vectors = mine_first(vector, traded(vector, "section", 1))
    first = lax.dynamic_index_in_dim(tokens, section, 0, False)
    first_edge = edge_of(first)
    got_z = traded(part_z, "section", 1)
    far_pack = traded(got_pack, "seq", 2)
    far_pack, got_z, part_out, pack, first, first_edge, *vectors = tied(
        far_pack, got_z, half_of(w_out[0]), pack, first, first_edge, *vectors
    )
    got_out = traded(part_out, "section", 1)
    sources_pack = (got_pack, far_pack, traded(got_pack, "seq", 1), traded(far_pack, "seq", 1))
    sources = dict(
        pack=(pack, *sources_pack), w_z=(w_z[0], got_z, traded(got_z, "seq", 1)), w_out=[w_out[0]]
    )
    weights = []
    for b in range(2):
        at = 0

        def take(size):
            nonlocal at
            at += size
            return vectors[b][at - size : at]

        block = dict(heads=heads, **sources)
        block["norm"] = take(model)[None]
        block["taps_x"] = take(CONV * width).reshape(CONV, width)
        block["taps_bc"] = take(CONV * shared).reshape(CONV, shared)
        block["dt_bias"] = jnp.pad(take(heads), (0, LANES - heads))[None]
        block["rate"] = jnp.pad(-jnp.exp(take(heads)), (0, LANES - heads))[None]
        block["skip"] = jnp.repeat(take(heads), width // heads)[None]
        block["gain"] = take(width)[None]
        weights.append(block)

    last_grad = lax.dynamic_index_in_dim(cotangent, section, 0, False)

    def fetch_out(inner, payloads):
        inner, part, *payloads = tied(inner, got_out, *payloads)
        sources["w_out"] += [part, traded(part, "seq", 1)]
        return inner, payloads

    part, sums, kept_first = block_forward(
        0, first, first_edge, weights[0], None, 1, fetch_out
    )
    summed = lax.psum_scatter(part, "head", scatter_dimension=0, tiled=True).astype(f32)
    sums_first = [sums, *others(sums, "head", 1)]
    scale_first = lax.rsqrt(sum(part[0] for part in sums_first) / INNER + epsilon)
    second_share = own_rows(first).astype(f32) + own_rows(scale_first)[:, None] * summed
    second = lax.all_gather(second_share.astype(bf16), "head", axis=0, tiled=True)

    outward, sums, kept_second = block_forward(
        1, second, edge_of(second), weights[1], last_grad, head_size
    )
    sums_second = [sums, *others(sums, "head", 1)]
    bits = list(bits_of("head"))

    grad_mixed, grad_gate, scaled, gain_sum, skip_sum, adjoint = gate_step(
        1, last_grad, sums_second, (), kept_second, weights[1]
    )
    normed = kept_second["normed"]
    early_sent = weights_backward([last_grad, normed], [scaled, grad_gate], False)
    grad_mixed, early_sent, outward, *arrived = tied(
        grad_mixed, early_sent, outward, *others(adjoint, "seq", -1)
    )
    packed, tail, back, taps_x, taps_bc, rate_sum, bias_sum = states_step(
        grad_mixed, arrived, kept_second, weights[1]
    )
    kept, sent = parted(outward, "head", bits[0])
    packed, kept, arrived = tied(
        fixed_tail(packed, tail, back), kept, traded(sent, "head", bits[0])
    )
    part, row_sum, norm_sum = part_backward(
        1, 1, grad_gate, packed, weights[1]["w_z"], weights[1]["pack"], second,
        weights[1]["norm"],
    )
    norm_sum, kept, taps_x, gain_sum, skip_sum, bias_sum, rate_sum, taps_bc = tied(
        norm_sum, kept, taps_x, gain_sum, skip_sum, bias_sum, rate_sum, taps_bc
    )
    outward = kept + arrived
    local_second, whole_second = vectors_of(
        heads, taps_x, gain_sum, skip_sum, bias_sum, rate_sum, norm_sum, taps_bc
    )
    part, packed, scaled, grad_gate = tied(part, packed, scaled, grad_gate)
    rows_part = lax.psum_scatter(part, "head", scatter_dimension=0, tiled=True)
    row_sums = [row_sum, *others(row_sum, "head", 1)]
    row_sum = sum(part[0] for part in row_sums)
    kept = weights_backward([last_grad, normed], [scaled, grad_gate], True)
    early_sent, early = core_sum(kept, traded(early_sent, "seq", 1), norm_sum)
    late_sent = weights_backward([normed], [packed], False)
    kept = weights_backward([normed], [packed], True)
    late_sent, late = core_sum(kept, traded(late_sent, "seq", 1), norm_sum)
    rows_part, early_sent, late_sent = tied(rows_part, early_sent, late_sent)
    early = early + traded(early_sent, "seq", 2)
    late = late + traded(late_sent, "seq", 2)
    middle_share = norm_backward(
        rows_part, own_rows(row_sum), own_rows(second), own_rows(kept_second["rescale"]),
        own_rows(last_grad), weights[1]["norm"], model,
    )
    middle_grad = lax.all_gather(middle_share, "head", axis=0, tiled=True)
    middle_grad, early_second, late_second, outward, local_second, whole_second = tied(
        middle_grad, early, late, outward, local_second, whole_second
    )
    for bit in bits[1:-1]:
        outward = halved(outward, "head", bit)
    out_kept, out_sent = parted(outward, "head", bits[-1])

    grad_mixed, grad_gate, scaled, gain_sum, skip_sum, adjoint = gate_step(
        0, middle_grad, sums_first, (second, first), kept_first, weights[0]
    )
    normed = kept_first["normed"]
    early_sent = weights_backward([middle_grad, normed], [scaled, grad_gate], False)
    grad_mixed, early_sent, out_sent, *arrived = tied(
        grad_mixed, early_sent, out_sent, *others(adjoint, "seq", -1)
    )
    packed, tail, back, taps_x, taps_bc, rate_sum, bias_sum = states_step(
        grad_mixed, arrived, kept_first, weights[0]
    )
    packed, out_arrived = tied(
        fixed_tail(packed, tail, back), traded(out_sent, "head", bits[-1])
    )
    late_sent = weights_backward([normed], [packed], False)
    kept = weights_backward([normed], [packed], True)
    late_sent, late = core_sum(kept, traded(late_sent, "seq", 1), None)
    packed, late_sent, late = tied(packed, late_sent, late)
    part, row_sum, norm_sum = part_backward(
        head_size, 0, grad_gate, packed, weights[0]["w_z"], weights[0]["pack"], first,
        weights[0]["norm"],
    )
    norm_sum, scaled, grad_gate, out_kept, *sums_second = tied(
        norm_sum, scaled, grad_gate, out_kept, *sums_second
    )
    outward = out_kept + out_arrived
    columns_part = lax.psum_scatter(part, "head", scatter_dimension=0, tiled=True)[0]
    row_sums = [row_sum, *others(row_sum, "head", 1)]
    row_sum = sum(part[0] for part in row_sums)
    kept = weights_backward([middle_grad, normed], [scaled, grad_gate], True)
    sent, early = core_sum(kept, traded(early_sent, "seq", 1), norm_sum)
    sent, late_arrived = tied(sent, traded(late_sent, "seq", 2))
    late = late + late_arrived
    late, sent, norm_sum, taps_x, gain_sum, skip_sum, bias_sum, rate_sum, taps_bc = tied(
        late, sent, norm_sum, taps_x, gain_sum, skip_sum, bias_sum, rate_sum, taps_bc
    )
    local_first, whole_first = vectors_of(
        heads, taps_x, gain_sum, skip_sum, bias_sum, rate_sum, norm_sum, taps_bc
    )
    vector = jnp.stack(
        [
            jnp.concatenate([whole_first, local_first]),
            jnp.concatenate([whole_second, local_second]),
        ]
    )
    vector = butterfly(vector, "seq")
    first_share = norm_backward(
        columns_part, row_sum, own_columns(first), kept_first["rescale"],
        own_columns(middle_grad), own_columns(weights[0]["norm"]), model,
    )
    vector = section_sum(vector[0], vector[1], first_share)
    late = section_sum(late, late_second, first_share)
    early = section_sum(early + traded(sent, "seq", 2), early_second, first_share)
    whole = butterfly(vector[: whole_first.shape[0]], "head")
    local = vector[whole_first.shape[0] :]
    last_share = lax.rsqrt(sum(part[0] for part in sums_second) / INNER + epsilon)
    last_share = last_share[:, None] * outward[0].astype(f32)
    last_share = (own_columns(second).astype(f32) + last_share).astype(bf16)
    block_outputs = both_sequences(own_columns(second), last_share, first_share)
    grad_w_bc = late[:, :shared].astype(bf16).reshape(quarter, head_size, shared // head_size)
    grad_w_bc = grad_w_bc.swapaxes(0, 1)
    for bit in bits:
        grad_w_bc = halved(grad_w_bc, "head", bit)
    input_grads = both_sequences(first_share, own_columns(middle_grad))
    at = 0

    def taken(size):
        nonlocal at
        at += size
        return local[at - size : at]

    grad_norm = lax.dynamic_slice_in_dim(whole, head_at * share, share, 0)
    grad_conv_bc = whole[model:].reshape(CONV, shared).T
    grad_conv_x = taken(CONV * width).reshape(CONV, width).T
    grad_gain = taken(width)
    grad_skip = jnp.sum(taken(width).reshape(heads, width // heads), axis=1)
    grad_bias = taken(heads)
    grad_rate = taken(heads)
    return (
        block_outputs[None],
        input_grads[None],
        grad_norm[None],
        early[None, :, width:],
        late[None, :, shared + LANES :],
        grad_w_bc.astype(f32),
        late[None, :, shared : shared + heads],
        grad_conv_x[None],
        grad_conv_bc[None],
        grad_bias[None],
        grad_rate[None],
        grad_skip[None],
        grad_gain[None],
        early[None, :, :width],
    )


def solution(mesh):
    placed = (
        P(None, "seq", None),
        P(None, "seq", None),
        P("section", None),
        P("section", None, "head"),
        P("section", None, "head"),
        P("section", None, None),
        P("section", None, "head"),
        P("section", "head", None),
        P("section", None, None),
        P("section", "head"),
        P("section", "head"),
        P("section", "head"),
        P("section", "head"),
        P("section", None, "head"),
    )
    return jax.shard_map(
        shards,
        mesh=mesh,
        in_specs=placed,
        out_specs=(
            P("section", None, "seq", "head"),
            P("section", None, "seq", "head"),
            P("section", "head"),
            P("section", "seq", "head"),
            P("section", "seq", "head"),
            P("section", "seq", "head"),
            P("section", "seq", "head"),
            P("section", "head", None),
            P("section", None, None),
            P("section", "head"),
            P("section", "head"),
            P("section", "head"),
            P("section", "head"),
            P("section", "seq", "head"),
        ),
        check_vma=False,
    )
```

```python
from functools import partial

import jax
import jax.numpy as jnp
from jax import lax
from jax.experimental import pallas as pl
from jax.experimental.pallas import tpu as pltpu
from jax.sharding import PartitionSpec as P

INNER = 3072
CONV = 4
CHUNK = 128
LANES = 128
ROWS = 256

epsilon = 1e-05
exact = lax.Precision.HIGHEST
f32 = jnp.float32
bf16 = jnp.bfloat16


def dot_nn(left, right, precision=None):
    return lax.dot_general(
        left, right, (((1,), (0,)), ((), ())), precision=precision, preferred_element_type=f32
    )


def dot_nt(left, right, precision=None):
    return lax.dot_general(
        left, right, (((1,), (1,)), ((), ())), precision=precision, preferred_element_type=f32
    )


def dot_tn(left, right):
    return lax.dot_general(left, right, (((0,), (0,)), ((), ())), preferred_element_type=f32)


def three_parts(values):
    high = values.astype(bf16)
    rest = values - high.astype(f32)
    middle = rest.astype(bf16)
    return high, middle, (rest - middle.astype(f32)).astype(bf16)


def lane_sums(values):
    ones = jnp.ones((8, values.shape[1]), bf16)
    return sum(dot_nt(ones, part) for part in three_parts(values))


def times_mask(values, mask):
    rows = values.shape[0]
    product = dot_nn(jnp.concatenate(three_parts(values), axis=0), mask)
    return product[:rows] + product[rows : 2 * rows] + product[2 * rows :]


def mask_times(mask, values):
    columns = values.shape[1]
    product = dot_nn(mask, jnp.concatenate(three_parts(values), axis=1))
    return product[:, :columns] + product[:, columns : 2 * columns] + product[:, 2 * columns :]


def sigmoid(values):
    return 0.5 * jnp.tanh(0.5 * values) + 0.5


def silu_parts(values):
    gate = sigmoid(values)
    return gate, values * gate


def silu_slope(values, gate):
    return gate * (1.0 + values * (1.0 - gate))


def weight_fetch(block, sources, held, sem):
    here = lax.axis_index("section") == block
    away = jnp.logical_not(here)

    @pl.when(here)
    def _():
        pltpu.make_async_copy(sources[0], held, sem).start()

    place = lax.axis_index("seq")
    if len(sources) == 3:
        rows = sources[1].shape[1]
        for piece in range(4):
            target = held.at[piece * rows : (piece + 1) * rows]
            for k in range(2):

                @pl.when(away & (lax.rem(place + piece, 2) == k))
                def _():
                    pltpu.make_async_copy(sources[1 + k].at[piece // 2], target, sem).start()

        return
    rows = sources[1].shape[0]
    for piece in range(4):
        target = held.at[piece * rows : (piece + 1) * rows]
        for k, bits in enumerate((0, 2, 1, 3)):
            bit_low = lax.rem(place + piece, 2) == bits % 2
            bit_high = lax.rem(place // 2 + piece // 2, 2) == bits // 2

            @pl.when(away & bit_low & bit_high)
            def _():
                pltpu.make_async_copy(sources[1 + k], target, sem).start()


def weight_wait(sources, held, sem):
    pltpu.make_async_copy(sources[0], held, sem).wait()


def anywhere():
    return pl.BlockSpec(memory_space=pl.ANY)


def weight_scratch(own):
    return [pltpu.VMEM(own.shape, own.dtype), pltpu.SemaphoreType.DMA]


def head_groups(width, heads):
    head_width = width // heads
    per_group = max(LANES // head_width, 1)
    found = []
    for first in range(0, heads, per_group):
        count = min(per_group, heads - first)
        found.append((first, count, first * head_width, count * head_width))
    return found


def spread(tile, first, count, lanes):
    rows = tile.shape[0]
    head_width = lanes // count
    out = jnp.broadcast_to(tile[:, first : first + 1], (rows, lanes))
    lane = lax.broadcasted_iota(jnp.int32, (rows, lanes), 1)
    for k in range(1, count):
        column = jnp.broadcast_to(tile[:, first + k : first + k + 1], (rows, lanes))
        out = jnp.where(lane >= k * head_width, column, out)
    return out


def own_lanes(tile, k, count):
    if count == 1:
        return tile
    head_width = tile.shape[1] // count
    lane = lax.broadcasted_iota(jnp.int32, tile.shape, 1)
    inside = (lane >= k * head_width) & (lane < (k + 1) * head_width)
    return jnp.where(inside, tile, jnp.zeros_like(tile))


def triangle(keep):
    row = lax.broadcasted_iota(jnp.int32, (CHUNK, CHUNK), 0)
    column = lax.broadcasted_iota(jnp.int32, (CHUNK, CHUNK), 1)
    return keep(row, column)


def decay_of(payload, state):
    rows = payload[state : state + 16].astype(f32)
    return jnp.exp(rows[0:1] + rows[8:9] + rows[12:13])


def project_kernel(
    heads,
    block,
    sources,
    x_in,
    x_edge,
    gain,
    *refs,
):
    pack_sources, refs = refs[:sources], refs[sources:]
    (
        dt_bias, rate, taps_x, taps_bc, normed_out, rescale_out, raw_x, raw_bc,
        edge_x, edge_bc, step_raw, pre_x, pre_bc, act_x, act_bc, dt_out,
        run_out, payload, ext_x, ext_bc, end_out, total_out, pack, pack_sem,
    ) = refs
    step = pl.program_id(0)
    groups = head_groups(raw_x.shape[1], heads)
    shared = act_bc.shape[1]
    state = shared // 2

    def normed_of(block):
        x = block.astype(f32)
        rescale = lax.rsqrt(jnp.mean(x * x, axis=-1, keepdims=True) + epsilon)
        return rescale, (x * rescale * gain[...]).astype(bf16)

    @pl.when(step == 0)
    def _():
        weight_fetch(block, pack_sources, pack, pack_sem)
        _, edge = normed_of(x_edge[...])
        weight_wait(pack_sources, pack, pack_sem)
        edge_x[...] = dot_nn(edge, pack[:, shared + LANES :]).astype(bf16).astype(f32)[8:]
        edge_bc[...] = dot_nn(edge, pack[:, :shared]).astype(bf16).astype(f32)[8:]
        ext_x[0:8] = edge_x[...]
        ext_bc[0:8] = edge_bc[...]
        end_out[...] = jnp.zeros_like(end_out)
        total_out[...] = jnp.zeros_like(total_out)

    @pl.when(step > 0)
    def _():
        ext_x[0:8] = ext_x[ROWS : ROWS + 8]
        ext_bc[0:8] = ext_bc[ROWS : ROWS + 8]

    rescale, normed = normed_of(x_in[...])
    rescale_out[...] = rescale
    normed_out[...] = normed
    low = dot_nn(normed, pack[:, :shared]).astype(bf16)
    raw_bc[...] = low
    ext_bc[8:] = low.astype(f32)
    step_in = dot_nn(normed, pack[:, shared : shared + LANES])
    step_raw[...] = step_in
    sizes = jax.nn.softplus(step_in + dt_bias[...])
    dt_out[...] = sizes
    low = dot_nn(normed, pack[:, shared + LANES :]).astype(bf16)
    raw_x[...] = low
    ext_x[8:] = low.astype(f32)
    for ext, taps, pre, act in ((ext_bc, taps_bc, pre_bc, act_bc), (ext_x, taps_x, pre_x, act_x)):
        total = ext[5 : 5 + ROWS] * taps[0:1]
        for k in range(1, CONV):
            total = total + ext[5 + k : 5 + k + ROWS] * taps[k : k + 1]
        pre[...] = total.astype(bf16)
        act[...] = silu_parts(total)[1].astype(bf16)
    lower = triangle(lambda t, s: t >= s).astype(bf16)
    for sub in range(ROWS // CHUNK):
        at = slice(sub * CHUNK, (sub + 1) * CHUNK)
        dt = sizes[at]
        run = mask_times(lower, dt * rate[...])
        run_out[at] = run
        last = run[CHUNK - 1 : CHUNK]
        weight = jnp.exp(last - run) * dt
        decay = jnp.exp(last)
        b_turned = act_bc[at, :state].astype(f32).T.astype(bf16)
        for first, count, lane, lanes in groups:
            cols = slice(lane, lane + lanes)
            scaled = act_x[at, cols].astype(f32) * spread(weight, first, count, lanes)
            end_out[:, cols] = spread(decay, first, count, lanes) * end_out[:, cols] + dot_nn(
                b_turned, scaled.astype(bf16)
            )
        total_out[...] += jnp.broadcast_to(last, total_out.shape)

    @pl.when(step == pl.num_programs(0) - 1)
    def _():
        for first, count, lane, lanes in groups:
            cols = slice(lane, lane + lanes)
            payload[:state, cols] = end_out[:, cols].astype(bf16)
            total = spread(total_out[...], first, count, lanes)
            high = total.astype(bf16).astype(f32)
            middle = (total - high).astype(bf16).astype(f32)
            low = total - high - middle
            row = lax.broadcasted_iota(jnp.int32, (8, lanes), 0)
            rest = jnp.where(row < 4, middle, low)
            payload[state:, cols] = jnp.concatenate([high, rest], axis=0).astype(bf16)


def full(shape):
    return pl.BlockSpec(shape, lambda i: (0,) * len(shape))


def rows_of(width, back=0):
    if back:
        return pl.BlockSpec((ROWS, width), lambda i: (back - 1 - i, 0))
    return pl.BlockSpec((ROWS, width), lambda i: (i, 0))


def pieces_of(pieces, count, model):
    if pieces == 1:
        return rows_of(model), (count, model)
    lanes = model // pieces
    return pl.BlockSpec((pieces, ROWS, lanes), lambda i: (0, i, 0)), (pieces, count, lanes)


def params():
    return pltpu.CompilerParams(
        dimension_semantics=("arbitrary",), vmem_limit_bytes=60 * 1024 * 1024
    )


def project_forward(
    heads, block, x, x_edge, gain, pack, dt_bias, rate, taps_x, taps_bc
):
    count, model = x.shape
    width, shared = taps_x.shape[1], taps_bc.shape[1]
    state = shared // 2
    return pl.pallas_call(
        partial(project_kernel, heads, block, len(pack)),
        grid=(count // ROWS,),
        in_specs=[
            rows_of(model),
            full((16, model)),
            full((1, model)),
            *[anywhere() for _ in pack],
            full((1, LANES)),
            full((1, LANES)),
            full((CONV, width)),
            full((CONV, shared)),
        ],
        out_specs=[
            rows_of(model),
            rows_of(1),
            rows_of(width),
            rows_of(shared),
            full((8, width)),
            full((8, shared)),
            rows_of(LANES),
            rows_of(width),
            rows_of(shared),
            rows_of(width),
            rows_of(shared),
            rows_of(LANES),
            rows_of(LANES),
            full((state + 16, width)),
        ],
        out_shape=[
            jax.ShapeDtypeStruct((count, model), bf16),
            jax.ShapeDtypeStruct((count, 1), f32),
            jax.ShapeDtypeStruct((count, width), bf16),
            jax.ShapeDtypeStruct((count, shared), bf16),
            jax.ShapeDtypeStruct((8, width), f32),
            jax.ShapeDtypeStruct((8, shared), f32),
            jax.ShapeDtypeStruct((count, LANES), f32),
            jax.ShapeDtypeStruct((count, width), bf16),
            jax.ShapeDtypeStruct((count, shared), bf16),
            jax.ShapeDtypeStruct((count, width), bf16),
            jax.ShapeDtypeStruct((count, shared), bf16),
            jax.ShapeDtypeStruct((count, LANES), f32),
            jax.ShapeDtypeStruct((count, LANES), f32),
            jax.ShapeDtypeStruct((state + 16, width), bf16),
        ],
        scratch_shapes=[
            pltpu.VMEM((8 + ROWS, width), f32),
            pltpu.VMEM((8 + ROWS, shared), f32),
            pltpu.VMEM((state, width), f32),
            pltpu.VMEM((8, LANES), f32),
            *weight_scratch(pack[0]),
        ],
        compiler_params=params(),
        cost_estimate=pl.CostEstimate(
            flops=2 * count * model * pack[0].shape[1],
            bytes_accessed=2 * pack[0].size + count * (4 * model + 6 * (width + shared)),
            transcendentals=count * (width + shared),
        ),
        name="project_forward",
    )(x, x_edge, gain, *pack, dt_bias, rate, taps_x, taps_bc)


def inner_kernel(
    heads, block, act_x, act_bc, dt_in, run_in, normed, *refs
):
    *z_sources, gate_out, inner_out, w_z, z_sem = refs

    @pl.when(pl.program_id(0) == 0)
    def _():
        weight_fetch(block, z_sources, w_z, z_sem)
        weight_wait(z_sources, w_z, z_sem)

    groups = head_groups(act_x.shape[1], heads)
    state = act_bc.shape[1] // 2
    gate_out[...] = dot_nn(normed[...], w_z[...])
    causal = triangle(lambda t, s: t >= s)
    for sub in range(ROWS // CHUNK):
        at = slice(sub * CHUNK, (sub + 1) * CHUNK)
        dt = dt_in[at]
        run = run_in[at]
        turned = run.T
        product = dot_nt(act_bc[at, state:], act_bc[at, :state])
        for first, count, lane, lanes in groups:
            cols = slice(lane, lane + lanes)
            stepped = act_x[at, cols].astype(f32) * spread(dt, first, count, lanes)
            low = stepped.astype(bf16)
            weights = []
            stacked = []
            for k in range(count):
                h = first + k
                gap = jnp.broadcast_to(run[:, h : h + 1], (CHUNK, CHUNK)) - turned[h : h + 1]
                factor = jnp.exp(jnp.where(causal, gap, -jnp.inf))
                weights.append((product * factor).astype(bf16))
                stacked.append(own_lanes(low, k, count))
            inner_out[at, cols] = dot_nn(
                jnp.concatenate(weights, axis=1), jnp.concatenate(stacked, axis=0)
            )


def inner_forward(heads, block, act_x, act_bc, dt, run, normed, w_z):
    count, width = act_x.shape
    model = normed.shape[1]
    shared = act_bc.shape[1]
    return pl.pallas_call(
        partial(inner_kernel, heads, block),
        grid=(count // ROWS,),
        in_specs=[
            rows_of(width),
            rows_of(shared),
            rows_of(LANES),
            rows_of(LANES),
            rows_of(model),
            *[anywhere() for _ in w_z],
        ],
        out_specs=[rows_of(width), rows_of(width)],
        out_shape=[
            jax.ShapeDtypeStruct((count, width), f32),
            jax.ShapeDtypeStruct((count, width), f32),
        ],
        scratch_shapes=weight_scratch(w_z[0]),
        compiler_params=params(),
        cost_estimate=pl.CostEstimate(
            flops=2 * count * width * (4 * CHUNK + model),
            bytes_accessed=count * (10 * width + 2 * model) + 2 * w_z[0].size,
            transcendentals=count * heads * CHUNK,
        ),
        name="inner_forward",
    )(act_x, act_bc, dt, run, normed, *w_z)


def outer_kernel(
    heads,
    block,
    sources,
    pieces,
    shards,
    act_x,
    act_bc,
    dt_in,
    run_in,
    gate_in,
    inner_in,
    *refs,
):
    out_sources, refs = refs[:sources], refs[sources:]
    skip, gain, *refs = refs
    arrived, refs = refs[: shards - 1], refs[shards - 1 :]
    grad_in, refs = (refs[0], refs[1:]) if len(refs) == 9 else (None, refs)
    mixed_out, scaled_out, part_out, sums_out, states_out, held, w_out, out_sem = refs
    groups = head_groups(act_x.shape[1], heads)
    state = act_bc.shape[1] // 2

    @pl.when(pl.program_id(0) == 0)
    def _():
        weight_fetch(block, out_sources, w_out, out_sem)
        place = lax.axis_index("seq")
        held[...] = jnp.zeros_like(held)
        for distance in reversed(range(1, shards)):

            @pl.when(place >= distance)
            def _():
                payload = arrived[distance - 1]
                held[...] = decay_of(payload, state) * held[...] + payload[:state].astype(f32)

    square_rows = []
    ones = jnp.ones((8, LANES), f32)
    for sub in range(ROWS // CHUNK):
        at = slice(sub * CHUNK, (sub + 1) * CHUNK)
        run = run_in[at]
        last = run[CHUNK - 1 : CHUNK]
        weight = jnp.exp(last - run) * dt_in[at]
        decay = jnp.exp(last)
        grown = jnp.exp(run)
        c_part = act_bc[at, state:]
        b_turned = act_bc[at, :state].astype(f32).T.astype(bf16)
        states_out[sub] = held[...].astype(bf16)
        squares = jnp.zeros((CHUNK, LANES), f32)
        for first, count, lane, lanes in groups:
            cols = slice(lane, lane + lanes)
            x_part = act_x[at, cols].astype(f32)
            before = held[:, cols]
            mixed = inner_in[at, cols] + spread(grown, first, count, lanes) * dot_nn(
                c_part, before.astype(bf16)
            )
            mixed = mixed + skip[:, cols] * x_part
            held[:, cols] = spread(decay, first, count, lanes) * before + dot_nn(
                b_turned, (x_part * spread(weight, first, count, lanes)).astype(bf16)
            )
            gated = mixed * silu_parts(gate_in[at, cols])[1]
            mixed_out[at, cols] = mixed.astype(bf16)
            scaled_out[at, cols] = (gated * gain[:, cols]).astype(bf16)
            square = gated * gated
            if lanes < LANES:
                fill = jnp.zeros((CHUNK, LANES - lanes), f32)
                square = jnp.concatenate([square, fill], axis=1)
            squares = squares + square
        square_rows.append(lane_sums(squares))

    @pl.when(pl.program_id(0) == 0)
    def _():
        weight_wait(out_sources, w_out, out_sem)

    part = dot_nt(scaled_out[...], w_out[...])
    if pieces == 1:
        part_out[...] = part.astype(bf16)
    else:
        wide = part.shape[1] // pieces
        for k in range(pieces):
            part_out[k] = part[:, k * wide : (k + 1) * wide].astype(bf16)
    row = lax.broadcasted_iota(jnp.int32, (8, CHUNK), 0)
    for sub in range(ROWS // CHUNK):
        at = slice(sub * CHUNK, (sub + 1) * CHUNK)
        pair_row = jnp.zeros((8, CHUNK), f32)
        if grad_in is not None:
            pairs = jnp.zeros((CHUNK, LANES), f32)
            for lane in range(0, part.shape[1], LANES):
                cols = slice(lane, lane + LANES)
                pairs = pairs + part[at, cols] * grad_in[at, cols].astype(f32)
            pair_row = lane_sums(pairs)
        sums_out[:, at] = jnp.where(row == 0, square_rows[sub], pair_row)


def outer_forward(
    heads, block, pieces, act_x, act_bc, dt, run, gate_in, inner, w_out, skip, gain, arrived, grad_in
):
    count, width = act_x.shape
    model = w_out[0].shape[0]
    part_spec, part_shape = pieces_of(pieces, count, model)
    shared = act_bc.shape[1]
    state = shared // 2
    subs = ROWS // CHUNK
    extra, extra_specs = [], []
    if grad_in is not None:
        extra, extra_specs = [grad_in], [rows_of(model)]
    return pl.pallas_call(
        partial(outer_kernel, heads, block, len(w_out), pieces, len(arrived) + 1),
        grid=(count // ROWS,),
        in_specs=[
            rows_of(width),
            rows_of(shared),
            rows_of(LANES),
            rows_of(LANES),
            rows_of(width),
            rows_of(width),
            *[anywhere() for _ in w_out],
            full((1, width)),
            full((1, width)),
            *[full(payload.shape) for payload in arrived],
            *extra_specs,
        ],
        out_specs=[
            rows_of(width),
            rows_of(width),
            part_spec,
            pl.BlockSpec((8, ROWS), lambda i: (0, i)),
            pl.BlockSpec((subs, state, width), lambda i: (i, 0, 0)),
        ],
        out_shape=[
            jax.ShapeDtypeStruct((count, width), bf16),
            jax.ShapeDtypeStruct((count, width), bf16),
            jax.ShapeDtypeStruct(part_shape, bf16),
            jax.ShapeDtypeStruct((8, count), f32),
            jax.ShapeDtypeStruct((count // CHUNK, state, width), bf16),
        ],
        scratch_shapes=[pltpu.VMEM((state, width), f32), *weight_scratch(w_out[0])],
        compiler_params=params(),
        cost_estimate=pl.CostEstimate(
            flops=2 * count * width * (2 * state + model),
            bytes_accessed=count * width * 18,
            transcendentals=count * width,
        ),
        name="outer_forward",
    )(
        act_x, act_bc, dt, run, gate_in, inner, *w_out, skip, gain, *arrived, *extra
    )


def ahead_kernel(block, sources, grad, *refs):
    *out_sources, out, w_out, out_sem = refs

    @pl.when(pl.program_id(0) == 0)
    def _():
        weight_fetch(block, out_sources, w_out, out_sem)
        weight_wait(out_sources, w_out, out_sem)

    out[...] = dot_nn(grad[...], w_out[...])


def ahead_backward(block, grad, w_out):
    count, model = grad.shape
    width = w_out[0].shape[1]
    return pl.pallas_call(
        partial(ahead_kernel, block, len(w_out)),
        grid=(count // ROWS,),
        in_specs=[rows_of(model), *[anywhere() for _ in w_out]],
        out_specs=rows_of(width),
        out_shape=jax.ShapeDtypeStruct((count, width), f32),
        scratch_shapes=weight_scratch(w_out[0]),
        compiler_params=params(),
        cost_estimate=pl.CostEstimate(
            flops=2 * count * width * model,
            bytes_accessed=count * (2 * model + 4 * width) + 2 * model * width,
            transcendentals=0,
        ),
        name="ahead_backward",
    )(grad, *w_out)


def gate_kernel(
    heads,
    block,
    sources,
    addends,
    between,
    grad,
    gate_in,
    mixed_in,
    scaled_in,
    act_x,
    act_bc,
    run_in,
    gain,
    *refs,
):
    out_sources, refs = refs[:sources], refs[sources:]
    sums, refs = refs[:addends], refs[addends:]
    later, earlier = refs[:2] if between else (None, None)
    refs = refs[2:] if between else refs
    grad_mixed, grad_gate, scaled_out, gain_sum, skip_sum, adjoint_out, *refs = refs
    if sources:
        grad_in, adjoint, scales, w_out, out_sem = refs
    else:
        grad_in, (adjoint, scales) = grad, refs
    step = pl.program_id(0)
    groups = head_groups(act_x.shape[1], heads)
    state = act_bc.shape[1] // 2

    @pl.when(step == 0)
    def _():
        if sources:
            weight_fetch(block, out_sources, w_out, out_sem)
        gain_sum[...] = jnp.zeros_like(gain_sum)
        skip_sum[...] = jnp.zeros_like(skip_sum)
        adjoint[...] = jnp.zeros_like(adjoint)
        scales[...] = jnp.zeros_like(scales)
        if sources:
            weight_wait(out_sources, w_out, out_sem)

    if sources:
        grad_in[...] = dot_nn(grad[...], w_out[...])
    total = sums[0][...]
    for more in sums[1:]:
        total = total + more[...]
    scale_row = lax.rsqrt(total[0:1] / INNER + epsilon)
    pull_row = total[1:2] * scale_row * scale_row * scale_row / INNER
    for sub in reversed(range(ROWS // CHUNK)):
        at = slice(sub * CHUNK, (sub + 1) * CHUNK)
        run = run_in[at]
        grown = jnp.exp(run)
        decay = grown[CHUNK - 1 : CHUNK]
        c_turned = act_bc[at, state:].astype(f32).T.astype(bf16)
        scales[0:1] = scale_row[:, at]
        scales[1:2] = pull_row[:, at]
        columns = scales[...].T
        row_scale = columns[:, 0:1]
        row_pull = columns[:, 1:2]
        if later is not None:
            moved = later[at].astype(f32) - earlier[at].astype(f32)
            pulled = jnp.sum(grad[at].astype(f32) * moved, axis=1, keepdims=True)
            row_pull = pulled * row_scale * row_scale * (1.0 / INNER)
        for first, count, lane, lanes in groups:
            cols = slice(lane, lane + lanes)
            gate = gate_in[at, cols]
            mixed = mixed_in[at, cols].astype(f32)
            share, active = silu_parts(gate)
            gated = mixed * active
            d_scaled = grad_in[at, cols] * row_scale
            d_gated = d_scaled * gain[:, cols] - row_pull * gated
            d_mixed = d_gated * active
            grad_mixed[at, cols] = d_mixed.astype(bf16)
            grad_gate[at, cols] = (d_gated * mixed * silu_slope(gate, share)).astype(bf16)
            scaled_out[at, cols] = (scaled_in[at, cols].astype(f32) * row_scale).astype(bf16)
            gain_sum[0:1, cols] += jnp.sum(d_scaled * gated, axis=0, keepdims=True)
            skip_sum[0:1, cols] += jnp.sum(
                d_mixed * act_x[at, cols].astype(f32), axis=0, keepdims=True
            )
            adjoint[:, cols] = spread(decay, first, count, lanes) * adjoint[:, cols] + dot_nn(
                c_turned, (d_mixed * spread(grown, first, count, lanes)).astype(bf16)
            )

    @pl.when(step == pl.num_programs(0) - 1)
    def _():
        adjoint_out[...] = adjoint[...].astype(bf16)


def gate_backward(
    heads, block, grad, w_out, gate_in, mixed, scaled, act_x, act_bc, run, gain, sums, ends
):
    count, width = act_x.shape
    model = grad.shape[1]
    shared = act_bc.shape[1]
    state = shared // 2
    steps = count // ROWS
    return pl.pallas_call(
        partial(gate_kernel, heads, block, len(w_out), len(sums), len(ends) > 0),
        grid=(steps,),
        in_specs=[
            rows_of(model, steps),
            rows_of(width, steps),
            rows_of(width, steps),
            rows_of(width, steps),
            rows_of(width, steps),
            rows_of(shared, steps),
            rows_of(LANES, steps),
            full((1, width)),
            *[anywhere() for _ in w_out],
            *[pl.BlockSpec((8, ROWS), lambda i: (0, steps - 1 - i)) for _ in sums],
            *[rows_of(model, steps) for _ in ends],
        ],
        out_specs=[
            rows_of(width, steps),
            rows_of(width, steps),
            rows_of(width, steps),
            full((8, width)),
            full((8, width)),
            full((state, width)),
        ],
        out_shape=[
            jax.ShapeDtypeStruct((count, width), bf16),
            jax.ShapeDtypeStruct((count, width), bf16),
            jax.ShapeDtypeStruct((count, width), bf16),
            jax.ShapeDtypeStruct((8, width), f32),
            jax.ShapeDtypeStruct((8, width), f32),
            jax.ShapeDtypeStruct((state, width), bf16),
        ],
        scratch_shapes=[
            *([pltpu.VMEM((ROWS, width), f32)] if w_out else []),
            pltpu.VMEM((state, width), f32),
            pltpu.VMEM((CHUNK, CHUNK), f32),
            *(weight_scratch(w_out[0]) if w_out else []),
        ],
        compiler_params=params(),
        cost_estimate=pl.CostEstimate(
            flops=2 * count * width * (state + model),
            bytes_accessed=count * width * 16,
            transcendentals=count * width,
        ),
        name="gate_backward",
    )(
        grad, gate_in, mixed, scaled, act_x, act_bc, run, gain, *w_out, *sums, *ends
    )


def states_kernel(
    heads,
    shards,
    grad_mixed,
    act_x,
    act_bc,
    pre_x,
    pre_bc,
    raw_x,
    raw_bc,
    edge_x,
    edge_bc,
    dt_in,
    run_in,
    step_raw,
    dt_bias,
    rate_rows,
    states_in,
    skip,
    taps_x,
    taps_bc,
    members,
    *refs,
):
    arrived, payloads, refs = refs[: shards - 1], refs[shards - 1 : 2 * shards - 2], refs[2 * shards - 2 :]
    packed, tail, back, tap_sum_x, tap_sum_bc, rate_sum, bias_sum, *refs = refs
    adjoint, d_pre_x, d_pre_bc, rows_ref, carry_ref, square_ref = refs
    step = pl.program_id(0)
    steps = pl.num_programs(0)
    groups = head_groups(act_x.shape[1], heads)
    shared = act_bc.shape[1]
    state = shared // 2
    padded = members.shape[0]

    @pl.when(step == 0)
    def _():
        place = lax.axis_index("seq")
        adjoint[...] = jnp.zeros_like(adjoint)
        for distance in reversed(range(1, shards)):

            @pl.when(place + distance < shards)
            def _():
                decay = decay_of(payloads[shards - 1 - distance], state)
                adjoint[...] = decay * adjoint[...] + arrived[distance - 1][...].astype(f32)

        d_pre_x[8:16] = jnp.zeros((8, d_pre_x.shape[1]), f32)
        d_pre_bc[8:16] = jnp.zeros((8, d_pre_bc.shape[1]), f32)
        tap_sum_x[...] = jnp.zeros_like(tap_sum_x)
        tap_sum_bc[...] = jnp.zeros_like(tap_sum_bc)
        rate_sum[...] = jnp.zeros_like(rate_sum)
        bias_sum[...] = jnp.zeros_like(bias_sum)
        rows_ref[...] = jnp.zeros_like(rows_ref)
        square_ref[...] = jnp.zeros_like(square_ref)

    upto = triangle(lambda s, t: s <= t)
    not_before = triangle(lambda s, t: s >= t).astype(bf16)
    before = triangle(lambda s, t: s < t).astype(bf16)
    head_lane = lax.broadcasted_iota(jnp.int32, (CHUNK, LANES), 1)
    for sub in reversed(range(ROWS // CHUNK)):
        at = slice(sub * CHUNK, (sub + 1) * CHUNK)
        dt = dt_in[at]
        run = run_in[at]
        last = run[CHUNK - 1 : CHUNK]
        grown = jnp.exp(run)
        decay = grown[CHUNK - 1 : CHUNK]
        to_end = jnp.exp(last - run)
        run_turned = run.T
        dt_turned = dt.T[0:padded]
        inside_tile = jnp.zeros((CHUNK, LANES), f32)
        b_part = act_bc[at, :state]
        c_part = act_bc[at, state:]
        c_turned = c_part.astype(f32).T.astype(bf16)
        product = dot_nt(b_part, c_part)
        d_product = jnp.zeros((CHUNK, CHUNK), f32)
        d_b = jnp.zeros((CHUNK, state), f32)
        d_c = jnp.zeros((CHUNK, state), f32)
        d_pre_x[CHUNK + 8 : CHUNK + 16] = d_pre_x[8:16]
        d_pre_bc[CHUNK + 8 : CHUNK + 16] = d_pre_bc[8:16]
        through = []
        for first, count, lane, lanes in groups:
            cols = slice(lane, lane + lanes)
            x_low = act_x[at, cols]
            x_part = x_low.astype(f32)
            dy_low = grad_mixed[at, cols]
            dy = dy_low.astype(f32)
            dt_wide = spread(dt, first, count, lanes)
            ending = spread(to_end, first, count, lanes)
            growing = spread(grown, first, count, lanes)
            lam = adjoint[:, cols]
            lam_low = lam.astype(bf16)
            held_low = states_in[sub][:, cols]
            weights = []
            stacked = []
            for k in range(count):
                h = first + k
                gap = run_turned[h : h + 1] - jnp.broadcast_to(run[:, h : h + 1], (CHUNK, CHUNK))
                factor = jnp.exp(jnp.where(upto, gap, -jnp.inf))
                weights.append((product * factor).astype(bf16))
                stacked.append(own_lanes(dy_low, k, count))
                paired = dot_nt(own_lanes(x_low, k, count), dy_low) * factor
                dt_column = jnp.broadcast_to(dt[:, h : h + 1], (CHUNK, CHUNK))
                d_product = d_product + paired * dt_column
                inside = paired * product
                rows_ref[h : h + 1] = jnp.sum(inside * dt_column, axis=0, keepdims=True)
                inside_tile = jnp.where(
                    head_lane == h, jnp.sum(inside, axis=1, keepdims=True), inside_tile
                )
            d_stepped = dot_nn(jnp.concatenate(weights, axis=1), jnp.concatenate(stacked, axis=0))
            from_end = ending * dot_nn(b_part, lam_low)
            d_x = dt_wide * (d_stepped + from_end) + skip[:, cols] * dy
            dy_grown = dy * growing
            dy_grown_low = dy_grown.astype(bf16)
            carry_ref[0, :, cols] = (x_part * from_end).astype(bf16)
            carry_ref[1, :, cols] = (dy_grown * dot_nn(c_part, held_low)).astype(bf16)
            d_b = d_b + dot_nt((x_part * dt_wide * ending).astype(bf16), lam_low)
            d_c = d_c + dot_nt(dy_grown_low, held_low)
            wide_decay = spread(decay, first, count, lanes)
            lam_decayed = wide_decay * lam
            through.append(
                jnp.sum(lam_decayed * held_low.astype(f32), axis=0, keepdims=True)
            )
            adjoint[:, cols] = lam_decayed + dot_nn(c_turned, dy_grown_low)
            pre = pre_x[at, cols].astype(f32)
            d_pre_x[8 : CHUNK + 8, cols] = d_x * silu_slope(pre, sigmoid(pre))
        member = members[...]
        kept = dot_nt(member, carry_ref[0])
        fed = dot_nt(member, carry_ref[1])
        wide_row = jnp.concatenate(through, axis=1)
        across = jnp.sum(member.astype(f32) * wide_row, axis=1, keepdims=True)
        inside_rows = inside_tile.T[0:padded]
        d_log = (
            times_mask(rows_ref[...] - dt_turned * inside_rows + fed, not_before)
            + times_mask(dt_turned * kept, before)
            + across
        )
        d_log_rate = d_log * rate_rows[...]
        rate_sum[...] += d_log_rate * dt_turned
        square_ref[0:padded] = d_log_rate + inside_rows + kept
        d_step_exact = square_ref[...].T * sigmoid(step_raw[at] + dt_bias[...])
        bias_sum[0:1] += jnp.sum(d_step_exact, axis=0, keepdims=True)
        packed[at, shared : shared + LANES] = d_step_exact.astype(bf16)
        if sub == ROWS // CHUNK - 1:

            @pl.when(step == 0)
            def _():
                tail[:, shared : shared + LANES] = d_step_exact[CHUNK - 16 :]

        d_product_low = d_product.astype(bf16)
        d_b = d_b + dot_nn(d_product_low, c_part)
        d_c = d_c + dot_nn(d_product.T.astype(bf16), b_part)
        pre = pre_bc[at].astype(f32)
        slope = silu_slope(pre, sigmoid(pre))
        d_pre_bc[8 : CHUNK + 8, :state] = d_b * slope[:, :state]
        d_pre_bc[8 : CHUNK + 8, state:] = d_c * slope[:, state:]
        for d_pre, raw, taps, place, tap_sum in (
            (d_pre_x, raw_x, taps_x, slice(shared + LANES, None), tap_sum_x),
            (d_pre_bc, raw_bc, taps_bc, slice(0, shared), tap_sum_bc),
        ):
            values = raw[at].astype(f32)
            total = jnp.zeros_like(values)
            for k in range(CONV):
                moved = d_pre[11 - k : 11 - k + CHUNK]
                total = total + moved * taps[k : k + 1]
                tap_sum[k : k + 1] += jnp.sum(values * moved, axis=0, keepdims=True)
            packed[at, place] = total.astype(bf16)
            if sub == ROWS // CHUNK - 1:

                @pl.when(step == 0)
                def _():
                    tail[:, place] = total[CHUNK - 16 :]

    @pl.when(step == steps - 1)
    def _():
        back[...] = jnp.zeros_like(back)
        for d_pre, edge, taps, tap_sum, place in (
            (d_pre_x, edge_x, taps_x, tap_sum_x, slice(shared + LANES, None)),
            (d_pre_bc, edge_bc, taps_bc, tap_sum_bc, slice(0, shared)),
        ):
            d_pre[0:8] = jnp.zeros((8, d_pre.shape[1]), f32)
            values = edge[...]
            total = jnp.zeros_like(values)
            for k in range(CONV):
                moved = d_pre[3 - k : 11 - k]
                total = total + moved * taps[k : k + 1]
                tap_sum[k : k + 1] += jnp.sum(values * moved, axis=0, keepdims=True)
            back[8:, place] = total


def states_backward(
    heads,
    grad_mixed,
    act_x,
    act_bc,
    pre_x,
    pre_bc,
    raw_x,
    raw_bc,
    edge_x,
    edge_bc,
    dt,
    run,
    step_raw,
    dt_bias,
    rate,
    states,
    skip,
    taps_x,
    taps_bc,
    arrived,
    payloads,
):
    count, width = act_x.shape
    shared = act_bc.shape[1]
    state = shared // 2
    steps = count // ROWS
    subs = ROWS // CHUNK
    padded = -(-heads // 16) * 16
    head_of = jnp.arange(width)[None, :] // (width // heads)
    members = (jnp.arange(padded)[:, None] == head_of).astype(bf16)
    rate_rows = jnp.broadcast_to(rate[0, :padded, None], (padded, CHUNK))
    return pl.pallas_call(
        partial(states_kernel, heads, len(arrived) + 1),
        grid=(steps,),
        in_specs=[
            rows_of(width, steps),
            rows_of(width, steps),
            rows_of(shared, steps),
            rows_of(width, steps),
            rows_of(shared, steps),
            rows_of(width, steps),
            rows_of(shared, steps),
            full((8, width)),
            full((8, shared)),
            rows_of(LANES, steps),
            rows_of(LANES, steps),
            rows_of(LANES, steps),
            full((1, LANES)),
            full((padded, CHUNK)),
            pl.BlockSpec((subs, state, width), lambda i: (steps - 1 - i, 0, 0)),
            full((1, width)),
            full((CONV, width)),
            full((CONV, shared)),
            full((padded, width)),
            *[full(array.shape) for array in (*arrived, *payloads)],
        ],
        out_specs=[
            rows_of(shared + LANES + width, steps),
            full((16, shared + LANES + width)),
            full((16, shared + LANES + width)),
            full((8, width)),
            full((8, shared)),
            full((padded, CHUNK)),
            full((8, LANES)),
        ],
        out_shape=[
            jax.ShapeDtypeStruct((count, shared + LANES + width), bf16),
            jax.ShapeDtypeStruct((16, shared + LANES + width), f32),
            jax.ShapeDtypeStruct((16, shared + LANES + width), f32),
            jax.ShapeDtypeStruct((8, width), f32),
            jax.ShapeDtypeStruct((8, shared), f32),
            jax.ShapeDtypeStruct((padded, CHUNK), f32),
            jax.ShapeDtypeStruct((8, LANES), f32),
        ],
        scratch_shapes=[
            pltpu.VMEM((state, width), f32),
            pltpu.VMEM((CHUNK + 16, width), f32),
            pltpu.VMEM((CHUNK + 16, shared), f32),
            pltpu.VMEM((padded, CHUNK), f32),
            pltpu.VMEM((2, CHUNK, width), bf16),
            pltpu.VMEM((CHUNK, CHUNK), f32),
        ],
        compiler_params=params(),
        cost_estimate=pl.CostEstimate(
            flops=20 * count * width * state,
            bytes_accessed=count * width * 16,
            transcendentals=count * heads * CHUNK * 2,
        ),
        name="states_backward",
    )(
        grad_mixed,
        act_x,
        act_bc,
        pre_x,
        pre_bc,
        raw_x,
        raw_bc,
        edge_x,
        edge_bc,
        dt,
        run,
        step_raw,
        dt_bias,
        rate_rows,
        states,
        skip,
        taps_x,
        taps_bc,
        members,
        *arrived,
        *payloads,
    )


def part_kernel(
    pieces,
    block,
    sources,
    grad_gate,
    packed,
    x_in,
    gain,
    *refs,
):
    z_sources, refs = refs[:sources], refs[sources:]
    *pack_sources, part_out, row_sum, norm_sum, part_ref, w_z, z_sem, pack, pack_sem = refs

    @pl.when(pl.program_id(0) == 0)
    def _():
        weight_fetch(block, z_sources, w_z, z_sem)
        weight_fetch(block, pack_sources, pack, pack_sem)
        weight_wait(z_sources, w_z, z_sem)
        weight_wait(pack_sources, pack, pack_sem)
        norm_sum[...] = jnp.zeros_like(norm_sum)

    x = x_in[...].astype(f32)
    rescale = lax.rsqrt(jnp.mean(x * x, axis=-1, keepdims=True) + epsilon)
    part_ref[...] = dot_nt(grad_gate[...], w_z[...]) + dot_nt(packed[...], pack[...])
    total = jnp.zeros((ROWS, LANES), f32)
    for lane in range(0, x.shape[1], LANES):
        cols = slice(lane, lane + LANES)
        pulled = part_ref[:, cols] * (x_in[:, cols].astype(f32) * rescale)
        norm_sum[0:1, cols] += jnp.sum(pulled, axis=0, keepdims=True)
        total = total + pulled * gain[:, cols]
    row_sum[...] = lane_sums(total)
    if pieces == 1:
        part_out[...] = part_ref[...].astype(bf16)
    else:
        lanes = x.shape[1] // pieces
        for k in range(pieces):
            part_out[k] = part_ref[:, k * lanes : (k + 1) * lanes].astype(bf16)


def part_backward(
    pieces, block, grad_gate, packed, w_z, pack, x, gain
):
    count, width = grad_gate.shape
    model = x.shape[1]
    part_spec, part_shape = pieces_of(pieces, count, model)
    return pl.pallas_call(
        partial(part_kernel, pieces, block, len(w_z)),
        grid=(count // ROWS,),
        in_specs=[
            rows_of(width),
            rows_of(packed.shape[1]),
            rows_of(model),
            full((1, model)),
            *[anywhere() for _ in (*w_z, *pack)],
        ],
        out_specs=[part_spec, pl.BlockSpec((8, ROWS), lambda i: (0, i)), full((8, model))],
        out_shape=[
            jax.ShapeDtypeStruct(part_shape, bf16),
            jax.ShapeDtypeStruct((8, count), f32),
            jax.ShapeDtypeStruct((8, model), f32),
        ],
        scratch_shapes=[
            pltpu.VMEM((ROWS, model), f32),
            *weight_scratch(w_z[0]),
            *weight_scratch(pack[0]),
        ],
        compiler_params=params(),
        cost_estimate=pl.CostEstimate(
            flops=2 * count * model * (width + packed.shape[1]),
            bytes_accessed=2 * (w_z[0].size + pack[0].size) + 8 * count * model,
            transcendentals=0,
        ),
        name="part_backward",
    )(grad_gate, packed, x, gain, *w_z, *pack)


def weights_kernel(count, low, *refs):
    lefts, rights, out = refs[:count], refs[count : 2 * count], refs[2 * count]
    lane = 0
    for left, right in zip(lefts, rights):
        lanes = right.shape[1]
        out[0, :, lane : lane + lanes] = dot_tn(left[...], right[...]).astype(bf16)
        lane += lanes


def weights_backward(lefts, rights, kept):
    count, model = lefts[0].shape
    rows = model // 4
    lanes = sum(right.shape[1] for right in rights)
    low = lax.rem(lax.axis_index("seq"), 2)
    low = (low if kept else 1 - low).astype(jnp.int32).reshape(1)
    return pl.pallas_call(
        partial(weights_kernel, len(lefts)),
        grid_spec=pltpu.PrefetchScalarGridSpec(
            num_scalar_prefetch=1,
            grid=(2,),
            in_specs=[
                *[pl.BlockSpec((count, rows), lambda i, low: (0, 2 * i + low[0])) for _ in lefts],
                *[pl.BlockSpec(right.shape, lambda i, low: (0, 0)) for right in rights],
            ],
            out_specs=pl.BlockSpec((1, rows, lanes), lambda i, low: (i, 0, 0)),
        ),
        out_shape=jax.ShapeDtypeStruct((2, rows, lanes), bf16),
        compiler_params=params(),
        cost_estimate=pl.CostEstimate(
            flops=count * model * lanes,
            bytes_accessed=2 * (len(lefts) * count * model + count * lanes + model * lanes),
            transcendentals=0,
        ),
        name="weights_backward",
    )(low, *lefts, *rights)


def traded(block, axis, bit):
    return lax.ppermute(block, axis, [(i, i ^ bit) for i in range(lax.axis_size(axis))])


def rotated(block, axis, distance):
    size = lax.axis_size(axis)
    return lax.ppermute(block, axis, [(i, (i + distance) % size) for i in range(size)])


def others(block, axis, sign):
    return [rotated(block, axis, sign * d) for d in range(1, lax.axis_size(axis))]


def bits_of(axis):
    bit = 1
    while bit < lax.axis_size(axis):
        yield bit
        bit *= 2


def butterfly(block, axis):
    for bit in bits_of(axis):
        block = block + traded(block, axis, bit)
    return block


def parted(pieces, axis, bit):
    pairs = pieces.reshape((pieces.shape[0] // 2, 2) + pieces.shape[1:])
    mine = lax.rem(lax.axis_index(axis) // bit, 2)
    return (
        lax.dynamic_index_in_dim(pairs, mine, 1, False),
        lax.dynamic_index_in_dim(pairs, 1 - mine, 1, False),
    )


def halved(pieces, axis, bit):
    kept, sent = parted(pieces, axis, bit)
    return kept + traded(sent, axis, bit)


def core_sum(kept, arrived, earlier):
    high = lax.axis_index("seq") // 2

    def summed(at):
        own = lax.dynamic_index_in_dim(kept, at, 0, False)
        both = own + lax.dynamic_index_in_dim(arrived, at, 0, False)
        return both if earlier is None else after(both, earlier)

    return summed(1 - high), summed(high)


def after(value, earlier):
    return value + (0.0 * earlier.reshape(-1)[0].astype(f32)).astype(value.dtype)


def moved_along(block, axis, distance):
    size, place = lax.axis_size(axis), lax.axis_index(axis)
    arrived = rotated(block, axis, distance)
    outside = (place < distance) | (place >= size + distance)
    return jnp.where(outside, jnp.zeros_like(arrived), arrived)


def tied(*values):
    return lax.optimization_barrier(values)


def block_forward(
    block, x, x_edge, weights, grad, pieces, mixed_inside=lambda inner, payloads: (inner, payloads)
):
    heads = weights["heads"]
    (
        normed, rescale, raw_x, raw_bc, edge_x, edge_bc, step_raw, pre_x, pre_bc, act_x, act_bc,
        dt, run, payload,
    ) = project_forward(
        heads, block, x, x_edge, weights["norm"], weights["pack"], weights["dt_bias"],
        weights["rate"], weights["taps_x"], weights["taps_bc"],
    )
    payloads = others(payload, "seq", 1)
    gate_in, inner = inner_forward(
        heads, block, act_x, act_bc, dt, run, normed, weights["w_z"]
    )
    inner, payloads = mixed_inside(inner, payloads)
    mixed, scaled, part, sums, states = outer_forward(
        heads, block, pieces, act_x, act_bc, dt, run, gate_in, inner, weights["w_out"],
        weights["skip"], weights["gain"], payloads, grad,
    )
    kept = dict(
        raw_x=raw_x, raw_bc=raw_bc, step_raw=step_raw, edge_x=edge_x, edge_bc=edge_bc,
        gate_in=gate_in, pre_x=pre_x, pre_bc=pre_bc, act_x=act_x, act_bc=act_bc, dt=dt, run=run,
        payloads=payloads, mixed=mixed, scaled=scaled, states=states, normed=normed,
        rescale=rescale,
    )
    return part, sums, kept


def gate_step(block, grad, w_out, sums, ends, kept, weights):
    return gate_backward(
        weights["heads"], block, grad, w_out, kept["gate_in"], kept["mixed"],
        kept["scaled"], kept["act_x"], kept["act_bc"], kept["run"], weights["gain"], sums, ends,
    )


def states_step(grad_mixed, arrived, kept, weights):
    return states_backward(
        weights["heads"], grad_mixed, kept["act_x"], kept["act_bc"], kept["pre_x"],
        kept["pre_bc"], kept["raw_x"], kept["raw_bc"], kept["edge_x"], kept["edge_bc"],
        kept["dt"], kept["run"], kept["step_raw"], weights["dt_bias"], weights["rate"],
        kept["states"], weights["skip"], weights["taps_x"], weights["taps_bc"], arrived,
        kept["payloads"],
    )


def fixed_tail(packed, tail, back):
    rows = tail + moved_along(back, "seq", -1)
    return packed.at[packed.shape[0] - 16 :].set(rows.astype(bf16))


def vectors_of(heads, taps_x, gain_sum, skip_sum, bias_sum, rate_sum, norm_sum, taps_bc):
    return (
        jnp.concatenate(
            [
                taps_x[:CONV].reshape(-1), gain_sum[0], skip_sum[0], bias_sum[0, :heads],
                jnp.sum(rate_sum[:heads], axis=1),
            ]
        ),
        jnp.concatenate([norm_sum[0], taps_bc[:CONV].reshape(-1)]),
    )


def norm_backward(d_normed, row_sum, x, rescale, grad, gain, model):
    unit = x.astype(f32) * rescale
    h = d_normed.astype(f32) * gain
    out = grad.astype(f32) + rescale * (h - unit * (row_sum / model)[:, None])
    return out.astype(bf16)


def shards(
    tokens, cotangent, norm_gain, w_z, w_x, w_bc, w_dt, conv_x, conv_bc, dt_bias, a_log, skip_d,
    gate_gain, w_out,
):
    section = lax.axis_index("section")
    seq_at = lax.axis_index("seq")
    seq_size = lax.axis_size("seq")
    count, model = tokens.shape[1:]
    head_size = lax.axis_size("head")
    head_at = lax.axis_index("head")
    heads = a_log.shape[1]
    width = w_x.shape[2]
    shared = w_bc.shape[2]
    share = model // head_size
    row_share = count // head_size
    quarter = model // seq_size

    def mine_first(of_first, of_second):
        return (
            jnp.where(section == 0, of_first, of_second),
            jnp.where(section == 0, of_second, of_first),
        )

    def quarter_of(weight):
        return lax.dynamic_slice_in_dim(weight, seq_at * quarter, quarter, 0)

    def half_of(weight):
        pairs = weight.reshape(2, 2, quarter, weight.shape[1])
        return lax.dynamic_index_in_dim(pairs, lax.rem(seq_at, 2), 1, False)

    def own_rows(array):
        return lax.dynamic_slice_in_dim(array, head_at * row_share, row_share, 0)

    def own_columns(array):
        return lax.dynamic_slice_in_dim(array, head_at * share, share, 1)

    def edge_of(x):
        return jnp.pad(moved_along(x[count - (CONV - 1) :], "seq", 1), ((16 - (CONV - 1), 0), (0, 0)))

    def section_sum(of_first, of_second, earlier=None):
        mine, other = mine_first(of_first, of_second)
        arrived = traded(other, "section", 1)
        if earlier is not None:
            arrived = after(arrived, earlier)
        return mine.astype(f32) + arrived.astype(f32)

    def both_sequences(of_first, of_second, earlier=None):
        mine, other = mine_first(of_first, of_second)
        arrived = traded(other, "section", 1)
        if earlier is not None:
            arrived = after(arrived, earlier)
        return jnp.stack(mine_first(mine, arrived))

    padded_dt = jnp.pad(w_dt[0], ((0, 0), (0, LANES - heads)))
    got_pack = traded(
        jnp.concatenate([quarter_of(w) for w in (w_bc[0], padded_dt, w_x[0])], axis=1),
        "section", 1,
    )
    pack = jnp.concatenate([w_bc[0], padded_dt, w_x[0]], axis=1)
    vector = jnp.concatenate(
        [
            norm_gain[0], conv_x[0].T.reshape(-1), conv_bc[0].T.reshape(-1), dt_bias[0], a_log[0],
            skip_d[0], gate_gain[0],
        ]
    )
    got_pack, part_z, vector = tied(got_pack, half_of(w_z[0]), vector)
    vectors = mine_first(vector, traded(vector, "section", 1))
    first = lax.dynamic_index_in_dim(tokens, section, 0, False)
    first_edge = edge_of(first)
    got_z = traded(part_z, "section", 1)
    far_pack = traded(got_pack, "seq", 2)
    far_pack, got_z, part_out, pack, first, first_edge, *vectors = tied(
        far_pack, got_z, half_of(w_out[0]), pack, first, first_edge, *vectors
    )
    got_out = traded(part_out, "section", 1)
    sources_pack = (got_pack, far_pack, traded(got_pack, "seq", 1), traded(far_pack, "seq", 1))
    sources = dict(
        pack=(pack, *sources_pack), w_z=(w_z[0], got_z, traded(got_z, "seq", 1)), w_out=[w_out[0]]
    )
    weights = []
    for b in range(2):
        at = 0

        def take(size):
            nonlocal at
            at += size
            return vectors[b][at - size : at]

        block = dict(heads=heads, **sources)
        block["norm"] = take(model)[None]
        block["taps_x"] = take(CONV * width).reshape(CONV, width)
        block["taps_bc"] = take(CONV * shared).reshape(CONV, shared)
        block["dt_bias"] = jnp.pad(take(heads), (0, LANES - heads))[None]
        block["rate"] = jnp.pad(-jnp.exp(take(heads)), (0, LANES - heads))[None]
        block["skip"] = jnp.repeat(take(heads), width // heads)[None]
        block["gain"] = take(width)[None]
        weights.append(block)

    last_grad = lax.dynamic_index_in_dim(cotangent, section, 0, False)

    def fetch_out(inner, payloads):
        inner, part, *payloads = tied(inner, got_out, *payloads)
        sources["w_out"] += [part, traded(part, "seq", 1)]
        return inner, payloads

    part, sums, kept_first = block_forward(
        0, first, first_edge, weights[0], None, 1, fetch_out
    )
    sums, last_grad = tied(sums, last_grad)
    summed, grad_ahead = tied(
        lax.psum_scatter(part, "head", scatter_dimension=0, tiled=True),
        ahead_backward(1, last_grad, weights[1]["w_out"]),
    )
    summed = summed.astype(f32)
    sums_first = [sums, *others(sums, "head", 1)]
    scale_first = lax.rsqrt(sum(part[0] for part in sums_first) / INNER + epsilon)
    second_share = own_rows(first).astype(f32) + own_rows(scale_first)[:, None] * summed
    second = lax.all_gather(second_share.astype(bf16), "head", axis=0, tiled=True)

    outward, sums, kept_second = block_forward(
        1, second, edge_of(second), weights[1], last_grad, head_size
    )
    sums_second = [sums, *others(sums, "head", 1)]
    bits = list(bits_of("head"))

    grad_mixed, grad_gate, scaled, gain_sum, skip_sum, adjoint = gate_step(
        1, grad_ahead, (), sums_second, (), kept_second, weights[1]
    )
    normed = kept_second["normed"]
    early_sent = weights_backward([last_grad, normed], [scaled, grad_gate], False)
    grad_mixed, early_sent, outward, *arrived = tied(
        grad_mixed, early_sent, outward, *others(adjoint, "seq", -1)
    )
    packed, tail, back, taps_x, taps_bc, rate_sum, bias_sum = states_step(
        grad_mixed, arrived, kept_second, weights[1]
    )
    kept, sent = parted(outward, "head", bits[0])
    packed, kept, arrived = tied(
        fixed_tail(packed, tail, back), kept, traded(sent, "head", bits[0])
    )
    part, row_sum, norm_sum = part_backward(
        1, 1, grad_gate, packed, weights[1]["w_z"], weights[1]["pack"], second,
        weights[1]["norm"],
    )
    norm_sum, kept, taps_x, gain_sum, skip_sum, bias_sum, rate_sum, taps_bc = tied(
        norm_sum, kept, taps_x, gain_sum, skip_sum, bias_sum, rate_sum, taps_bc
    )
    outward = kept + arrived
    local_second, whole_second = vectors_of(
        heads, taps_x, gain_sum, skip_sum, bias_sum, rate_sum, norm_sum, taps_bc
    )
    part, packed, scaled, grad_gate = tied(part, packed, scaled, grad_gate)
    rows_part = lax.psum_scatter(part, "head", scatter_dimension=0, tiled=True)
    row_sums = [row_sum, *others(row_sum, "head", 1)]
    row_sum = sum(part[0] for part in row_sums)
    kept = weights_backward([last_grad, normed], [scaled, grad_gate], True)
    early_sent, early = core_sum(kept, traded(early_sent, "seq", 1), norm_sum)
    late_sent = weights_backward([normed], [packed], False)
    kept = weights_backward([normed], [packed], True)
    late_sent, late = core_sum(kept, traded(late_sent, "seq", 1), norm_sum)
    rows_part, early_sent, late_sent = tied(rows_part, early_sent, late_sent)
    early = early + traded(early_sent, "seq", 2)
    late = late + traded(late_sent, "seq", 2)
    middle_share = norm_backward(
        rows_part, own_rows(row_sum), own_rows(second), own_rows(kept_second["rescale"]),
        own_rows(last_grad), weights[1]["norm"], model,
    )
    middle_grad = lax.all_gather(middle_share, "head", axis=0, tiled=True)
    middle_grad, early_second, late_second, outward, local_second, whole_second = tied(
        middle_grad, early, late, outward, local_second, whole_second
    )
    for bit in bits[1:-1]:
        outward = halved(outward, "head", bit)
    out_kept, out_sent = parted(outward, "head", bits[-1])

    grad_mixed, grad_gate, scaled, gain_sum, skip_sum, adjoint = gate_step(
        0, middle_grad, weights[0]["w_out"], sums_first, (second, first), kept_first, weights[0]
    )
    normed = kept_first["normed"]
    early_sent = weights_backward([middle_grad, normed], [scaled, grad_gate], False)
    grad_mixed, early_sent, out_sent, *arrived = tied(
        grad_mixed, early_sent, out_sent, *others(adjoint, "seq", -1)
    )
    packed, tail, back, taps_x, taps_bc, rate_sum, bias_sum = states_step(
        grad_mixed, arrived, kept_first, weights[0]
    )
    packed, out_arrived = tied(
        fixed_tail(packed, tail, back), traded(out_sent, "head", bits[-1])
    )
    late_sent = weights_backward([normed], [packed], False)
    kept = weights_backward([normed], [packed], True)
    late_sent, late = core_sum(kept, traded(late_sent, "seq", 1), None)
    packed, late_sent, late = tied(packed, late_sent, late)
    part, row_sum, norm_sum = part_backward(
        head_size, 0, grad_gate, packed, weights[0]["w_z"], weights[0]["pack"], first,
        weights[0]["norm"],
    )
    norm_sum, scaled, grad_gate, out_kept, *sums_second = tied(
        norm_sum, scaled, grad_gate, out_kept, *sums_second
    )
    outward = out_kept + out_arrived
    columns_part = lax.psum_scatter(part, "head", scatter_dimension=0, tiled=True)[0]
    row_sums = [row_sum, *others(row_sum, "head", 1)]
    row_sum = sum(part[0] for part in row_sums)
    kept = weights_backward([middle_grad, normed], [scaled, grad_gate], True)
    sent, early = core_sum(kept, traded(early_sent, "seq", 1), norm_sum)
    sent, late_arrived = tied(sent, traded(late_sent, "seq", 2))
    late = late + late_arrived
    late, sent, norm_sum, taps_x, gain_sum, skip_sum, bias_sum, rate_sum, taps_bc = tied(
        late, sent, norm_sum, taps_x, gain_sum, skip_sum, bias_sum, rate_sum, taps_bc
    )
    local_first, whole_first = vectors_of(
        heads, taps_x, gain_sum, skip_sum, bias_sum, rate_sum, norm_sum, taps_bc
    )
    vector = jnp.stack(
        [
            jnp.concatenate([whole_first, local_first]),
            jnp.concatenate([whole_second, local_second]),
        ]
    )
    vector = butterfly(vector, "seq")
    first_share = norm_backward(
        columns_part, row_sum, own_columns(first), kept_first["rescale"],
        own_columns(middle_grad), own_columns(weights[0]["norm"]), model,
    )
    vector = section_sum(vector[0], vector[1], first_share)
    late = section_sum(late, late_second, first_share)
    early = section_sum(early + traded(sent, "seq", 2), early_second, first_share)
    whole = butterfly(vector[: whole_first.shape[0]], "head")
    local = vector[whole_first.shape[0] :]
    last_share = lax.rsqrt(sum(part[0] for part in sums_second) / INNER + epsilon)
    last_share = last_share[:, None] * outward[0].astype(f32)
    last_share = (own_columns(second).astype(f32) + last_share).astype(bf16)
    block_outputs = both_sequences(own_columns(second), last_share, first_share)
    grad_w_bc = late[:, :shared].astype(bf16).reshape(quarter, head_size, shared // head_size)
    grad_w_bc = grad_w_bc.swapaxes(0, 1)
    for bit in bits:
        grad_w_bc = halved(grad_w_bc, "head", bit)
    input_grads = both_sequences(first_share, own_columns(middle_grad))
    at = 0

    def taken(size):
        nonlocal at
        at += size
        return local[at - size : at]

    grad_norm = lax.dynamic_slice_in_dim(whole, head_at * share, share, 0)
    grad_conv_bc = whole[model:].reshape(CONV, shared).T
    grad_conv_x = taken(CONV * width).reshape(CONV, width).T
    grad_gain = taken(width)
    grad_skip = jnp.sum(taken(width).reshape(heads, width // heads), axis=1)
    grad_bias = taken(heads)
    grad_rate = taken(heads)
    return (
        block_outputs[None],
        input_grads[None],
        grad_norm[None],
        early[None, :, width:],
        late[None, :, shared + LANES :],
        grad_w_bc.astype(f32),
        late[None, :, shared : shared + heads],
        grad_conv_x[None],
        grad_conv_bc[None],
        grad_bias[None],
        grad_rate[None],
        grad_skip[None],
        grad_gain[None],
        early[None, :, :width],
    )


def solution(mesh):
    placed = (
        P(None, "seq", None),
        P(None, "seq", None),
        P("section", None),
        P("section", None, "head"),
        P("section", None, "head"),
        P("section", None, None),
        P("section", None, "head"),
        P("section", "head", None),
        P("section", None, None),
        P("section", "head"),
        P("section", "head"),
        P("section", "head"),
        P("section", "head"),
        P("section", None, "head"),
    )
    return jax.shard_map(
        shards,
        mesh=mesh,
        in_specs=placed,
        out_specs=(
            P("section", None, "seq", "head"),
            P("section", None, "seq", "head"),
            P("section", "head"),
            P("section", "seq", "head"),
            P("section", "seq", "head"),
            P("section", "seq", "head"),
            P("section", "seq", "head"),
            P("section", "head", None),
            P("section", None, None),
            P("section", "head"),
            P("section", "head"),
            P("section", "head"),
            P("section", "head"),
            P("section", "seq", "head"),
        ),
        check_vma=False,
    )
```
